32 devices in a mesh: dp: 4 (over y, x), fsdp: 8 (over z, core).
Axes of the slice: x: 2, y: 2, z: 4, core: 2. Of those that a mesh axis runs over, the one named last changes fastest.
Arguments:
- latents: bfloat16 [32, 128, 1024], P(('dp', 'fsdp')), may hold values from -6 to 6
- inputs: bfloat16 [32, 1024, 1024], P(('dp', 'fsdp')), may hold values from -6 to 6
- frames: int32 [32], P(('dp', 'fsdp')), may hold values from 4 to 16, as said below
- norm_latent: float32 [1024], P(('dp', 'fsdp')), may hold values from 0.5 to 1.5
- norm_input: float32 [1024], P(('dp', 'fsdp')), may hold values from 0.5 to 1.5
- cross_query: float32 [1024, 1024], P(('dp', 'fsdp')), may hold values from -0.1875 to 0.1875
- cross_key: float32 [1024, 1024], P(('dp', 'fsdp')), may hold values from -0.1875 to 0.1875
- cross_value: float32 [1024, 1024], P(('dp', 'fsdp')), may hold values from -0.1875 to 0.1875
- cross_output: float32 [1024, 1024], P(('dp', 'fsdp')), may hold values from -2 to 2
- norm_first: float32 [1024], P(('dp', 'fsdp')), may hold values from 0.5 to 1.5
- first_up: float32 [1024, 4096], P(('dp', 'fsdp')), may hold values from -0.1875 to 0.1875
- first_down: float32 [4096, 1024], P(('dp', 'fsdp')), may hold values from -0.09375 to 0.09375
- norm_self: float32 [1024], P(('dp', 'fsdp')), may hold values from 0.5 to 1.5
- self_query: float32 [1024, 1024], P(('dp', 'fsdp')), may hold values from -0.1875 to 0.1875
- self_key: float32 [1024, 1024], P(('dp', 'fsdp')), may hold values from -0.1875 to 0.1875
- self_value: float32 [1024, 1024], P(('dp', 'fsdp')), may hold values from -0.1875 to 0.1875
- self_output: float32 [1024, 1024], P(('dp', 'fsdp')), may hold values from -1 to 1
- norm_second: float32 [1024], P(('dp', 'fsdp')), may hold values from 0.5 to 1.5
- second_up: float32 [1024, 4096], P(('dp', 'fsdp')), may hold values from -0.1875 to 0.1875
- second_down: float32 [4096, 1024], P(('dp', 'fsdp')), may hold values from -0.09375 to 0.09375
- cotangent: bfloat16 [32, 128, 1024], P(('dp', 'fsdp')), may hold values from -6 to 6
Outputs:
- out_latents: bfloat16 [32, 128, 1024], P(('dp', 'fsdp'))
- grad_latents: bfloat16 [32, 128, 1024], P(('dp', 'fsdp'))
- grad_inputs: bfloat16 [32, 1024, 1024], P(('dp', 'fsdp'))
- grad_norm_latent: float32 [1024], P(('dp', 'fsdp'))
- grad_norm_input: float32 [1024], P(('dp', 'fsdp'))
- grad_cross_query: float32 [1024, 1024], P(('dp', 'fsdp'))
- grad_cross_key: float32 [1024, 1024], P(('dp', 'fsdp'))
- grad_cross_value: float32 [1024, 1024], P(('dp', 'fsdp'))
- grad_cross_output: float32 [1024, 1024], P(('dp', 'fsdp'))
- grad_norm_first: float32 [1024], P(('dp', 'fsdp'))
- grad_first_up: float32 [1024, 4096], P(('dp', 'fsdp'))
- grad_first_down: float32 [4096, 1024], P(('dp', 'fsdp'))
- grad_norm_self: float32 [1024], P(('dp', 'fsdp'))
- grad_self_query: float32 [1024, 1024], P(('dp', 'fsdp'))
- grad_self_key: float32 [1024, 1024], P(('dp', 'fsdp'))
- grad_self_value: float32 [1024, 1024], P(('dp', 'fsdp'))
- grad_self_output: float32 [1024, 1024], P(('dp', 'fsdp'))
- grad_norm_second: float32 [1024], P(('dp', 'fsdp'))
- grad_second_up: float32 [1024, 4096], P(('dp', 'fsdp'))
- grad_second_down: float32 [4096, 1024], P(('dp', 'fsdp'))
The draws below stay inside these ranges and needn't reach their ends.
Inputs may be any that keep to these rules, and one draw needn't show every extreme that they name: Each entry of frames is 4 or 16 (nothing in between); in every draw some group has 4 frames and some has 16.
All inputs are finite; a program needn't handle non-finite values.
Results may differ from the reference program's by a relative error of at most 0.024.
Values may be sent and summed in bfloat16 or wider, within the bound.
A program may use at most 256 MiB of HBM per device.

```python
import jax
import jax.numpy as jnp
from jax import lax

D = 1024
HEADS = 8
HD = 128
FF = 4096
LAT = 128
FRAME_TOK = 64
LMAX = 1024
GROUPS = 32


def draw_frames(key, part):
    key = jax.random.fold_in(key, 11)
    first, second, third = jax.random.split(key, 3)
    coins = jax.random.randint(first, (GROUPS,), 0, 2)
    frames = jnp.where(coins == 1, 16, 4).astype(jnp.int32)
    long_spot = jax.random.randint(second, (), 0, GROUPS)
    short_spot = (long_spot + 1 + jax.random.randint(third, (), 0, GROUPS - 1)) % GROUPS
    frames = frames.at[long_spot].set(16)
    frames = frames.at[short_spot].set(4)
    return frames.astype(jnp.int32)


def shard_levels(stream_key, extent, cuts, smallest, top_value):
    level, own = 1.0, jax.random.fold_in(stream_key, 6)
    for position, blocks in cuts:
        heights = jnp.exp(jax.random.uniform(jax.random.fold_in(own, position), (blocks,), jnp.float32, smallest / len(cuts), top_value / len(cuts)))
        level = level * jnp.repeat(heights, extent[position] // blocks).reshape([-1 if axis == position else 1 for axis in range(len(extent))])
    return level


def gaussian(stream_key, extent, scale, bound, cuts=(), held_as=jnp.bfloat16):
    drawn = jax.random.normal(stream_key, extent, jnp.float32) * scale
    if len(cuts) > 0:
        drawn = shard_levels(stream_key, extent, cuts, -0.22, 0.18) * drawn
    return jnp.clip(drawn, min=-bound, max=bound).astype(held_as)


def setup_inputs(seed: int = 0) -> dict:
    splits = jax.random.split(jax.random.key(seed), 22)
    latents = gaussian(splits[0], (GROUPS, LAT, D), 1.0, 6.0, ((0, 32),))
    inputs = gaussian(splits[1], (GROUPS, LMAX, D), 1.0, 6.0, ((0, 32),))
    frames = draw_frames(jax.random.fold_in(splits[21], 71), 0)
    norm_latent = jnp.clip(1.0 + 0.1 * jax.random.normal(splits[3], (D,), jnp.float32), 0.5, 1.5)
    norm_input = jnp.clip(1.0 + 0.1 * jax.random.normal(splits[4], (D,), jnp.float32), 0.5, 1.5)
    cross_query = gaussian(splits[5], (D, D), D ** -0.5, 0.1875, ((0, 32),), jnp.float32)
    cross_key = gaussian(splits[6], (D, D), D ** -0.5, 0.1875, ((0, 32),), jnp.float32)
    cross_value = gaussian(splits[7], (D, D), D ** -0.5, 0.1875, ((0, 32),), jnp.float32)
    cross_output = gaussian(splits[8], (D, D), (D // 128) ** -0.5, 2.0, ((0, 32),), jnp.float32)
    norm_first = jnp.clip(1.0 + 0.1 * jax.random.normal(splits[9], (D,), jnp.float32), 0.5, 1.5)
    first_up = gaussian(splits[10], (D, FF), D ** -0.5, 0.1875, ((0, 32),), jnp.float32)
    first_down = gaussian(splits[11], (FF, D), FF ** -0.5, 0.09375, ((0, 32),), jnp.float32)
    norm_self = jnp.clip(1.0 + 0.1 * jax.random.normal(splits[12], (D,), jnp.float32), 0.5, 1.5)
    self_query = gaussian(splits[13], (D, D), D ** -0.5, 0.1875, ((0, 32),), jnp.float32)
    self_key = gaussian(splits[14], (D, D), D ** -0.5, 0.1875, ((0, 32),), jnp.float32)
    self_value = gaussian(splits[15], (D, D), D ** -0.5, 0.1875, ((0, 32),), jnp.float32)
    self_output = gaussian(splits[16], (D, D), (D // 32) ** -0.5, 1.0, ((0, 32),), jnp.float32)
    norm_second = jnp.clip(1.0 + 0.1 * jax.random.normal(splits[17], (D,), jnp.float32), 0.5, 1.5)
    second_up = gaussian(splits[18], (D, FF), D ** -0.5, 0.1875, ((0, 32),), jnp.float32)
    second_down = gaussian(splits[19], (FF, D), FF ** -0.5, 0.09375, ((0, 32),), jnp.float32)
    cotangent = gaussian(splits[20], (GROUPS, LAT, D), 1.0, 6.0, ((0, 32),))
    return {"latents": latents, "inputs": inputs, "frames": frames, "norm_latent": norm_latent, "norm_input": norm_input, "cross_query": cross_query, "cross_key": cross_key, "cross_value": cross_value, "cross_output": cross_output, "norm_first": norm_first, "first_up": first_up, "first_down": first_down, "norm_self": norm_self, "self_query": self_query, "self_key": self_key, "self_value": self_value, "self_output": self_output, "norm_second": norm_second, "second_up": second_up, "second_down": second_down, "cotangent": cotangent}


EPS = 1e-05
NEG = -1000000000.0

@jax.custom_vjp
def low(v):
    return lax.optimization_barrier(v.astype(jnp.bfloat16)).astype(jnp.float32)

@jax.custom_vjp
def low_back(v):
    return v

def low_keep(v):
    return (low(v), None)

def low_pass(kept, grad):
    return (grad,)

def back_keep(v):
    return (v, None)

def back_low(kept, grad):
    return (low(grad),)
low.defvjp(low_keep, low_pass)
low_back.defvjp(back_keep, back_low)

def layer_norm(value, gain):
    center = value - lax.optimization_barrier(jnp.mean(value, axis=-1, keepdims=True))
    spread = lax.optimization_barrier(jnp.mean(center * center, axis=-1, keepdims=True))
    return center * lax.rsqrt(spread + EPS) * gain

def rounded_both(value):
    return low(low_back(value))

def matmul(left, right):
    return jnp.dot(left, right, precision=lax.Precision.HIGHEST)

def attend(query, key, value, valid):
    rows = query.shape[0]
    keys = key.shape[0]
    query_heads = query.reshape(rows, HEADS, HD)
    key_heads = key.reshape(keys, HEADS, HD)
    value_heads = value.reshape(keys, HEADS, HD)
    scores = jnp.einsum('qhd,khd->hqk', query_heads, key_heads, precision=lax.Precision.HIGHEST) * HD ** (-0.5)
    scores = low_back(scores)
    scores = jnp.where(valid[None, None, :], scores, NEG)
    probs = low(jax.nn.softmax(scores, axis=-1))
    mixed = jnp.einsum('hqk,khd->qhd', probs, value_heads, precision=lax.Precision.HIGHEST)
    return rounded_both(mixed.reshape(rows, HEADS * HD))

def feed(resid, gain, w_up, w_down):
    normed = low(layer_norm(resid, gain))
    hidden = low(jax.nn.gelu(low_back(matmul(normed, w_up)), approximate=True))
    return resid + low_back(matmul(hidden, w_down))

def group_layer(latent_rows, input_rows, length, weights):
    g_lat, g_inp, w_query, w_key, w_value, w_out, g_first, up_one, down_one, g_self, s_query, s_key, s_value, s_out, g_second, up_two, down_two = weights
    normed_lat = low(layer_norm(latent_rows, g_lat))
    normed_inp = low(layer_norm(input_rows, g_inp))
    valid = jnp.arange(input_rows.shape[0], dtype=jnp.int32) < length
    mixed = attend(rounded_both(matmul(normed_lat, w_query)), rounded_both(matmul(normed_inp, w_key)), rounded_both(matmul(normed_inp, w_value)), valid)
    first = latent_rows + low_back(matmul(mixed, w_out))
    second = feed(first, g_first, up_one, down_one)
    normed_self = low(layer_norm(second, g_self))
    every = jnp.ones((latent_rows.shape[0],), dtype=bool)
    mixed_self = attend(rounded_both(matmul(normed_self, s_query)), rounded_both(matmul(normed_self, s_key)), rounded_both(matmul(normed_self, s_value)), every)
    third = second + low_back(matmul(mixed_self, s_out))
    return feed(third, g_second, up_two, down_two)

def reference(latents, inputs, frames, norm_latent, norm_input, cross_query, cross_key, cross_value, cross_output, norm_first, first_up, first_down, norm_self, self_query, self_key, self_value, self_output, norm_second, second_up, second_down, cotangent):
    lengths = (frames * FRAME_TOK).astype(jnp.int32)

    def total(latent_all, input_all, *weights):
        rounded = tuple((low(weight) for weight in weights))

        def one_group(item):
            return group_layer(item[0], item[1], item[2], rounded)
        return lax.map(jax.checkpoint(one_group), (latent_all, input_all, lengths))
    result, pull = jax.vjp(total, latents.astype(jnp.float32), inputs.astype(jnp.float32), norm_latent, norm_input, cross_query, cross_key, cross_value, cross_output, norm_first, first_up, first_down, norm_self, self_query, self_key, self_value, self_output, norm_second, second_up, second_down)
    grads = pull(cotangent.astype(jnp.float32))
    return (result.astype(jnp.bfloat16), grads[0].astype(jnp.bfloat16), grads[1].astype(jnp.bfloat16), grads[2], grads[3], grads[4], grads[5], grads[6], grads[7], grads[8], grads[9], grads[10], grads[11], grads[12], grads[13], grads[14], grads[15], grads[16], grads[17], grads[18])
```

```python
import functools

import jax
import jax.numpy as jnp
from jax import lax
from jax.sharding import PartitionSpec as P

HEADS = 8
FRAME_TOK = 64


EPS = 1e-05
NEG = -1000000000.0


def layer_norm(value, gain):
    center = value - jnp.mean(value, axis=-1, keepdims=True)
    spread = jnp.mean(center * center, axis=-1, keepdims=True)
    return center * lax.rsqrt(spread + EPS) * gain


def activate(value):
    return jax.nn.gelu(value, approximate=True)


def product(left, right):
    return jnp.dot(left, right, preferred_element_type=jnp.float32)


def weight_grad(left, right):
    return lax.dot_general(
        left, right, (((0,), (0,)), ((), ())), preferred_element_type=jnp.float32
    )


def back_product(grad, weight):
    return lax.dot_general(
        grad, weight, (((1,), (1,)), ((), ())), preferred_element_type=jnp.float32
    )


def norm_back(value, gain, grad):
    _, pull = jax.vjp(layer_norm, value, gain)
    return pull(grad)


def activate_back(value, grad):
    _, pull = jax.vjp(activate, value)
    return pull(grad)[0]


def split_heads(value, groups):
    return value.reshape(groups, -1, HEADS, value.shape[-1] // HEADS)


def merge_heads(value):
    return value.reshape(-1, value.shape[2] * value.shape[3])


def masked_scores(query, key, valid):
    scale = query.shape[-1] ** (-0.5)
    scores = jnp.einsum("gqhd,gkhd->ghqk", query, key, preferred_element_type=jnp.float32) * scale
    return jnp.where(valid[:, None, None, :], scores, NEG)


def attend_forward(query, key, value, valid):
    scores = masked_scores(query, key, valid)
    top = jnp.max(scores, axis=-1, keepdims=True)
    expo = jnp.exp(scores - top)
    denom = jnp.sum(expo, axis=-1, keepdims=True)
    weights = (expo / denom).astype(jnp.bfloat16)
    mixed = jnp.einsum("ghqk,gkhd->gqhd", weights, value, preferred_element_type=jnp.float32)
    return (merge_heads(mixed).astype(jnp.bfloat16), top + jnp.log(denom))


def attend_back(query, key, value, valid, logsum, grad_mixed):
    scale = query.shape[-1] ** (-0.5)
    probs = jnp.exp(masked_scores(query, key, valid) - logsum)
    grad_probs = jnp.einsum(
        "gqhd,gkhd->ghqk", grad_mixed, value, preferred_element_type=jnp.float32
    )
    inner = jnp.sum(probs * grad_probs, axis=-1, keepdims=True)
    grad_scores = (probs * (grad_probs - inner)).astype(jnp.bfloat16)
    weights = probs.astype(jnp.bfloat16)
    grad_query = (
        jnp.einsum("ghqk,gkhd->gqhd", grad_scores, key, preferred_element_type=jnp.float32) * scale
    )
    grad_key = (
        jnp.einsum("ghqk,gqhd->gkhd", grad_scores, query, preferred_element_type=jnp.float32)
        * scale
    )
    grad_value = jnp.einsum(
        "ghqk,gqhd->gkhd", weights, grad_mixed, preferred_element_type=jnp.float32
    )
    return (
        merge_heads(grad_query).astype(jnp.bfloat16),
        merge_heads(grad_key).astype(jnp.bfloat16),
        merge_heads(grad_value).astype(jnp.bfloat16),
    )


def feed_forward(resid, gain, w_up, w_down):
    normed = layer_norm(resid, gain.astype(jnp.float32)).astype(jnp.bfloat16)
    before = product(normed, w_up)
    hidden = activate(before).astype(jnp.bfloat16)
    return (resid + product(hidden, w_down), (normed, before, hidden))


def feed_back(grad, resid, gain, saved, w_up, w_down):
    normed, before, hidden = saved
    grad_low = grad.astype(jnp.bfloat16)
    grad_down = weight_grad(hidden, grad_low)
    grad_before = activate_back(before, back_product(grad_low, w_down)).astype(jnp.bfloat16)
    grad_up = weight_grad(normed, grad_before)
    grad_resid, grad_gain = norm_back(
        resid, gain.astype(jnp.float32), back_product(grad_before, w_up)
    )
    return (grad + grad_resid, grad_gain, grad_up, grad_down)


def project_back(grad, mixed, w_out, query, key, value, valid, logsum, groups):
    grad_low = grad.astype(jnp.bfloat16)
    grad_out = weight_grad(mixed, grad_low)
    grad_mixed = back_product(grad_low, w_out).astype(jnp.bfloat16)
    grad_query, grad_key, grad_value = attend_back(
        split_heads(query, groups),
        split_heads(key, groups),
        split_heads(value, groups),
        valid,
        logsum,
        split_heads(grad_mixed, groups),
    )
    return (grad_out, grad_query, grad_key, grad_value)


def local(
    latents,
    inputs,
    frames,
    norm_latent,
    norm_input,
    cross_query,
    cross_key,
    cross_value,
    cross_output,
    norm_first,
    first_up,
    first_down,
    norm_self,
    self_query,
    self_key,
    self_value,
    self_output,
    norm_second,
    second_up,
    second_down,
    cotangent,
    mesh_size,
):
    groups, lat_rows, width = latents.shape
    span = inputs.shape[1]
    hidden_width = first_up.shape[1]
    low_type = jnp.bfloat16
    parts = mesh_size
    gains = (norm_latent, norm_input, norm_first, norm_self, norm_second)
    mats = (cross_query, cross_key, cross_value, cross_output, first_up, first_down,
            self_query, self_key, self_value, self_output, second_up, second_down)
    blocks = []
    for mat in mats:
        for start in range(0, mat.shape[1], width):
            blocks.append(mat[:, start:start + width])
    gain_row = jnp.concatenate([jnp.concatenate(gains), jnp.zeros((width - 5 * gains[0].shape[0],), jnp.float32)])
    gain_rows = jnp.concatenate([gain_row[None], jnp.zeros((15, width), jnp.float32)])
    packed = jnp.concatenate([gain_rows] + blocks).astype(low_type)
    whole = lax.all_gather(packed, ("dp", "fsdp"), axis=0, tiled=False)
    per = gains[0].shape[0]
    gathered_gains = [whole[:, 0, i * per:(i + 1) * per].reshape(width) for i in range(5)]
    gain_lat, gain_inp, gain_first, gain_self, gain_second = gathered_gains
    at = 16
    full = []
    for mat in mats:
        columns = []
        for start in range(0, mat.shape[1], width):
            columns.append(whole[:, at:at + mat.shape[0]].reshape(parts * mat.shape[0], width))
            at += mat.shape[0]
        full.append(columns[0] if len(columns) == 1 else jnp.concatenate(columns, axis=1))
    w_query, w_key, w_value, w_out, up_one, down_one, s_query, s_key, s_value, s_out, up_two, down_two = full
    positions = jnp.arange(span, dtype=jnp.int32)
    valid = positions[None, :] < (frames * FRAME_TOK)[:, None]
    every = jnp.ones((groups, lat_rows), dtype=bool)
    latent_rows = latents.reshape(groups * lat_rows, width).astype(jnp.float32)
    input_rows = inputs.reshape(groups * span, width).astype(jnp.float32)
    normed_lat = layer_norm(latent_rows, gain_lat.astype(jnp.float32)).astype(low_type)
    normed_inp = layer_norm(input_rows, gain_inp.astype(jnp.float32)).astype(low_type)
    query_one = product(normed_lat, w_query).astype(low_type)
    key_one = product(normed_inp, w_key).astype(low_type)
    value_one = product(normed_inp, w_value).astype(low_type)
    mixed_one, logsum_one = attend_forward(
        split_heads(query_one, groups),
        split_heads(key_one, groups),
        split_heads(value_one, groups),
        valid,
    )
    first_resid = latent_rows + product(mixed_one, w_out)
    second_resid, saved_one = feed_forward(first_resid, gain_first, up_one, down_one)
    normed_self = layer_norm(second_resid, gain_self.astype(jnp.float32)).astype(low_type)
    query_two = product(normed_self, s_query).astype(low_type)
    key_two = product(normed_self, s_key).astype(low_type)
    value_two = product(normed_self, s_value).astype(low_type)
    mixed_two, logsum_two = attend_forward(
        split_heads(query_two, groups),
        split_heads(key_two, groups),
        split_heads(value_two, groups),
        every,
    )
    third_resid = second_resid + product(mixed_two, s_out)
    final_resid, saved_two = feed_forward(third_resid, gain_second, up_two, down_two)
    result = final_resid.reshape(groups, lat_rows, width).astype(low_type)
    grad_final = cotangent.reshape(groups * lat_rows, width).astype(jnp.float32)
    grad_third, grad_gain_second, grad_up_two, grad_down_two = feed_back(
        grad_final, third_resid, gain_second, saved_two, up_two, down_two
    )
    grad_s_out, grad_query_two, grad_key_two, grad_value_two = project_back(
        grad_third, mixed_two, s_out, query_two, key_two, value_two, every, logsum_two, groups
    )
    grad_s_query = weight_grad(normed_self, grad_query_two)
    grad_s_key = weight_grad(normed_self, grad_key_two)
    grad_s_value = weight_grad(normed_self, grad_value_two)
    grad_normed_self = (
        back_product(grad_query_two, s_query)
        + back_product(grad_key_two, s_key)
        + back_product(grad_value_two, s_value)
    )
    grad_from_self, grad_gain_self = norm_back(
        second_resid, gain_self.astype(jnp.float32), grad_normed_self
    )
    grad_second = grad_third + grad_from_self
    grad_first, grad_gain_first, grad_up_one, grad_down_one = feed_back(
        grad_second, first_resid, gain_first, saved_one, up_one, down_one
    )
    grad_w_out, grad_query_one, grad_key_one, grad_value_one = project_back(
        grad_first, mixed_one, w_out, query_one, key_one, value_one, valid, logsum_one, groups
    )
    grad_w_query = weight_grad(normed_lat, grad_query_one)
    grad_w_key = weight_grad(normed_inp, grad_key_one)
    grad_w_value = weight_grad(normed_inp, grad_value_one)
    grad_from_lat, grad_gain_lat = norm_back(
        latent_rows, gain_lat.astype(jnp.float32), back_product(grad_query_one, w_query)
    )
    grad_latent_rows = grad_first + grad_from_lat
    grad_normed_inp = back_product(grad_key_one, w_key) + back_product(grad_value_one, w_value)
    grad_input_rows, grad_gain_inp = norm_back(
        input_rows, gain_inp.astype(jnp.float32), grad_normed_inp
    )
    grad_mats = (grad_w_query, grad_w_key, grad_w_value, grad_w_out, grad_up_one, grad_down_one,
                 grad_s_query, grad_s_key, grad_s_value, grad_s_out, grad_up_two, grad_down_two)
    gain_grads = jnp.stack([grad_gain_lat, grad_gain_inp, grad_gain_first, grad_gain_self, grad_gain_second])
    gain_grads = jnp.moveaxis(gain_grads.reshape(5, parts, per), 1, 0).reshape(parts, 1, 5 * per)
    gain_grads = jnp.pad(gain_grads, ((0, 0), (0, 15), (0, width - 5 * per)))
    pieces = [gain_grads.astype(low_type)]
    for grad in grad_mats:
        for start in range(0, grad.shape[1], width):
            pieces.append(grad[:, start:start + width].reshape(parts, -1, width).astype(low_type))
    summed = lax.psum_scatter(jnp.concatenate(pieces, axis=1), ("dp", "fsdp"), scatter_dimension=0, tiled=False)
    summed = summed.astype(jnp.float32)
    gain_out = [summed[0, i * per:(i + 1) * per] for i in range(5)]
    at = 16
    out = []
    for mat in mats:
        columns = []
        for start in range(0, mat.shape[1], width):
            columns.append(summed[at:at + mat.shape[0]])
            at += mat.shape[0]
        out.append(columns[0] if len(columns) == 1 else jnp.concatenate(columns, axis=1))
    grad_latents = grad_latent_rows.reshape(groups, lat_rows, width).astype(low_type)
    grad_inputs = grad_input_rows.reshape(groups, span, width).astype(low_type)
    return (
        result, grad_latents, grad_inputs,
        gain_out[0], gain_out[1], out[0], out[1], out[2], out[3],
        gain_out[2], out[4], out[5],
        gain_out[3], out[6], out[7], out[8], out[9],
        gain_out[4], out[10], out[11],
    )


def solution(mesh):
    in_specs = (
        P(("dp", "fsdp"), None, None),
        P(("dp", "fsdp"), None, None),
        P(("dp", "fsdp")),
        P(("dp", "fsdp")),
        P(("dp", "fsdp")),
        P(("dp", "fsdp"), None),
        P(("dp", "fsdp"), None),
        P(("dp", "fsdp"), None),
        P(("dp", "fsdp"), None),
        P(("dp", "fsdp")),
        P(("dp", "fsdp"), None),
        P(("dp", "fsdp"), None),
        P(("dp", "fsdp")),
        P(("dp", "fsdp"), None),
        P(("dp", "fsdp"), None),
        P(("dp", "fsdp"), None),
        P(("dp", "fsdp"), None),
        P(("dp", "fsdp")),
        P(("dp", "fsdp"), None),
        P(("dp", "fsdp"), None),
        P(("dp", "fsdp"), None, None),
    )
    out_specs = (
        P(("dp", "fsdp"), None, None),
        P(("dp", "fsdp"), None, None),
        P(("dp", "fsdp"), None, None),
        P(("dp", "fsdp")),
        P(("dp", "fsdp")),
        P(("dp", "fsdp"), None),
        P(("dp", "fsdp"), None),
        P(("dp", "fsdp"), None),
        P(("dp", "fsdp"), None),
        P(("dp", "fsdp")),
        P(("dp", "fsdp"), None),
        P(("dp", "fsdp"), None),
        P(("dp", "fsdp")),
        P(("dp", "fsdp"), None),
        P(("dp", "fsdp"), None),
        P(("dp", "fsdp"), None),
        P(("dp", "fsdp"), None),
        P(("dp", "fsdp")),
        P(("dp", "fsdp"), None),
        P(("dp", "fsdp"), None),
    )
    return jax.shard_map(functools.partial(local, mesh_size=mesh.size), mesh=mesh, in_specs=in_specs, out_specs=out_specs, check_vma=False)
```

```python
import functools

import jax
import jax.numpy as jnp
from jax import lax
from jax.experimental import pallas as pl
from jax.experimental.pallas import tpu as pltpu
from jax.sharding import PartitionSpec as P

HEADS = 8
FRAME_TOK = 64
EPS = 1e-05
NEG = -1000000000.0
F32 = jnp.float32
BF16 = jnp.bfloat16
MESH = pl.DeviceIdType.MESH
NN = (((1,), (0,)), ((), ()))
NT = (((1,), (1,)), ((), ()))
TN = (((0,), (0,)), ((), ()))
GC0 = 0.7978845608
GC1 = 0.044715


def dot(left, right, dims):
    return lax.dot_general(left, right, dims, preferred_element_type=F32)


def low(value):
    return value.astype(BF16)


def flip(value, mask, size):
    out = 0
    bit = 1
    while bit < size:
        one = lax.rem(lax.div(value, jnp.int32(bit)), jnp.int32(2))
        if isinstance(mask, int):
            other = jnp.int32((mask // bit) % 2)
        else:
            other = lax.rem(lax.div(mask, jnp.int32(bit)), jnp.int32(2))
        out = out + lax.rem(one + other, jnp.int32(2)) * bit
        bit *= 2
    return out


def norm_parts(value):
    center = value - jnp.mean(value, axis=-1, keepdims=True)
    spread = jnp.mean(center * center, axis=-1, keepdims=True)
    inv = lax.rsqrt(spread + EPS)
    return center * inv, inv


def norm(value, gain):
    hat, _ = norm_parts(value)
    return low(hat * gain)


def norm_back(value, gain, grad):
    hat, inv = norm_parts(value)
    scaled = grad * gain
    out = inv * (
        scaled
        - jnp.mean(scaled, axis=-1, keepdims=True)
        - hat * jnp.mean(scaled * hat, axis=-1, keepdims=True)
    )
    return out, jnp.sum(grad * hat, axis=0, keepdims=True)


def gelu_both(value):
    square = value * value
    tan = jnp.tanh(GC0 * value * (1.0 + GC1 * square))
    half = 0.5 * (1.0 + tan)
    slope = half + 0.5 * value * (1.0 - tan * tan) * (GC0 * (1.0 + 3.0 * GC1 * square))
    return value * half, slope


INPUTS = ("frames", "gains", "latents", "inputs", "cot",
          "cq", "ck", "cv", "co", "fu", "fd", "sq_", "sk_", "sv_", "so_", "gu_", "gd_")
OUTPUTS = ("out", "glat", "ginp", "ggain",
           "ocq", "ock", "ocv", "oco", "ofu", "ofd", "osq", "osk", "osv", "oso", "ogu", "ogd")


def scratch_list(nd, nf, rows, width, lat, span, heads):
    nz = nf // 2
    hd = width // heads
    tp_cols = width // nd
    four = (nd, nf, rows, width)
    act = (nd, nz, rows, width)
    three = (nd - 1, nz, rows, width)
    vm = pltpu.VMEM
    return {
        "wx": vm((4,) + four, BF16),
        "up1": vm(four, BF16), "dn1": vm(four, BF16),
        "up2": vm(four, BF16), "dn2": vm(four, BF16),
        "sq": vm((3, nd, nf, rows, tp_cols), BF16), "so": vm((nf, rows, width), BF16),
        "sqs": vm((nd, 3, rows, tp_cols), BF16),
        "xn": vm((span, width), BF16), "kk": vm((span, width), BF16), "vv": vm((span, width), BF16),
        "pp": vm((heads, lat, span), BF16),
        "ag1": vm(act, BF16), "u1": vm(act, BF16), "d1": vm(act, BF16), "bg": vm(act, BF16),
        "ag2": vm(act, BF16), "u2": vm(act, BF16), "d2": vm(act, BF16),
        "gg": vm(act, BF16), "ggs": vm(act, BF16),
        "q2": vm((nd, lat, tp_cols), BF16), "k2": vm((nd, lat, tp_cols), BF16),
        "v2": vm((nd, lat, tp_cols), BF16), "c2": vm((nd, lat, tp_cols), BF16),
        "p2": vm((nd, heads // nd, lat, lat), BF16),
        "ra": vm(three, BF16), "rb": vm(three, BF16), "sa": vm(three, BF16), "sc": vm(three, BF16),
        "xw": vm((4,) + three, BF16), "zw": vm((4, nz - 1, rows, width), BF16),
        "GU": vm((2, nz, nd, rows, width), BF16), "GD": vm((2, nz, nd, rows, width), BF16),
        "GQ": vm((2, nz, nd, 3, rows, tp_cols), BF16), "GO": vm((2, nz, rows, width), BF16),
        "SU": vm((nz, nd, rows, width), BF16), "SD": vm((nz, nd, rows, width), BF16),
        "SQ": vm((nz, nd, 3, rows, tp_cols), BF16), "SO": vm((nz, rows, width), BF16),
        "ZU": vm((nz - 1, nd, rows, width), BF16), "ZD": vm((nz - 1, nd, rows, width), BF16),
        "ZQ": vm((nz - 1, nd, 3, rows, tp_cols), BF16), "ZO": vm((nz - 1, rows, width), BF16),
        "CU1": vm((nd - 1, rows, width), BF16), "CU2": vm((nd - 1, rows, width), BF16),
        "CQ": vm((nd - 1, 3, rows, tp_cols), BF16),
        "z1": vm((lat, width), F32), "z2": vm((lat, width), F32), "z3": vm((lat, width), F32),
        "ga": vm((lat, width), F32), "own": vm((lat, width), F32), "st": vm((lat, width), F32),
        "lt": vm((lat, width), BF16), "an": vm((lat, width), BF16), "qq": vm((lat, width), BF16),
        "cc": vm((lat, width), BF16), "gb": vm((lat, width), BF16), "dc": vm((lat, width), BF16),
        "gn": vm((8, width), F32), "dg": vm((8, width), F32),
        "gr": vm((2, 1 + nz - 1 + nd - 1, 8, width), F32),
        "ss": pltpu.SemaphoreType.DMA((SEMS,)), "rs": pltpu.SemaphoreType.DMA((SEMS,)),
        "ls": pltpu.SemaphoreType.DMA((64,)),
    }


SEMS = 224


def layer_kernel(names, nd, nf, rows, *refs):
    r = dict(zip(names, refs))

    class Space:
        pass

    n = Space()
    for key, ref in r.items():
        setattr(n, key, ref)
    nz = nf // 2
    width = n.lt.shape[1]
    lat = n.lt.shape[0]
    span = n.xn.shape[0]
    hd = width // HEADS
    cols = width // nd
    local_heads = HEADS // nd
    scale = hd ** (-0.5)
    a = lax.axis_index("dp")
    b = lax.axis_index("fsdp")
    z = lax.div(b, jnp.int32(2))
    c = lax.rem(b, jnp.int32(2))
    sib = (a, z * 2 + 1 - c)

    def apos(k):
        return flip(a, k, nd)

    def zpos(m):
        return flip(z, m, nz)

    def bpos(m):
        return zpos(m) * 2 + c

    taken = [0, 0]

    def group(count, make):
        base = taken[0]
        taken[0] += count
        assert taken[0] <= SEMS

        def desc(i):
            src, dst, peer = make(i)
            return pltpu.make_async_remote_copy(
                src_ref=src, dst_ref=dst, send_sem=n.ss.at[base + i], recv_sem=n.rs.at[base + i],
                device_id=peer, device_id_type=MESH)

        desc.count = count
        return desc

    def start(g):
        for i in range(g.count):
            g(i).start()

    def recv(g):
        for i in range(g.count):
            g(i).wait_recv()

    def sent(g):
        for i in range(g.count):
            g(i).wait_send()

    def load(src, dst):
        i = taken[1]
        taken[1] += 1
        copy = pltpu.make_async_copy(src, dst, n.ls.at[i])
        copy.start()
        return copy

    def dp_group(src, dst):
        return group(nd - 1, lambda i: (src(i + 1), dst(i + 1), (apos(i + 1), b)))

    def z_group(src, dst):
        return group(nz - 1, lambda i: (src(i + 1), dst(i + 1), (a, bpos(i + 1))))

    def sib_group(src, dst):
        return group(1, lambda i: (src, dst, sib))

    def stage(refs, dst):
        return [load(ref, dst.at[pl.ds(i * rows, rows)]) for i, ref in enumerate(refs)]

    blocks = [pl.ds(j * width, width) for j in range(nd)]
    in_cross = stage((n.cq, n.ck, n.cv, n.co), n.z1)
    in_up1 = stage([n.fu.at[:, s] for s in blocks], n.z2)
    in_dn1 = [load(n.fd, n.z3)]
    in_lat = [load(n.latents.at[0], n.lt)]
    in_x = [load(n.inputs.at[0], n.xn)]
    in_self = stage((n.sq_, n.sk_, n.sv_, n.so_), n.ga)
    in_up2 = stage([n.gu_.at[:, s] for s in blocks], n.own)
    in_dn2 = [load(n.gd_, n.st)]
    in_cot = [load(n.cot.at[0], n.gb)]

    def arrived(copies):
        for copy in copies:
            copy.wait()

    peers = [(apos(k), b) for k in range(1, nd)] + [(a, bpos(m)) for m in range(1, nz)] + [sib]
    barrier = pltpu.get_barrier_semaphore()
    for peer in peers:
        pl.semaphore_signal(barrier, inc=1, device_id=peer, device_id_type=MESH)

    arrived(in_cross)
    for i in range(4):
        n.wx[i, a, b] = low(n.z1[i * rows:(i + 1) * rows])
    pl.semaphore_wait(barrier, len(peers))

    def small_sum(buf, which):
        slots = n.gr.at[which]
        hops = (group(1, lambda i: (buf, slots.at[0], sib)),
                group(nd - 1, lambda i: (buf, slots.at[1 + i], (apos(i + 1), b))),
                group(nz - 1, lambda i: (buf, slots.at[nd + i], (a, bpos(i + 1)))))
        phases = []
        first = 0
        for g in hops:
            def finish(g=g, first=first):
                recv(g)
                sent(g)
                total = buf[...]
                for i in range(g.count):
                    total = total + slots[first + i]
                buf[...] = total

            phases.append((functools.partial(start, g), finish))
            first += g.count
        return phases

    def wx_at(ai, bi):
        return n.wx.at[:, ai, bi]

    cross_z = z_group(lambda m: wx_at(a, b), lambda m: wx_at(a, b))
    cross_dp = []
    for m in range(nz):
        at = wx_at(a, bpos(m))
        cross_dp.append(dp_group(lambda k, at=at: at, lambda k, at=at: at))
    cross_sib = [[sib_group(wx_at(apos(k), bpos(m)), wx_at(apos(k), bpos(m))) for m in range(nz)]
                 for k in range(nd)]
    start(cross_z)
    start(cross_dp[0])
    start(cross_sib[0][0])
    n.gn[...] = low(n.gains[...]).astype(F32)
    for begin, finish in small_sum(n.gn, 0):
        begin()
        finish()

    su1, su2 = n.xw.at[3, 0], n.xw.at[3, 1]

    def put_up(staged, sends, up):
        for j in range(nd):
            sends[j] = low(staged[j * rows:(j + 1) * rows])
        up[a, b] = sends[a]

    def put_dn(staged, dn):
        dn[lax.div(b * nd, jnp.int32(nf)), pl.ds(lax.rem(b * nd, jnp.int32(nf)), nd)] = (
            low(staged[...]).reshape(nd, rows, width))

    def dn_at(dn, bi):
        return dn.at[lax.div(bi * nd, jnp.int32(nf)), pl.ds(lax.rem(bi * nd, jnp.int32(nf)), nd)]

    arrived(in_up1)
    put_up(n.z2, su1, n.up1)
    up1_dp = dp_group(lambda k: su1.at[apos(k)], lambda k: n.up1.at[a, b])
    start(up1_dp)
    arrived(in_dn1)
    put_dn(n.z3, n.dn1)
    arrived(in_self)
    for i in range(3):
        for j in range(nd):
            n.sqs[j, i] = low(n.ga[i * rows:(i + 1) * rows, j * cols:(j + 1) * cols])
    for i in range(3):
        n.sq[i, a, b] = n.sqs[a, i]
    n.so[b] = low(n.ga[3 * rows:4 * rows])
    arrived(in_up2)
    put_up(n.own, su2, n.up2)
    arrived(in_dn2)
    put_dn(n.st, n.dn2)
    arrived(in_cot)
    act_rows = (nz, rows, width)
    n.gg[0] = n.gb[...].reshape(act_rows)

    def up_z(up):
        return z_group(lambda m: up.at[:, b], lambda m: up.at[:, b])

    def up_sib(up):
        return [sib_group(up.at[:, bpos(m)], up.at[:, bpos(m)]) for m in range(nz)]

    def dn_z(dn):
        return z_group(lambda m: dn_at(dn, b), lambda m: dn_at(dn, b))

    def dn_sib(dn):
        return [sib_group(dn_at(dn, bpos(m)), dn_at(dn, bpos(m))) for m in range(nz)]

    gain = [n.gn.at[i:i + 1] for i in range(5)]

    arrived(in_lat)
    n.an[...] = norm(n.lt[...].astype(F32), gain[0][...])
    arrived(in_x)
    for m in range(1, nz):
        cross_z(m - 1).wait_recv()
        start(cross_dp[m])
        start(cross_sib[0][m])

    up1_z, up1_sib, dn1_z, dn1_sib = up_z(n.up1), up_sib(n.up1), dn_z(n.dn1), dn_sib(n.dn1)
    recv(up1_dp)
    start(up1_z)
    start(dn1_z)

    block = lat

    def token_norm(i, _):
        at = pl.ds(pl.multiple_of(i * block, block), block)
        n.xn[at] = norm(n.xn[at].astype(F32), gain[1][...])
        return 0

    lax.fori_loop(0, span // block, token_norm, 0)

    for m in range(nz):
        for k in range(1, nd):
            cross_dp[m](k - 1).wait_recv()
            start(cross_sib[k][m])
    up2_dp = dp_group(lambda k: su2.at[apos(k)], lambda k: n.up2.at[a, b])
    sq_dp = dp_group(lambda k: n.sqs.at[apos(k)], lambda k: n.sq.at[:, a, b])
    cot_dp = dp_group(lambda k: n.gg.at[0], lambda k: n.gg.at[k])
    start(sq_dp)
    start(up2_dp)
    start(cot_dp)
    for k in range(nd):
        for m in range(nz):
            recv(cross_sib[k][m])

    def wcols(i, at):
        return n.wx[i, :, :, :, at].reshape(width, at.size)

    def full(ref):
        return ref[...].reshape(width, width)

    n.qq[...] = low(dot(n.an[...], n.wx[0].reshape(width, width), NN))
    wide = 256

    def token_proj(i, _):
        at = pl.ds(pl.multiple_of(i * wide, wide), wide)
        n.kk[:, at] = low(dot(n.xn[...], wcols(1, at), NN))
        n.vv[:, at] = low(dot(n.xn[...], wcols(2, at), NN))
        return 0

    lax.fori_loop(0, width // wide, token_proj, 0)
    valid = lax.broadcasted_iota(jnp.int32, (lat, span), 1) < n.frames[0] * FRAME_TOK

    def softmax(scores):
        expo = jnp.exp(scores - jnp.max(scores, axis=-1, keepdims=True))
        return low(expo / jnp.sum(expo, axis=-1, keepdims=True))

    def cross_head(h, _):
        at = pl.ds(pl.multiple_of(h * hd, hd), hd)
        scores = jnp.where(valid, dot(n.qq[:, at], n.kk[:, at], NT) * scale, NEG)
        probs = softmax(scores)
        n.pp[h] = probs
        n.cc[:, at] = low(dot(probs, n.vv[:, at], NN))
        return 0

    lax.fori_loop(0, HEADS, cross_head, 0)
    z1 = n.lt[...].astype(F32) + dot(n.cc[...], n.wx[3].reshape(width, width), NN)
    n.z1[...] = z1

    def rows_of(ref, k):
        return ref[k].reshape(lat, width)

    def spread(buf, value):
        buf[0] = value.reshape(act_rows)
        g = dp_group(lambda k: buf.at[0], lambda k: buf.at[k])
        start(g)
        return g

    def collect(make, gathered, sends, slots, previous):
        if previous is not None:
            sent(previous)
        back = dp_group(lambda k: sends.at[k - 1], lambda k: slots.at[k - 1])
        back.gathered = gathered
        n.own[...] = make(0)

        def step(i, _):
            gathered(i).wait_recv()
            sends[i] = low(make(i + 1)).reshape(act_rows)
            back(i).start()
            return 0

        lax.fori_loop(0, nd - 1, step, 0)
        return back

    def gather_sum(back, slots):
        sent(back.gathered)
        total = n.own[...]
        for i in range(nd - 1):
            back(i).wait_recv()
            total = total + slots[i].reshape(lat, width).astype(F32)
        return total

    def feed_make(ag, u, d, up, dn):
        def make(k):
            value, slope = gelu_both(dot(rows_of(ag, k), full(up), NN))
            hidden = low(value)
            u[k] = hidden.reshape(act_rows)
            d[k] = low(slope).reshape(act_rows)
            return dot(hidden, full(dn), NN)

        return make

    ag1_dp = spread(n.ag1, norm(z1, gain[2][...]))
    start(up1_sib[0])
    start(dn1_sib[0])
    for m in range(1, nz):
        up1_z(m - 1).wait_recv()
        start(up1_sib[m])
        dn1_z(m - 1).wait_recv()
        start(dn1_sib[m])
    recv(sq_dp)
    sq_z = z_group(lambda m: n.sq.at[:, :, b], lambda m: n.sq.at[:, :, b])
    so_z = z_group(lambda m: n.so.at[b], lambda m: n.so.at[b])
    sq_sib = [sib_group(n.sq.at[:, :, bpos(m)], n.sq.at[:, :, bpos(m)]) for m in range(nz)]
    so_sib = [sib_group(n.so.at[bpos(m)], n.so.at[bpos(m)]) for m in range(nz)]
    start(sq_z)
    start(so_z)
    start(sq_sib[0])
    start(so_sib[0])
    recv(up2_dp)
    up2_z, up2_sib, dn2_z, dn2_sib = up_z(n.up2), up_sib(n.up2), dn_z(n.dn2), dn_sib(n.dn2)
    start(up2_z)
    start(dn2_z)
    start(up2_sib[0])
    start(dn2_sib[0])
    for m in range(nz):
        recv(up1_sib[m])
        recv(dn1_sib[m])
    out1 = collect(feed_make(n.ag1, n.u1, n.d1, n.up1, n.dn1), ag1_dp, n.sa, n.ra, None)
    for m in range(1, nz):
        sq_z(m - 1).wait_recv()
        start(sq_sib[m])
        so_z(m - 1).wait_recv()
        start(so_sib[m])
    z2 = n.z1[...] + gather_sum(out1, n.ra)
    n.z2[...] = z2

    bg_dp = spread(n.bg, norm(z2, gain[3][...]))
    for m in range(nz):
        recv(sq_sib[m])
        recv(so_sib[m])

    def self_make(k):
        normed = rows_of(n.bg, k)
        for i, ref in enumerate((n.q2, n.k2, n.v2)):
            ref[k] = low(dot(normed, n.sq[i].reshape(width, cols), NN))
        for h in range(local_heads):
            at = slice(h * hd, (h + 1) * hd)
            probs = softmax(dot(n.q2[k, :, at], n.k2[k, :, at], NT) * scale)
            n.p2[k, h] = probs
            n.c2[k, :, at] = low(dot(probs, n.v2[k, :, at], NN))
        return dot(n.c2[k], n.so[...].reshape(cols, width), NN)

    out_self = collect(self_make, bg_dp, n.sa, n.rb, out1)
    z3 = n.z2[...] + gather_sum(out_self, n.rb)
    n.z3[...] = z3

    ag2_dp = spread(n.ag2, norm(z3, gain[4][...]))
    for m in range(1, nz):
        up2_z(m - 1).wait_recv()
        start(up2_sib[m])
        dn2_z(m - 1).wait_recv()
        start(dn2_sib[m])
    recv(cot_dp)
    for m in range(nz):
        recv(up2_sib[m])
        recv(dn2_sib[m])

    sc, rc = n.sc, n.rb

    def feed_back(g, d, up, dn):
        def make(k):
            grad = dot(rows_of(g, k), full(dn), NT)
            grad_low = low(rows_of(d, k).astype(F32) * grad)
            d[k] = grad_low.reshape(act_rows)
            return dot(grad_low, full(up), NT)

        return make

    feed2 = feed_make(n.ag2, n.u2, n.d2, n.up2, n.dn2)
    back2 = feed_back(n.gg, n.d2, n.up2, n.dn2)
    final_dp = dp_group(lambda k: sc.at[k - 1], lambda k: rc.at[k - 1])
    n.st[...] = n.z3[...] + feed2(0)

    def both(k):
        if not isinstance(k, int):
            sc[k - 1] = low(feed2(k)).reshape(act_rows)
        return back2(k)

    sent(up1_dp)
    sent(up2_dp)
    dm2 = collect(both, ag2_dp, n.sa, n.ra, out_self)

    def put_grad(value, ref, first):
        for i in range(value.shape[0] // rows):
            ai, bi = divmod(first + i, nf)
            zi, ci = divmod(bi, 2)
            ref[ci, zi, ai] = value[i * rows:(i + 1) * rows]

    def put_down(value, ref, first):
        for i in range(value.shape[0] // rows):
            bi, ai = divmod(first + i, nd)
            zi, ci = divmod(bi, 2)
            ref[ci, zi, ai] = value[i * rows:(i + 1) * rows]

    tall = 256

    def every_row(ref, at=slice(None)):
        value = ref[:, :, :, at]
        return value.reshape(value.shape[0] * value.shape[1] * value.shape[2], value.shape[3])

    def feed_grads(ag, u, d, g):
        for i in range(width // tall):
            at = slice(i * tall, (i + 1) * tall)
            put_grad(low(dot(every_row(ag, at), every_row(d), TN)), n.GU, i * tall // rows)
            put_down(low(dot(every_row(u, at), every_row(g), TN)), n.GD, i * tall // rows)

    def core_sum(grad, other):
        for i in range(nz):
            grad[c, i] = low(grad[c, i].astype(F32) + other[i].astype(F32))

    def sib_grads(grad, other):
        g = sib_group(grad.at[1 - c], other)
        start(g)
        return g

    def z_grads(grad, slots):
        g = z_group(lambda m: grad.at[c, zpos(m)], lambda m: slots.at[m - 1])
        start(g)
        return g

    def z_total(g, grad, slots):
        recv(g)
        total = grad[c, z].astype(F32)
        for i in range(nz - 1):
            total = total + slots[i].astype(F32)
        return total

    feed_grads(n.ag2, n.u2, n.d2, n.gg)
    gu2_sib = sib_grads(n.GU, n.SU)
    gd2_sib = sib_grads(n.GD, n.SD)

    def set_gain(i, value):
        n.dg[i:i + 1] = value

    n.dg[...] = jnp.zeros_like(n.dg)
    back, gain_part = norm_back(n.z3[...], gain[4][...], gather_sum(dm2, n.ra))
    set_gain(4, gain_part)
    ga = rows_of(n.gg, 0).astype(F32) + back
    n.ga[...] = ga

    gs_dp = spread(n.ggs, low(ga))
    recv(gu2_sib)
    core_sum(n.GU, n.SU)
    recv(gd2_sib)
    core_sum(n.GD, n.SD)
    gu2_z = z_grads(n.GU, n.ZU)
    gd2_z = z_grads(n.GD, n.ZD)

    def attend_back(q, k, v, probs, grad):
        grad_probs = dot(grad, v, NT)
        wide_probs = probs.astype(F32)
        inner = jnp.sum(wide_probs * grad_probs, axis=-1, keepdims=True)
        scores = low(wide_probs * (grad_probs - inner))
        return (low(dot(scores, k, NN) * scale), low(dot(scores, q, TN) * scale),
                low(dot(probs, grad, TN)))

    def self_back(k):
        grad = low(dot(rows_of(n.ggs, k), n.so[...].reshape(cols, width), NT))
        for h in range(local_heads):
            at = slice(h * hd, (h + 1) * hd)
            dq, dk, dv = attend_back(n.q2[k, :, at], n.k2[k, :, at], n.v2[k, :, at],
                                     n.p2[k, h], grad[:, at])
            n.q2[k, :, at] = dq
            n.k2[k, :, at] = dk
            n.v2[k, :, at] = dv
        total = 0.0
        for i, ref in enumerate((n.q2, n.k2, n.v2)):
            total = total + dot(ref[k], n.sq[i].reshape(width, cols), NT)
        return total

    db = collect(self_back, gs_dp, n.sa, n.rb, dm2)
    for i, ref in enumerate((n.q2, n.k2, n.v2)):
        value = low(dot(every_row(n.bg), ref[...].reshape(nd * lat, cols), TN))
        for j in range(width // rows):
            ai, bi = divmod(j, nf)
            zi, ci = divmod(bi, 2)
            n.GQ[ci, zi, ai, i] = value[j * rows:(j + 1) * rows]
    value = low(dot(n.c2[...].reshape(nd * lat, cols), every_row(n.ggs), TN))
    for bi in range(nf):
        zi, ci = divmod(bi, 2)
        n.GO[ci, zi] = value[bi * rows:(bi + 1) * rows]
    gq_sib = sib_grads(n.GQ, n.SQ)
    go_sib = sib_grads(n.GO, n.SO)
    back, gain_part = norm_back(n.z2[...], gain[3][...], gather_sum(db, n.rb))
    set_gain(3, gain_part)
    ga = n.ga[...] + back
    n.ga[...] = ga

    sent(cot_dp)
    outs = []
    gf_dp = spread(n.gg, low(ga))
    recv(gq_sib)
    core_sum(n.GQ, n.SQ)
    recv(go_sib)
    core_sum(n.GO, n.SO)
    gq_z = z_grads(n.GQ, n.ZQ)
    go_z = z_grads(n.GO, n.ZO)
    dm1 = collect(feed_back(n.gg, n.d1, n.up1, n.dn1), gf_dp, n.sa, n.ra, db)
    start(final_dp)

    def out_rows(value, staged, target):
        staged[...] = value.reshape(staged.shape)
        return load(staged, target)

    total = z_total(gd2_z, n.GD, n.ZD)
    outs.append(out_rows(total, n.z3, n.ogd))
    total = z_total(gu2_z, n.GU, n.ZU)

    def column_grads(total, sends, slots):
        sends[...] = low(total)
        g = dp_group(lambda k: sends.at[apos(k)], lambda k: slots.at[k - 1])
        start(g)
        return g

    su3, su4 = n.d2.at[0], n.d2.at[1]
    cu2_dp = column_grads(total, su3, n.CU2)
    for g in (gu2_sib, gd2_sib, gu2_z, gd2_z):
        sent(g)
    feed_grads(n.ag1, n.u1, n.d1, n.gg)
    gu1_sib = sib_grads(n.GU, n.SU)
    gd1_sib = sib_grads(n.GD, n.SD)
    back, gain_part = norm_back(n.z1[...], gain[2][...], gather_sum(dm1, n.ra))
    set_gain(2, gain_part)
    ga = n.ga[...] + back
    n.ga[...] = ga

    n.gb[...] = low(ga)
    mats = (n.up2, n.dn2, n.up1, n.dn1)
    others = (n.u1, n.d1, n.ag1, n.bg)

    def put_cross(value, ref, first):
        for i in range(value.shape[0] // rows):
            ai, bi = divmod(first + i, nf)
            zi, ci = divmod(bi, 2)
            ref[ai, ci * nz + zi] = value[i * rows:(i + 1) * rows]

    def cross_grad(left, right, which):
        for i in range(width // tall):
            put_cross(low(dot(left[:, i * tall:(i + 1) * tall], right, TN)), mats[which],
                      i * tall // rows)

    def half(ref, ci):
        return ref.at[:, pl.ds(ci * nz, nz)]

    for g in up1_sib + dn1_sib + up2_sib + dn2_sib + [up1_z, dn1_z, up2_z, dn2_z]:
        sent(g)
    cross_grad(n.cc, n.gb[...], 3)
    recv(gu1_sib)
    core_sum(n.GU, n.SU)
    recv(gd1_sib)
    core_sum(n.GD, n.SD)
    zu1, zd1 = n.ag2, n.u2
    gu1_z = z_grads(n.GU, zu1)
    gd1_z = z_grads(n.GD, zd1)
    core_dp = [group(1, lambda i, w=w: (half(mats[w], 1 - c), others[w], sib)) for w in range(4)]
    start(core_dp[3])
    n.dc[...] = low(dot(n.gb[...], n.wx[3].reshape(width, width), NT))

    def cross_back(h, _):
        at = pl.ds(pl.multiple_of(h * hd, hd), hd)
        dq, dk, dv = attend_back(n.qq[:, at], n.kk[:, at], n.vv[:, at], n.pp[h], n.dc[:, at])
        n.qq[:, at] = dq
        n.kk[:, at] = dk
        n.vv[:, at] = dv
        return 0

    lax.fori_loop(0, HEADS, cross_back, 0)
    again = [load(n.inputs.at[0, pl.ds(i * block, block)], n.pp.at[i]) for i in range(span // block)]
    cross_grad(n.an, n.qq[...], 0)
    start(core_dp[0])
    cross_grad(n.xn, n.kk[...], 1)
    start(core_dp[1])
    cross_grad(n.xn, n.vv[...], 2)
    start(core_dp[2])

    own_half = pl.ds(c * nz, nz)
    cross_xy, cross_back_z = {}, {}
    for w in (3, 0, 1, 2):
        recv(core_dp[w])
        for ai in range(nd):
            mats[w][ai, own_half] = low(mats[w][ai, own_half].astype(F32) + others[w][ai].astype(F32))
        cross_xy[w] = dp_group(lambda k, w=w: mats[w].at[apos(k), own_half],
                               lambda k, w=w: n.xw.at[w, k - 1])
        start(cross_xy[w])

    back, gain_part = norm_back(n.lt[...].astype(F32), gain[0][...],
                                dot(n.qq[...], n.wx[0].reshape(width, width), NT))
    set_gain(0, gain_part)
    n.gb[...] = low(n.ga[...] + back)
    outs.append(load(n.gb, n.glat.at[0]))
    arrived(again)

    def token_back(i, total):
        at = pl.ds(pl.multiple_of(i * block, block), block)
        grad = (dot(n.kk[at], n.wx[1].reshape(width, width), NT)
                + dot(n.vv[at], n.wx[2].reshape(width, width), NT))
        back, gain_part = norm_back(n.pp[i].astype(F32), gain[1][...], grad)
        n.pp[i] = low(back)
        return total + gain_part

    set_gain(1, lax.fori_loop(0, span // block, token_back, jnp.zeros((1, width), F32)))
    for i in range(span // block):
        outs.append(load(n.pp.at[i], n.ginp.at[0, pl.ds(i * block, block)]))
    gain_hops = small_sum(n.dg, 1)
    gain_hops[0][0]()

    recv(final_dp)
    total = n.st[...]
    for i in range(nd - 1):
        total = total + rc[i].reshape(lat, width).astype(F32)
    n.dc[...] = low(total)
    outs.append(load(n.dc, n.out.at[0]))

    gain_hops[0][1]()
    gain_hops[1][0]()
    total = z_total(gd1_z, n.GD, zd1)
    outs.append(out_rows(total, n.z1, n.ofd))
    cu1_dp = column_grads(z_total(gu1_z, n.GU, zu1), su4, n.CU1)
    total = z_total(go_z, n.GO, n.ZO)
    n.z2[0:rows] = total
    outs.append(load(n.z2.at[0:rows], n.oso))
    total = z_total(gq_z, n.GQ, n.ZQ)
    sq_send = n.sqs
    sent(sq_dp)
    sq_send[...] = low(total)
    cq_dp = dp_group(lambda k: sq_send.at[apos(k)], lambda k: n.CQ.at[k - 1])
    start(cq_dp)

    for w in (3, 0, 1, 2):
        recv(cross_xy[w])
        total = mats[w][a, own_half].astype(F32)
        for i in range(nd - 1):
            total = total + n.xw[w, i].astype(F32)
        mats[w][a, own_half] = low(total)
        cross_back_z[w] = z_group(lambda m, w=w: mats[w].at[a, c * nz + zpos(m)],
                                  lambda m, w=w: n.zw.at[w, m - 1])
        start(cross_back_z[w])

    gain_hops[1][1]()
    gain_hops[2][0]()

    def put_columns(g, own, slots, staged, target):
        staged[0:rows] = own
        copies = [load(staged.at[0:rows], target.at[:, pl.ds(pl.multiple_of(a * width, width), width)])]
        for i in range(nd - 1):
            g(i).wait_recv()
            staged[(i + 1) * rows:(i + 2) * rows] = slots[i].astype(F32)
            copies.append(load(staged.at[(i + 1) * rows:(i + 2) * rows],
                               target.at[:, pl.ds(pl.multiple_of(apos(i + 1) * width, width), width)]))
        return copies

    outs += put_columns(cu2_dp, su3[a].astype(F32), n.CU2, n.st, n.ogu)
    outs += put_columns(cu1_dp, su4[a].astype(F32), n.CU1, n.own, n.ofu)
    recv(cq_dp)
    for i, target in enumerate((n.osq, n.osk, n.osv)):
        at = slice((i + 1) * rows, (i + 2) * rows)
        n.z2[at, pl.ds(pl.multiple_of(a * cols, cols), cols)] = sq_send[a, i].astype(F32)
        for k in range(1, nd):
            n.z2[at, pl.ds(pl.multiple_of(apos(k) * cols, cols), cols)] = n.CQ[k - 1, i].astype(F32)
        outs.append(load(n.z2.at[at], target))
    for w, target in ((3, n.oco), (0, n.ocq), (1, n.ock), (2, n.ocv)):
        recv(cross_back_z[w])
        total = mats[w][a, c * nz + z].astype(F32)
        for i in range(nz - 1):
            total = total + n.zw[w, i].astype(F32)
        at = slice(w * rows, (w + 1) * rows)
        n.ga[at] = total
        outs.append(load(n.ga.at[at], target))
    gain_hops[2][1]()
    outs.append(load(n.dg, n.ggain))
    for g in ([cross_z, final_dp, dm1, sq_z, so_z, gq_sib, go_sib, gq_z, go_z,
               cu1_dp, cu2_dp, cq_dp, gu1_sib, gd1_sib, gu1_z, gd1_z]
              + cross_dp + sq_sib + so_sib + core_dp + list(cross_xy.values()) + list(cross_back_z.values())
              + [g for line in cross_sib for g in line]):
        sent(g)
    arrived(outs)


def layer_norm(value, gain):
    center = value - jnp.mean(value, axis=-1, keepdims=True)
    spread = jnp.mean(center * center, axis=-1, keepdims=True)
    return center * lax.rsqrt(spread + EPS) * gain


def activate(value):
    return jax.nn.gelu(value, approximate=True)


def product(left, right):
    return jnp.dot(left, right, preferred_element_type=jnp.float32)


def weight_grad(left, right):
    return lax.dot_general(
        left, right, (((0,), (0,)), ((), ())), preferred_element_type=jnp.float32
    )


def back_product(grad, weight):
    return lax.dot_general(
        grad, weight, (((1,), (1,)), ((), ())), preferred_element_type=jnp.float32
    )


def plain_norm_back(value, gain, grad):
    _, pull = jax.vjp(layer_norm, value, gain)
    return pull(grad)


def activate_back(value, grad):
    _, pull = jax.vjp(activate, value)
    return pull(grad)[0]


def split_heads(value, groups):
    return value.reshape(groups, -1, HEADS, value.shape[-1] // HEADS)


def merge_heads(value):
    return value.reshape(-1, value.shape[2] * value.shape[3])


def masked_scores(query, key, valid):
    scale = query.shape[-1] ** (-0.5)
    scores = jnp.einsum("gqhd,gkhd->ghqk", query, key, preferred_element_type=jnp.float32) * scale
    return jnp.where(valid[:, None, None, :], scores, NEG)


def attend_forward(query, key, value, valid):
    scores = masked_scores(query, key, valid)
    top = jnp.max(scores, axis=-1, keepdims=True)
    expo = jnp.exp(scores - top)
    denom = jnp.sum(expo, axis=-1, keepdims=True)
    weights = (expo / denom).astype(jnp.bfloat16)
    mixed = jnp.einsum("ghqk,gkhd->gqhd", weights, value, preferred_element_type=jnp.float32)
    return (merge_heads(mixed).astype(jnp.bfloat16), top + jnp.log(denom))


def plain_attend_back(query, key, value, valid, logsum, grad_mixed):
    scale = query.shape[-1] ** (-0.5)
    probs = jnp.exp(masked_scores(query, key, valid) - logsum)
    grad_probs = jnp.einsum(
        "gqhd,gkhd->ghqk", grad_mixed, value, preferred_element_type=jnp.float32
    )
    inner = jnp.sum(probs * grad_probs, axis=-1, keepdims=True)
    grad_scores = (probs * (grad_probs - inner)).astype(jnp.bfloat16)
    weights = probs.astype(jnp.bfloat16)
    grad_query = (
        jnp.einsum("ghqk,gkhd->gqhd", grad_scores, key, preferred_element_type=jnp.float32) * scale
    )
    grad_key = (
        jnp.einsum("ghqk,gqhd->gkhd", grad_scores, query, preferred_element_type=jnp.float32)
        * scale
    )
    grad_value = jnp.einsum(
        "ghqk,gqhd->gkhd", weights, grad_mixed, preferred_element_type=jnp.float32
    )
    return (
        merge_heads(grad_query).astype(jnp.bfloat16),
        merge_heads(grad_key).astype(jnp.bfloat16),
        merge_heads(grad_value).astype(jnp.bfloat16),
    )


def feed_forward(resid, gain, w_up, w_down):
    normed = layer_norm(resid, gain.astype(jnp.float32)).astype(jnp.bfloat16)
    before = product(normed, w_up)
    hidden = activate(before).astype(jnp.bfloat16)
    return (resid + product(hidden, w_down), (normed, before, hidden))


def plain_feed_back(grad, resid, gain, saved, w_up, w_down):
    normed, before, hidden = saved
    grad_low = grad.astype(jnp.bfloat16)
    grad_down = weight_grad(hidden, grad_low)
    grad_before = activate_back(before, back_product(grad_low, w_down)).astype(jnp.bfloat16)
    grad_up = weight_grad(normed, grad_before)
    grad_resid, grad_gain = plain_norm_back(
        resid, gain.astype(jnp.float32), back_product(grad_before, w_up)
    )
    return (grad + grad_resid, grad_gain, grad_up, grad_down)


def project_back(grad, mixed, w_out, query, key, value, valid, logsum, groups):
    grad_low = grad.astype(jnp.bfloat16)
    grad_out = weight_grad(mixed, grad_low)
    grad_mixed = back_product(grad_low, w_out).astype(jnp.bfloat16)
    grad_query, grad_key, grad_value = plain_attend_back(
        split_heads(query, groups),
        split_heads(key, groups),
        split_heads(value, groups),
        valid,
        logsum,
        split_heads(grad_mixed, groups),
    )
    return (grad_out, grad_query, grad_key, grad_value)


def plain_layer(
    latents,
    inputs,
    frames,
    norm_latent,
    norm_input,
    cross_query,
    cross_key,
    cross_value,
    cross_output,
    norm_first,
    first_up,
    first_down,
    norm_self,
    self_query,
    self_key,
    self_value,
    self_output,
    norm_second,
    second_up,
    second_down,
    cotangent,
    mesh_size,
):
    groups, lat_rows, width = latents.shape
    span = inputs.shape[1]
    hidden_width = first_up.shape[1]
    low_type = jnp.bfloat16
    parts = mesh_size
    gains = (norm_latent, norm_input, norm_first, norm_self, norm_second)
    mats = (cross_query, cross_key, cross_value, cross_output, first_up, first_down,
            self_query, self_key, self_value, self_output, second_up, second_down)
    blocks = []
    for mat in mats:
        for start in range(0, mat.shape[1], width):
            blocks.append(mat[:, start:start + width])
    gain_row = jnp.concatenate([jnp.concatenate(gains), jnp.zeros((width - 5 * gains[0].shape[0],), jnp.float32)])
    gain_rows = jnp.concatenate([gain_row[None], jnp.zeros((15, width), jnp.float32)])
    packed = jnp.concatenate([gain_rows] + blocks).astype(low_type)
    whole = lax.all_gather(packed, ("dp", "fsdp"), axis=0, tiled=False)
    per = gains[0].shape[0]
    gathered_gains = [whole[:, 0, i * per:(i + 1) * per].reshape(width) for i in range(5)]
    gain_lat, gain_inp, gain_first, gain_self, gain_second = gathered_gains
    at = 16
    full = []
    for mat in mats:
        columns = []
        for start in range(0, mat.shape[1], width):
            columns.append(whole[:, at:at + mat.shape[0]].reshape(parts * mat.shape[0], width))
            at += mat.shape[0]
        full.append(columns[0] if len(columns) == 1 else jnp.concatenate(columns, axis=1))
    w_query, w_key, w_value, w_out, up_one, down_one, s_query, s_key, s_value, s_out, up_two, down_two = full
    positions = jnp.arange(span, dtype=jnp.int32)
    valid = positions[None, :] < (frames * FRAME_TOK)[:, None]
    every = jnp.ones((groups, lat_rows), dtype=bool)
    latent_rows = latents.reshape(groups * lat_rows, width).astype(jnp.float32)
    input_rows = inputs.reshape(groups * span, width).astype(jnp.float32)
    normed_lat = layer_norm(latent_rows, gain_lat.astype(jnp.float32)).astype(low_type)
    normed_inp = layer_norm(input_rows, gain_inp.astype(jnp.float32)).astype(low_type)
    query_one = product(normed_lat, w_query).astype(low_type)
    key_one = product(normed_inp, w_key).astype(low_type)
    value_one = product(normed_inp, w_value).astype(low_type)
    mixed_one, logsum_one = attend_forward(
        split_heads(query_one, groups),
        split_heads(key_one, groups),
        split_heads(value_one, groups),
        valid,
    )
    first_resid = latent_rows + product(mixed_one, w_out)
    second_resid, saved_one = feed_forward(first_resid, gain_first, up_one, down_one)
    normed_self = layer_norm(second_resid, gain_self.astype(jnp.float32)).astype(low_type)
    query_two = product(normed_self, s_query).astype(low_type)
    key_two = product(normed_self, s_key).astype(low_type)
    value_two = product(normed_self, s_value).astype(low_type)
    mixed_two, logsum_two = attend_forward(
        split_heads(query_two, groups),
        split_heads(key_two, groups),
        split_heads(value_two, groups),
        every,
    )
    third_resid = second_resid + product(mixed_two, s_out)
    final_resid, saved_two = feed_forward(third_resid, gain_second, up_two, down_two)
    result = final_resid.reshape(groups, lat_rows, width).astype(low_type)
    grad_final = cotangent.reshape(groups * lat_rows, width).astype(jnp.float32)
    grad_third, grad_gain_second, grad_up_two, grad_down_two = plain_feed_back(
        grad_final, third_resid, gain_second, saved_two, up_two, down_two
    )
    grad_s_out, grad_query_two, grad_key_two, grad_value_two = project_back(
        grad_third, mixed_two, s_out, query_two, key_two, value_two, every, logsum_two, groups
    )
    grad_s_query = weight_grad(normed_self, grad_query_two)
    grad_s_key = weight_grad(normed_self, grad_key_two)
    grad_s_value = weight_grad(normed_self, grad_value_two)
    grad_normed_self = (
        back_product(grad_query_two, s_query)
        + back_product(grad_key_two, s_key)
        + back_product(grad_value_two, s_value)
    )
    grad_from_self, grad_gain_self = plain_norm_back(
        second_resid, gain_self.astype(jnp.float32), grad_normed_self
    )
    grad_second = grad_third + grad_from_self
    grad_first, grad_gain_first, grad_up_one, grad_down_one = plain_feed_back(
        grad_second, first_resid, gain_first, saved_one, up_one, down_one
    )
    grad_w_out, grad_query_one, grad_key_one, grad_value_one = project_back(
        grad_first, mixed_one, w_out, query_one, key_one, value_one, valid, logsum_one, groups
    )
    grad_w_query = weight_grad(normed_lat, grad_query_one)
    grad_w_key = weight_grad(normed_inp, grad_key_one)
    grad_w_value = weight_grad(normed_inp, grad_value_one)
    grad_from_lat, grad_gain_lat = plain_norm_back(
        latent_rows, gain_lat.astype(jnp.float32), back_product(grad_query_one, w_query)
    )
    grad_latent_rows = grad_first + grad_from_lat
    grad_normed_inp = back_product(grad_key_one, w_key) + back_product(grad_value_one, w_value)
    grad_input_rows, grad_gain_inp = plain_norm_back(
        input_rows, gain_inp.astype(jnp.float32), grad_normed_inp
    )
    grad_mats = (grad_w_query, grad_w_key, grad_w_value, grad_w_out, grad_up_one, grad_down_one,
                 grad_s_query, grad_s_key, grad_s_value, grad_s_out, grad_up_two, grad_down_two)
    gain_grads = jnp.stack([grad_gain_lat, grad_gain_inp, grad_gain_first, grad_gain_self, grad_gain_second])
    gain_grads = jnp.moveaxis(gain_grads.reshape(5, parts, per), 1, 0).reshape(parts, 1, 5 * per)
    gain_grads = jnp.pad(gain_grads, ((0, 0), (0, 15), (0, width - 5 * per)))
    pieces = [gain_grads.astype(low_type)]
    for grad in grad_mats:
        for start in range(0, grad.shape[1], width):
            pieces.append(grad[:, start:start + width].reshape(parts, -1, width).astype(low_type))
    summed = lax.psum_scatter(jnp.concatenate(pieces, axis=1), ("dp", "fsdp"), scatter_dimension=0, tiled=False)
    summed = summed.astype(jnp.float32)
    gain_out = [summed[0, i * per:(i + 1) * per] for i in range(5)]
    at = 16
    out = []
    for mat in mats:
        columns = []
        for start in range(0, mat.shape[1], width):
            columns.append(summed[at:at + mat.shape[0]])
            at += mat.shape[0]
        out.append(columns[0] if len(columns) == 1 else jnp.concatenate(columns, axis=1))
    grad_latents = grad_latent_rows.reshape(groups, lat_rows, width).astype(low_type)
    grad_inputs = grad_input_rows.reshape(groups, span, width).astype(low_type)
    return (
        result, grad_latents, grad_inputs,
        gain_out[0], gain_out[1], out[0], out[1], out[2], out[3],
        gain_out[2], out[4], out[5],
        gain_out[3], out[6], out[7], out[8], out[9],
        gain_out[4], out[10], out[11],
    )


def fits(mesh, lat, span, width, hidden):
    nd, nf = mesh.shape["dp"], mesh.shape["fsdp"]
    return (nf == 2 * nd and nd & (nd - 1) == 0 and HEADS % nd == 0 and hidden == nd * width
            and width % (32 * nd * nf) == 0 and span == HEADS * lat and width // HEADS % 128 == 0)


def local(latents, inputs, frames, *rest, mesh):
    nd, nf = mesh.shape["dp"], mesh.shape["fsdp"]
    groups, lat, width = latents.shape
    span = inputs.shape[1]
    if groups != 1 or not fits(mesh, lat, span, width, rest[7].shape[1]):
        return plain_layer(latents, inputs, frames, *rest, mesh_size=mesh.size)
    (norm_latent, norm_input, cross_query, cross_key, cross_value, cross_output, norm_first, first_up,
     first_down, norm_self, self_query, self_key, self_value, self_output, norm_second, second_up,
     second_down, cotangent) = rest
    rows = cross_query.shape[0]
    index = lax.axis_index("dp") * nf + lax.axis_index("fsdp")
    gains = jnp.stack([norm_latent, norm_input, norm_first, norm_self, norm_second])
    gains = jnp.pad(gains, ((0, 3), (0, 0)))
    gains = lax.dynamic_update_slice(jnp.zeros((8, width), F32), gains, (0, index * rows))
    scratch = scratch_list(nd, nf, rows, width, lat, span, HEADS)
    anywhere = pl.BlockSpec(memory_space=pl.ANY)
    out_shape = (
        [jax.ShapeDtypeStruct(latents.shape, BF16)] * 2 + [jax.ShapeDtypeStruct(inputs.shape, BF16)]
        + [jax.ShapeDtypeStruct((8, width), F32)]
        + [jax.ShapeDtypeStruct(w.shape, F32) for w in (
            cross_query, cross_key, cross_value, cross_output, first_up, first_down,
            self_query, self_key, self_value, self_output, second_up, second_down)])
    flops = 2 * 3 * (lat * width * width * 22 + span * width * width * 2)
    (result, grad_latents, grad_inputs, gain_grads, g_cq, g_ck, g_cv, g_co, g_fu, g_fd,
     g_sq, g_sk, g_sv, g_so, g_gu, g_gd) = pl.pallas_call(
        functools.partial(layer_kernel, INPUTS + OUTPUTS + tuple(scratch), nd, nf, rows),
        out_shape=out_shape,
        in_specs=[pl.BlockSpec(memory_space=pltpu.SMEM), pl.BlockSpec(memory_space=pltpu.VMEM)]
        + [anywhere] * (len(INPUTS) - 2),
        out_specs=[anywhere] * len(OUTPUTS),
        scratch_shapes=list(scratch.values()),
        compiler_params=pltpu.CompilerParams(
            collective_id=0, has_side_effects=True, vmem_limit_bytes=64 * 1024 * 1024),
        cost_estimate=pl.CostEstimate(flops=flops, bytes_accessed=30_000_000, transcendentals=4_000_000),
        name="layer",
    )(frames, gains, latents, inputs, cotangent, cross_query, cross_key, cross_value, cross_output,
      first_up, first_down, self_query, self_key, self_value, self_output, second_up, second_down)
    own = lax.dynamic_slice(gain_grads, (0, index * rows), (8, rows))
    return (result, grad_latents, grad_inputs, own[0], own[1], g_cq, g_ck, g_cv, g_co, own[2], g_fu, g_fd,
            own[3], g_sq, g_sk, g_sv, g_so, own[4], g_gu, g_gd)


def solution(mesh):
    in_specs = (
        P(("dp", "fsdp"), None, None),
        P(("dp", "fsdp"), None, None),
        P(("dp", "fsdp")),
        P(("dp", "fsdp")),
        P(("dp", "fsdp")),
        P(("dp", "fsdp"), None),
        P(("dp", "fsdp"), None),
        P(("dp", "fsdp"), None),
        P(("dp", "fsdp"), None),
        P(("dp", "fsdp")),
        P(("dp", "fsdp"), None),
        P(("dp", "fsdp"), None),
        P(("dp", "fsdp")),
        P(("dp", "fsdp"), None),
        P(("dp", "fsdp"), None),
        P(("dp", "fsdp"), None),
        P(("dp", "fsdp"), None),
        P(("dp", "fsdp")),
        P(("dp", "fsdp"), None),
        P(("dp", "fsdp"), None),
        P(("dp", "fsdp"), None, None),
    )
    out_specs = (
        P(("dp", "fsdp"), None, None),
        P(("dp", "fsdp"), None, None),
        P(("dp", "fsdp"), None, None),
        P(("dp", "fsdp")),
        P(("dp", "fsdp")),
        P(("dp", "fsdp"), None),
        P(("dp", "fsdp"), None),
        P(("dp", "fsdp"), None),
        P(("dp", "fsdp"), None),
        P(("dp", "fsdp")),
        P(("dp", "fsdp"), None),
        P(("dp", "fsdp"), None),
        P(("dp", "fsdp")),
        P(("dp", "fsdp"), None),
        P(("dp", "fsdp"), None),
        P(("dp", "fsdp"), None),
        P(("dp", "fsdp"), None),
        P(("dp", "fsdp")),
        P(("dp", "fsdp"), None),
        P(("dp", "fsdp"), None),
    )
    return jax.shard_map(functools.partial(local, mesh=mesh), mesh=mesh, in_specs=in_specs, out_specs=out_specs,
                         check_vma=False)
```

```python
import functools

import jax
import jax.numpy as jnp
from jax import lax
from jax.experimental import pallas as pl
from jax.experimental.pallas import tpu as pltpu
from jax.sharding import PartitionSpec as P

HEADS = 8
FRAME_TOK = 64
EPS = 1e-05
NEG = -1000000000.0
F32 = jnp.float32
BF16 = jnp.bfloat16
MESH = pl.DeviceIdType.MESH
NN = (((1,), (0,)), ((), ()))
NT = (((1,), (1,)), ((), ()))
TN = (((0,), (0,)), ((), ()))
GC0 = 0.7978845608
GC1 = 0.044715


def dot(left, right, dims):
    return lax.dot_general(left, right, dims, preferred_element_type=F32)


def low(value):
    return value.astype(BF16)


def flip(value, mask, size):
    out = 0
    bit = 1
    while bit < size:
        one = lax.rem(lax.div(value, jnp.int32(bit)), jnp.int32(2))
        if isinstance(mask, int):
            other = jnp.int32((mask // bit) % 2)
        else:
            other = lax.rem(lax.div(mask, jnp.int32(bit)), jnp.int32(2))
        out = out + lax.rem(one + other, jnp.int32(2)) * bit
        bit *= 2
    return out


def norm_parts(value):
    center = value - jnp.mean(value, axis=-1, keepdims=True)
    spread = jnp.mean(center * center, axis=-1, keepdims=True)
    inv = lax.rsqrt(spread + EPS)
    return center * inv, inv


def norm(value, gain):
    hat, _ = norm_parts(value)
    return low(hat * gain)


def norm_back(value, gain, grad):
    hat, inv = norm_parts(value)
    scaled = grad * gain
    out = inv * (
        scaled
        - jnp.mean(scaled, axis=-1, keepdims=True)
        - hat * jnp.mean(scaled * hat, axis=-1, keepdims=True)
    )
    return out, jnp.sum(grad * hat, axis=0, keepdims=True)


def gelu_both(value):
    square = value * value
    tan = jnp.tanh(GC0 * value * (1.0 + GC1 * square))
    half = 0.5 * (1.0 + tan)
    slope = half + 0.5 * value * (1.0 - tan * tan) * (GC0 * (1.0 + 3.0 * GC1 * square))
    return value * half, slope


INPUTS = ("frames", "gains", "latents", "inputs", "cot",
          "cq", "ck", "cv", "co", "fu", "fd", "sq_", "sk_", "sv_", "so_", "gu_", "gd_")
OUTPUTS = ("out", "glat", "ginp", "ggain",
           "ocq", "ock", "ocv", "oco", "ofu", "ofd", "osq", "osk", "osv", "oso", "ogu", "ogd")


def scratch_list(nd, nf, rows, width, lat, span, heads):
    nz = nf // 2
    hd = width // heads
    tp_cols = width // nd
    four = (nd, nf, rows, width)
    act = (nd, nz, rows, width)
    three = (nd - 1, nz, rows, width)
    vm = pltpu.VMEM
    return {
        "wx": vm((4,) + four, BF16),
        "up1": vm(four, BF16), "dn1": vm(four, BF16),
        "up2": vm(four, BF16), "dn2": vm(four, BF16),
        "sq": vm((3, nd, nf, rows, tp_cols), BF16), "so": vm((nf, rows, width), BF16),
        "sqs": vm((nd, 3, rows, tp_cols), BF16),
        "xn": vm((span, width), BF16), "kk": vm((span, width), BF16), "vv": vm((span, width), BF16),
        "pp": vm((heads, lat, span), BF16),
        "ag1": vm(act, BF16), "u1": vm(act, BF16), "d1": vm(act, BF16), "bg": vm(act, BF16),
        "ag2": vm(act, BF16), "u2": vm(act, BF16), "d2": vm(act, BF16),
        "gg": vm(act, BF16), "ggs": vm(act, BF16),
        "q2": vm((nd, lat, tp_cols), BF16), "k2": vm((nd, lat, tp_cols), BF16),
        "v2": vm((nd, lat, tp_cols), BF16), "c2": vm((nd, lat, tp_cols), BF16),
        "p2": vm((nd, heads // nd, lat, lat), BF16),
        "ra": vm(three, BF16), "rb": vm(three, BF16), "sa": vm(three, BF16), "sc": vm(three, BF16),
        "xw": vm((4,) + three, BF16),
        "GU": vm((2, nz, nd, rows, width), BF16), "GD": vm((2, nz, nd, rows, width), BF16),
        "GQ": vm((2, nz, nd, 3, rows, tp_cols), BF16), "GO": vm((2, nz, rows, width), BF16),
        "SU": vm((nz, nd, rows, width), BF16), "SD": vm((nz, nd, rows, width), BF16),
        "SQ": vm((nz, nd, 3, rows, tp_cols), BF16), "SO": vm((nz, rows, width), BF16),
        "ZU": vm((nz, nd, rows, width), BF16), "ZD": vm((nz, nd, rows, width), BF16),
        "ZQ": vm((nz, nd, 3, rows, tp_cols), BF16), "ZO": vm((nz, rows, width), BF16),
        "CU1": vm((nd - 1, rows, width), BF16), "CU2": vm((nd - 1, rows, width), BF16),
        "CQ": vm((nd - 1, 3, rows, tp_cols), BF16),
        "z1": vm((lat, width), F32), "z2": vm((lat, width), F32), "z3": vm((lat, width), F32),
        "ga": vm((lat, width), F32), "own": vm((lat, width), F32), "st": vm((lat, width), F32),
        "lt": vm((lat, width), BF16), "an": vm((lat, width), BF16), "qq": vm((lat, width), BF16),
        "cc": vm((lat, width), BF16), "gb": vm((lat, width), BF16), "dc": vm((lat, width), BF16),
        "gn": vm((8, width), F32), "dg": vm((8, width), F32),
        "gr": vm((1 + nz - 1 + nd - 1, 8, width), F32), "gs": vm((nd, nf, 8, 128), F32),
        "ss": pltpu.SemaphoreType.DMA((SEMS,)), "rs": pltpu.SemaphoreType.DMA((SEMS,)),
        "ls": pltpu.SemaphoreType.DMA((64,)),
    }


SEMS = 320


def layer_kernel(names, nd, nf, rows, *refs):
    r = dict(zip(names, refs))

    class Space:
        pass

    n = Space()
    for key, ref in r.items():
        setattr(n, key, ref)
    nz = nf // 2
    width = n.lt.shape[1]
    lat = n.lt.shape[0]
    span = n.xn.shape[0]
    hd = width // HEADS
    cols = width // nd
    local_heads = HEADS // nd
    scale = hd ** (-0.5)
    a = lax.axis_index("dp")
    b = lax.axis_index("fsdp")
    z = lax.div(b, jnp.int32(2))
    c = lax.rem(b, jnp.int32(2))
    sib = (a, z * 2 + 1 - c)

    def apos(k):
        return flip(a, k, nd)

    def zpos(m):
        return flip(z, m, nz)

    def bpos(m):
        return zpos(m) * 2 + c

    taken = [0, 0]

    def group(count, make):
        base = taken[0]
        taken[0] += count
        assert taken[0] <= SEMS

        def desc(i):
            src, dst, peer, *where = make(i)
            return pltpu.make_async_remote_copy(
                src_ref=src, dst_ref=dst, send_sem=n.ss.at[base + i],
                recv_sem=n.rs.at[base + (where[0] if where else i)],
                device_id=peer, device_id_type=MESH)

        desc.count = count
        return desc

    def start(g):
        for i in range(g.count):
            g(i).start()

    def recv(g):
        for i in range(g.count):
            g(i).wait_recv()

    def sent(g):
        if hasattr(g, "sent"):
            g.sent()
            return
        for i in range(g.count):
            g(i).wait_send()

    def load(src, dst):
        i = taken[1]
        taken[1] += 1
        copy = pltpu.make_async_copy(src, dst, n.ls.at[i])
        copy.start()
        return copy

    def dp_group(src, dst):
        return group(nd - 1, lambda i: (src(i + 1), dst(i + 1), (apos(i + 1), b)))

    inner = lax.rem(z, jnp.int32(3)) != 0
    outer = jnp.logical_not(inner)

    class Gather:
        def __init__(self, block):
            self.g = group(4, lambda i: (
                (block(b), block(b), (a, bpos(i + 1))) if i < 3
                else (block(bpos(2)), block(bpos(2)), (a, bpos(1)), 2)))

        def start(self):
            self.g(1).start()
            self.g(0).start()
            pl.when(inner)(lambda: self.g(2).start())

        def relay(self):
            self.g(1).wait_recv()
            pl.when(inner)(lambda: self.g(3).start())

        def recv(self, m):
            self.g(m - 1).wait_recv()

        def sent(self):
            self.g(0).wait_send()
            self.g(1).wait_send()

            @pl.when(inner)
            def _():
                self.g(2).wait_send()
                self.g(3).wait_send()

    class Reduce:
        def __init__(self, part, slots):
            self.part, self.slots = part, slots
            self.g = group(4, lambda i: (
                (part(zpos(i + 1)), slots.at[i], (a, bpos(i + 1))) if i < 3
                else (part(zpos(3)), slots.at[3], (a, bpos(1)))))

        def start(self):
            @pl.when(outer)
            def _():
                self.g(3).start()
                self.g(1).start()

            pl.when(inner)(lambda: self.g(2).start())
            self.g(0).start()

        def combine(self):
            @pl.when(inner)
            def _():
                self.g(3).wait_recv()
                ref = self.part(zpos(2))
                ref[...] = low(ref[...].astype(F32) + self.slots[3].astype(F32))
                self.g(1).start()

        def total(self):
            self.g(0).wait_recv()
            self.g(1).wait_recv()
            ref = self.part(z)

            @pl.when(inner)
            def _():
                self.g(2).wait_recv()
                ref[...] = low(ref[...].astype(F32) + self.slots[2].astype(F32))

            return ref[...].astype(F32) + self.slots[0].astype(F32) + self.slots[1].astype(F32)

        def sent(self):
            self.g(0).wait_send()
            self.g(1).wait_send()
            pl.when(outer)(lambda: self.g(3).wait_send())
            pl.when(inner)(lambda: self.g(2).wait_send())

    class Share:
        def __init__(self, one, two, three):
            def make(i):
                if i in (0, 2):
                    return one(i // 2) + ((apos(1), b),)
                if i in (1, 3):
                    return two(1 - i // 2) + ((apos(2), b),)
                return three(i - 4) + ((apos(2 - (i - 4)), b),)

            self.g = group(6, make)

        def start(self):
            for i in range(4):
                self.g(i).start()

        def relay(self):
            for i in range(2):
                self.g(i).wait_recv()
                self.g(4 + i).start()

        def recv(self, k):
            if isinstance(k, int):
                for i in ((2,), (3,), (4, 5))[k - 1]:
                    self.g(i).wait_recv()
                return
            for j in (1, 2, 3):
                pl.when(k == j)(lambda j=j: self.recv(j))

        def sent(self):
            for i in range(6):
                self.g(i).wait_send()

    def sib_group(src, dst):
        return group(1, lambda i: (src, dst, sib))

    def stage(refs, dst):
        return [load(ref, dst.at[pl.ds(i * rows, rows)]) for i, ref in enumerate(refs)]

    blocks = [pl.ds(j * width, width) for j in range(nd)]
    in_cross = stage((n.cq, n.ck, n.cv, n.co), n.z1)
    in_up1 = stage([n.fu.at[:, s] for s in blocks], n.z2)
    in_dn1 = [load(n.fd, n.z3)]
    in_lat = [load(n.latents.at[0], n.lt)]
    in_x = [load(n.inputs.at[0], n.xn)]
    in_self = stage((n.sq_, n.sk_, n.sv_, n.so_), n.ga)
    in_up2 = stage([n.gu_.at[:, s] for s in blocks], n.own)
    in_dn2 = [load(n.gd_, n.st)]
    in_cot = [load(n.cot.at[0], n.gb)]

    def arrived(copies):
        for copy in copies:
            copy.wait()

    peers = [(apos(k), b) for k in range(1, nd)] + [(a, bpos(m)) for m in range(1, nz)] + [sib]
    barrier = pltpu.get_barrier_semaphore()
    for peer in peers:
        pl.semaphore_signal(barrier, inc=1, device_id=peer, device_id_type=MESH)

    def small_sum(buf):
        slots = n.gr
        hops = (group(1, lambda i: (buf, slots.at[0], sib)),
                group(nd - 1, lambda i: (buf, slots.at[1 + i], (apos(i + 1), b))),
                group(nz - 1, lambda i: (buf, slots.at[nd + i], (a, bpos(i + 1)))))
        phases = []
        first = 0
        for g in hops:
            def finish(g=g, first=first):
                recv(g)
                sent(g)
                total = buf[...]
                for i in range(g.count):
                    total = total + slots[first + i]
                buf[...] = total

            phases.append((functools.partial(start, g), finish))
            first += g.count
        return phases

    pl.semaphore_wait(barrier, len(peers))
    n.gs[a, b] = low(n.gains[...]).astype(F32)
    gains_z = Gather(lambda bi: n.gs.at[a, bi])
    gains_sib = [sib_group(n.gs.at[a, bpos(m)], n.gs.at[a, bpos(m)]) for m in range(nz)]
    gains_dp = dp_group(lambda k: n.gs.at[a], lambda k: n.gs.at[a])
    gains_z.start()
    start(gains_sib[0])
    arrived(in_cross)
    for i in range(4):
        n.wx[i, a, b] = low(n.z1[i * rows:(i + 1) * rows])

    def wx_at(ai, bi):
        return n.wx.at[:, ai, bi]

    cross_z = Gather(lambda bi: n.wx.at[:, a, bi])
    cross_dp = []
    for m in range(nz):
        def direct(h, m=m):
            at = n.wx.at[2 * h:2 * h + 2, a, bpos(m)]
            return at, at

        def relayed(h, m=m):
            at = n.wx.at[2 * h:2 * h + 2, apos(1 + h), bpos(m)]
            return at, at

        cross_dp.append(Share(direct, direct, relayed))
    cross_sib = [[sib_group(wx_at(apos(k), bpos(m)), wx_at(apos(k), bpos(m))) for m in range(nz)]
                 for k in range(nd)]
    cross_z.start()
    cross_dp[0].start()
    start(cross_sib[0][0])

    su1, su2 = n.xw.at[3, 0], n.xw.at[3, 1]

    def put_up(staged, sends, up):
        for j in range(nd):
            sends[j] = low(staged[j * rows:(j + 1) * rows])
        up[a, b] = sends[a]

    def put_dn(staged, dn):
        dn[lax.div(b * nd, jnp.int32(nf)), pl.ds(lax.rem(b * nd, jnp.int32(nf)), nd)] = (
            low(staged[...]).reshape(nd, rows, width))

    def dn_at(dn, bi):
        return dn.at[lax.div(bi * nd, jnp.int32(nf)), pl.ds(lax.rem(bi * nd, jnp.int32(nf)), nd)]

    arrived(in_up1)
    put_up(n.z2, su1, n.up1)
    up1_dp = dp_group(lambda k: su1.at[apos(k)], lambda k: n.up1.at[a, b])
    start(up1_dp)
    arrived(in_dn1)
    put_dn(n.z3, n.dn1)
    arrived(in_self)
    for i in range(3):
        for j in range(nd):
            n.sqs[j, i] = low(n.ga[i * rows:(i + 1) * rows, j * cols:(j + 1) * cols])
    for i in range(3):
        n.sq[i, a, b] = n.sqs[a, i]
    n.so[b] = low(n.ga[3 * rows:4 * rows])
    arrived(in_up2)
    put_up(n.own, su2, n.up2)
    arrived(in_dn2)
    put_dn(n.st, n.dn2)
    arrived(in_cot)
    act_rows = (nz, rows, width)

    def up_z(up):
        return Gather(lambda bi: up.at[:, bi])

    def up_sib(up):
        return [sib_group(up.at[:, bpos(m)], up.at[:, bpos(m)]) for m in range(nz)]

    def dn_z(dn):
        return Gather(lambda bi: dn_at(dn, bi))

    def dn_sib(dn):
        return [sib_group(dn_at(dn, bpos(m)), dn_at(dn, bpos(m))) for m in range(nz)]

    gain = [n.gn.at[i:i + 1] for i in range(5)]

    arrived(in_lat)
    arrived(in_x)
    gains_z.relay()
    start(gains_sib[2])
    gains_z.recv(1)
    start(gains_sib[1])
    gains_z.recv(3)
    start(gains_sib[3])
    for g in gains_sib:
        recv(g)
    start(gains_dp)
    cross_z.relay()
    cross_dp[2].start()
    start(cross_sib[0][2])
    cross_z.recv(1)
    cross_dp[1].start()
    start(cross_sib[0][1])
    cross_dp[0].relay()
    cross_z.recv(3)
    cross_dp[3].start()
    start(cross_sib[0][3])
    up1_z, up1_sib, dn1_z, dn1_sib = up_z(n.up1), up_sib(n.up1), dn_z(n.dn1), dn_sib(n.dn1)
    recv(up1_dp)
    up1_z.start()
    dn1_z.start()
    cross_dp[2].relay()
    cross_dp[1].relay()
    recv(gains_dp)
    per = 128 // rows
    for j in range(width // 128):
        tile = 0.0
        for i in range(j * per, (j + 1) * per):
            tile = tile + n.gs[i // nf, i % nf]
        n.gn[:, j * 128:(j + 1) * 128] = tile

    block = lat
    big = 1

    def token_norm(i, _):
        at = pl.ds(pl.multiple_of(i * block, block), block)
        n.xn[at] = norm(n.xn[at].astype(F32), gain[1][...])
        return 0

    n.an[...] = norm(n.lt[...].astype(F32), gain[0][...])
    lax.fori_loop(0, span // block, token_norm, 0)

    cross_dp[3].relay()
    for m in (0, 2, 1, 3):
        for k in range(1, nd):
            cross_dp[m].recv(k)
            start(cross_sib[k][m])
    up2_dp = dp_group(lambda k: su2.at[apos(k)], lambda k: n.up2.at[a, b])
    sq_dp = dp_group(lambda k: n.sqs.at[apos(k)], lambda k: n.sq.at[:, a, b])
    start(sq_dp)
    start(up2_dp)
    up1_z.relay()
    start(up1_sib[0])
    start(up1_sib[2])
    dn1_z.relay()
    start(dn1_sib[0])
    start(dn1_sib[2])
    for k in range(nd):
        for m in range(nz):
            recv(cross_sib[k][m])

    def rows_of(ref, k):
        return ref[k].reshape(lat, width)

    mid = nz // 2
    halves = (slice(0, mid), slice(mid, nz))

    def spread(buf, value):
        buf[0] = value.reshape(act_rows)
        g = Share(lambda h: (buf.at[0, halves[h]], buf.at[1, halves[h]]),
                  lambda h: (buf.at[0, halves[h]], buf.at[2, halves[h]]),
                  lambda h: (buf.at[1 + h, halves[h]], buf.at[3, halves[h]]))
        g.start()
        return g

    cot_dp = spread(n.gg, n.gb[...])
    def wcols(i, at):
        return n.wx[i, :, :, :, at].reshape(width, at.size)

    def full(ref):
        return ref[...].reshape(width, width)

    n.qq[...] = low(dot(n.an[...], n.wx[0].reshape(width, width), NN))
    wide = 256

    def token_proj(i, _):
        at = pl.ds(pl.multiple_of(i * wide, wide), wide)
        n.kk[:, at] = low(dot(n.xn[...], wcols(1, at), NN))
        n.vv[:, at] = low(dot(n.xn[...], wcols(2, at), NN))
        return 0

    lax.fori_loop(0, width // wide, token_proj, 0)
    valid = lax.broadcasted_iota(jnp.int32, (lat, span), 1) < n.frames[0] * FRAME_TOK

    def softmax(scores):
        expo = jnp.exp(scores - jnp.max(scores, axis=-1, keepdims=True))
        return low(expo / jnp.sum(expo, axis=-1, keepdims=True))

    def cross_head(h, _):
        at = pl.ds(pl.multiple_of(h * hd, hd), hd)
        scores = jnp.where(valid, dot(n.qq[:, at], n.kk[:, at], NT) * scale, NEG)
        probs = softmax(scores)
        n.pp[h] = probs
        n.cc[:, at] = low(dot(probs, n.vv[:, at], NN))
        return 0

    lax.fori_loop(0, HEADS, cross_head, 0, unroll=2)
    cot_dp.relay()
    z1 = n.lt[...].astype(F32) + dot(n.cc[...], n.wx[3].reshape(width, width), NN)
    n.z1[...] = z1

    def collect(make, gathered, sends, slots, previous):
        if previous is not None:
            sent(previous)
        back = dp_group(lambda k: sends.at[k - 1], lambda k: slots.at[k - 1])
        back.gathered = gathered
        n.own[...] = make(0)
        gathered.relay()

        def step(i, _):
            gathered.recv(i + 1)
            sends[i] = low(make(i + 1)).reshape(act_rows)
            back(i).start()
            return 0

        lax.fori_loop(0, nd - 1, step, 0)
        return back

    def gather_sum(back, slots):
        sent(back.gathered)
        total = n.own[...]
        for i in range(nd - 1):
            back(i).wait_recv()
            total = total + slots[i].reshape(lat, width).astype(F32)
        return total

    def feed_make(ag, u, d, up, dn):
        def make(k):
            value, slope = gelu_both(dot(rows_of(ag, k), full(up), NN))
            hidden = low(value)
            u[k] = hidden.reshape(act_rows)
            d[k] = low(slope).reshape(act_rows)
            return dot(hidden, full(dn), NN)

        return make

    ag1_dp = spread(n.ag1, norm(z1, gain[2][...]))
    recv(sq_dp)
    sq_z = Gather(lambda bi: n.sq.at[:, :, bi])
    so_z = Gather(lambda bi: n.so.at[bi])
    sq_sib = [sib_group(n.sq.at[:, :, bpos(m)], n.sq.at[:, :, bpos(m)]) for m in range(nz)]
    so_sib = [sib_group(n.so.at[bpos(m)], n.so.at[bpos(m)]) for m in range(nz)]
    recv(up2_dp)
    up2_z, up2_sib, dn2_z, dn2_sib = up_z(n.up2), up_sib(n.up2), dn_z(n.dn2), dn_sib(n.dn2)
    for m in (1, 3):
        up1_z.recv(m)
        start(up1_sib[m])
        dn1_z.recv(m)
        start(dn1_sib[m])
    sq_z.start()
    so_z.start()
    up2_z.start()
    dn2_z.start()
    start(sq_sib[0])
    start(so_sib[0])
    start(up2_sib[0])
    start(dn2_sib[0])
    for m in range(nz):
        recv(up1_sib[m])
        recv(dn1_sib[m])
    out1 = collect(feed_make(n.ag1, n.u1, n.d1, n.up1, n.dn1), ag1_dp, n.sa, n.ra, None)
    sq_z.relay()
    start(sq_sib[2])
    so_z.relay()
    start(so_sib[2])
    z2 = n.z1[...] + gather_sum(out1, n.ra)
    n.z2[...] = z2

    bg_dp = spread(n.bg, norm(z2, gain[3][...]))
    for m in (1, 3):
        sq_z.recv(m)
        start(sq_sib[m])
        so_z.recv(m)
        start(so_sib[m])
    for m in range(nz):
        recv(sq_sib[m])
        recv(so_sib[m])

    def self_make(k):
        normed = rows_of(n.bg, k)
        for i, ref in enumerate((n.q2, n.k2, n.v2)):
            ref[k] = low(dot(normed, n.sq[i].reshape(width, cols), NN))
        for h in range(local_heads):
            at = slice(h * hd, (h + 1) * hd)
            probs = softmax(dot(n.q2[k, :, at], n.k2[k, :, at], NT) * scale)
            n.p2[k, h] = probs
            n.c2[k, :, at] = low(dot(probs, n.v2[k, :, at], NN))
        return dot(n.c2[k], n.so[...].reshape(cols, width), NN)

    out_self = collect(self_make, bg_dp, n.sa, n.rb, out1)
    up2_z.relay()
    start(up2_sib[2])
    dn2_z.relay()
    start(dn2_sib[2])
    z3 = n.z2[...] + gather_sum(out_self, n.rb)
    n.z3[...] = z3

    ag2_dp = spread(n.ag2, norm(z3, gain[4][...]))
    for m in (1, 3):
        up2_z.recv(m)
        start(up2_sib[m])
        dn2_z.recv(m)
        start(dn2_sib[m])
    for k in range(1, nd):
        cot_dp.recv(k)
    for m in range(nz):
        recv(up2_sib[m])
        recv(dn2_sib[m])

    sc, rc = n.sc, n.rb

    def feed_back(g, d, up, dn):
        def make(k):
            grad = dot(rows_of(g, k), full(dn), NT)
            grad_low = low(rows_of(d, k).astype(F32) * grad)
            d[k] = grad_low.reshape(act_rows)
            return dot(grad_low, full(up), NT)

        return make

    feed2 = feed_make(n.ag2, n.u2, n.d2, n.up2, n.dn2)
    back2 = feed_back(n.gg, n.d2, n.up2, n.dn2)
    final_dp = dp_group(lambda k: sc.at[k - 1], lambda k: rc.at[k - 1])
    n.st[...] = n.z3[...] + feed2(0)

    def both(k):
        if not isinstance(k, int):
            sc[k - 1] = low(feed2(k)).reshape(act_rows)
        return back2(k)

    sent(up1_dp)
    sent(up2_dp)
    dm2 = collect(both, ag2_dp, n.sa, n.ra, out_self)

    def put_grad(value, ref, first):
        for i in range(value.shape[0] // rows):
            ai, bi = divmod(first + i, nf)
            zi, ci = divmod(bi, 2)
            ref[ci, zi, ai] = value[i * rows:(i + 1) * rows]

    def put_down(value, ref, first):
        for i in range(value.shape[0] // rows):
            bi, ai = divmod(first + i, nd)
            zi, ci = divmod(bi, 2)
            ref[ci, zi, ai] = value[i * rows:(i + 1) * rows]

    tall = 256

    def every_row(ref, at=slice(None)):
        value = ref[:, :, :, at]
        return value.reshape(value.shape[0] * value.shape[1] * value.shape[2], value.shape[3])

    def feed_grads(ag, u, d, g):
        for i in range(width // tall):
            at = slice(i * tall, (i + 1) * tall)
            put_grad(low(dot(every_row(ag, at), every_row(d), TN)), n.GU, i * tall // rows)
            put_down(low(dot(every_row(u, at), every_row(g), TN)), n.GD, i * tall // rows)

    def core_sum(grad, other):
        for i in range(nz):
            grad[c, i] = low(grad[c, i].astype(F32) + other[i].astype(F32))

    def sib_grads(grad, other):
        g = sib_group(grad.at[1 - c], other)
        start(g)
        return g

    def z_grads(grad, slots):
        g = Reduce(lambda zi: grad.at[c, zi], slots)
        g.start()
        return g

    feed_grads(n.ag2, n.u2, n.d2, n.gg)
    gu2_sib = sib_grads(n.GU, n.SU)
    gd2_sib = sib_grads(n.GD, n.SD)

    def set_gain(i, value):
        n.dg[i:i + 1] = value

    n.dg[...] = jnp.zeros_like(n.dg)
    back, gain_part = norm_back(n.z3[...], gain[4][...], gather_sum(dm2, n.ra))
    set_gain(4, gain_part)
    ga = rows_of(n.gg, 0).astype(F32) + back
    n.ga[...] = ga

    sent(cot_dp)

    gs_dp = spread(n.ggs, low(ga))
    recv(gu2_sib)
    core_sum(n.GU, n.SU)
    recv(gd2_sib)
    core_sum(n.GD, n.SD)
    gu2_z = z_grads(n.GU, n.ZU)
    gd2_z = z_grads(n.GD, n.ZD)

    def attend_back(q, k, v, probs, grad):
        grad_probs = dot(grad, v, NT)
        wide_probs = probs.astype(F32)
        inner = jnp.sum(wide_probs * grad_probs, axis=-1, keepdims=True)
        scores = low(wide_probs * (grad_probs - inner))
        return (low(dot(scores, k, NN) * scale), low(dot(scores, q, TN) * scale),
                low(dot(probs, grad, TN)))

    def self_back(k):
        grad = low(dot(rows_of(n.ggs, k), n.so[...].reshape(cols, width), NT))
        for h in range(local_heads):
            at = slice(h * hd, (h + 1) * hd)
            dq, dk, dv = attend_back(n.q2[k, :, at], n.k2[k, :, at], n.v2[k, :, at],
                                     n.p2[k, h], grad[:, at])
            n.q2[k, :, at] = dq
            n.k2[k, :, at] = dk
            n.v2[k, :, at] = dv
        total = 0.0
        for i, ref in enumerate((n.q2, n.k2, n.v2)):
            total = total + dot(ref[k], n.sq[i].reshape(width, cols), NT)
        return total

    db = collect(self_back, gs_dp, n.sa, n.rb, dm2)
    for i, ref in enumerate((n.q2, n.k2, n.v2)):
        value = low(dot(every_row(n.bg), ref[...].reshape(nd * lat, cols), TN))
        for j in range(width // rows):
            ai, bi = divmod(j, nf)
            zi, ci = divmod(bi, 2)
            n.GQ[ci, zi, ai, i] = value[j * rows:(j + 1) * rows]
    value = low(dot(n.c2[...].reshape(nd * lat, cols), every_row(n.ggs), TN))
    for bi in range(nf):
        zi, ci = divmod(bi, 2)
        n.GO[ci, zi] = value[bi * rows:(bi + 1) * rows]
    gq_sib = sib_grads(n.GQ, n.SQ)
    go_sib = sib_grads(n.GO, n.SO)
    back, gain_part = norm_back(n.z2[...], gain[3][...], gather_sum(db, n.rb))
    set_gain(3, gain_part)
    ga = n.ga[...] + back
    n.ga[...] = ga

    outs = []
    gf_dp = spread(n.gg, low(ga))
    recv(gq_sib)
    core_sum(n.GQ, n.SQ)
    recv(go_sib)
    core_sum(n.GO, n.SO)
    gq_z = z_grads(n.GQ, n.ZQ)
    go_z = z_grads(n.GO, n.ZO)
    gu2_z.combine()
    gd2_z.combine()
    dm1 = collect(feed_back(n.gg, n.d1, n.up1, n.dn1), gf_dp, n.sa, n.ra, db)

    def out_rows(value, staged, target):
        staged[...] = value.reshape(staged.shape)
        return load(staged, target)

    gq_z.combine()
    go_z.combine()
    total = gd2_z.total()
    outs.append(out_rows(total, n.z3, n.ogd))
    total = gu2_z.total()

    def column_grads(total, sends, slots):
        sends[...] = low(total)
        return dp_group(lambda k: sends.at[apos(k)], lambda k: slots.at[k - 1])

    su3, su4 = n.d2.at[0], n.d2.at[1]
    cu2_dp = column_grads(total, su3, n.CU2)
    for g in (gu2_sib, gd2_sib, gu2_z, gd2_z):
        sent(g)
    feed_grads(n.ag1, n.u1, n.d1, n.gg)
    gu1_sib = sib_grads(n.GU, n.SU)
    gd1_sib = sib_grads(n.GD, n.SD)
    back, gain_part = norm_back(n.z1[...], gain[2][...], gather_sum(dm1, n.ra))
    set_gain(2, gain_part)
    ga = n.ga[...] + back
    n.ga[...] = ga

    n.gb[...] = low(ga)
    mats = (n.up2, n.dn2, n.up1, n.dn1)
    others = (n.u1, n.d1, n.ag1, n.bg)

    def put_cross(value, ref, first):
        for i in range(value.shape[0] // rows):
            ai, bi = divmod(first + i, nf)
            zi, ci = divmod(bi, 2)
            ref[ai, ci * nz + zi] = value[i * rows:(i + 1) * rows]

    def cross_grad(left, right, which):
        for i in range(width // tall):
            put_cross(low(dot(left[:, i * tall:(i + 1) * tall], right, TN)), mats[which],
                      i * tall // rows)

    def half(ref, ci):
        return ref.at[:, pl.ds(ci * nz, nz)]

    for g in up1_sib + dn1_sib + up2_sib + dn2_sib + [up1_z, dn1_z, up2_z, dn2_z]:
        sent(g)
    start(final_dp)
    cross_grad(n.cc, n.gb[...], 3)
    core_dp = [group(1, lambda i, w=w: (half(mats[w], 1 - c), others[w], sib)) for w in range(4)]
    start(core_dp[3])
    n.dc[...] = low(dot(n.gb[...], n.wx[3].reshape(width, width), NT))
    recv(gu1_sib)
    core_sum(n.GU, n.SU)
    recv(gd1_sib)
    core_sum(n.GD, n.SD)
    zu1, zd1 = n.ag2, n.u2
    gu1_z = z_grads(n.GU, zu1)
    gd1_z = z_grads(n.GD, zd1)
    own_half = pl.ds(c * nz, nz)
    cross_xy, cross_back_z = {}, {}

    def over_dp(w):
        recv(core_dp[w])
        for ai in range(nd):
            mats[w][ai, own_half] = low(mats[w][ai, own_half].astype(F32) + others[w][ai].astype(F32))
        cross_xy[w] = dp_group(lambda k, w=w: mats[w].at[apos(k), own_half],
                               lambda k, w=w: n.xw.at[w, k - 1])
        start(cross_xy[w])

    over_dp(3)

    def cross_back(h, _):
        at = pl.ds(pl.multiple_of(h * hd, hd), hd)
        dq, dk, dv = attend_back(n.qq[:, at], n.kk[:, at], n.vv[:, at], n.pp[h], n.dc[:, at])
        n.qq[:, at] = dq
        n.kk[:, at] = dk
        n.vv[:, at] = dv
        return 0

    lax.fori_loop(0, HEADS, cross_back, 0, unroll=2)
    again = [load(n.inputs.at[0, pl.ds(i * block, block)], n.pp.at[i]) for i in range(span // block)]
    cross_grad(n.xn, n.vv[...], 2)
    start(core_dp[2])
    cross_grad(n.xn, n.kk[...], 1)
    start(core_dp[1])
    over_dp(2)
    cross_grad(n.an, n.qq[...], 0)
    start(core_dp[0])
    over_dp(1)
    gu1_z.combine()
    gd1_z.combine()
    over_dp(0)

    back, gain_part = norm_back(n.lt[...].astype(F32), gain[0][...],
                                dot(n.qq[...], n.wx[0].reshape(width, width), NT))
    set_gain(0, gain_part)
    n.gb[...] = low(n.ga[...] + back)
    outs.append(load(n.gb, n.glat.at[0]))
    arrived(again)

    def token_back(i, total):
        at = pl.ds(pl.multiple_of(i * big * block, big * block), big * block)
        grad = (dot(n.kk[at], n.wx[1].reshape(width, width), NT)
                + dot(n.vv[at], n.wx[2].reshape(width, width), NT))
        tokens = n.pp[pl.ds(i * big, big)].reshape(big * block, width).astype(F32)
        back, gain_part = norm_back(tokens, gain[1][...], grad)
        n.pp[pl.ds(i * big, big)] = low(back).reshape(big, block, width)
        return total + gain_part

    set_gain(1, lax.fori_loop(0, span // (big * block), token_back, jnp.zeros((1, width), F32)))
    for i in range(span // block):
        outs.append(load(n.pp.at[i], n.ginp.at[0, pl.ds(i * block, block)]))
    gain_hops = small_sum(n.dg)
    gain_hops[0][0]()

    recv(final_dp)
    total = n.st[...]
    for i in range(nd - 1):
        total = total + rc[i].reshape(lat, width).astype(F32)
    n.dc[...] = low(total)
    outs.append(load(n.dc, n.out.at[0]))

    gain_hops[0][1]()
    gain_hops[1][0]()
    start(cu2_dp)
    total = gd1_z.total()
    outs.append(out_rows(total, n.z1, n.ofd))
    cu1_dp = column_grads(gu1_z.total(), su4, n.CU1)
    start(cu1_dp)
    total = go_z.total()
    n.z2[0:rows] = total
    outs.append(load(n.z2.at[0:rows], n.oso))
    total = gq_z.total()
    sq_send = n.sqs
    sent(sq_dp)
    sq_send[...] = low(total)
    cq_dp = dp_group(lambda k: sq_send.at[apos(k)], lambda k: n.CQ.at[k - 1])
    start(cq_dp)

    order = (3, 2, 1, 0)
    for at, w in enumerate(order):
        recv(cross_xy[w])
        total = mats[w][a, own_half].astype(F32)
        for i in range(nd - 1):
            total = total + n.xw[w, i].astype(F32)
        mats[w][a, own_half] = low(total)
        cross_back_z[w] = Reduce(lambda zi, w=w: mats[w].at[a, c * nz + zi], n.ZU.at[w])
        cross_back_z[w].start()
        if at > 0:
            cross_back_z[order[at - 1]].combine()
    cross_back_z[order[-1]].combine()

    gain_hops[1][1]()
    gain_hops[2][0]()

    def put_columns(g, own, slots, staged, target):
        staged[0:rows] = own
        copies = [load(staged.at[0:rows], target.at[:, pl.ds(pl.multiple_of(a * width, width), width)])]
        for i in range(nd - 1):
            g(i).wait_recv()
            staged[(i + 1) * rows:(i + 2) * rows] = slots[i].astype(F32)
            copies.append(load(staged.at[(i + 1) * rows:(i + 2) * rows],
                               target.at[:, pl.ds(pl.multiple_of(apos(i + 1) * width, width), width)]))
        return copies

    outs += put_columns(cu2_dp, su3[a].astype(F32), n.CU2, n.st, n.ogu)
    outs += put_columns(cu1_dp, su4[a].astype(F32), n.CU1, n.own, n.ofu)
    recv(cq_dp)
    for i, target in enumerate((n.osq, n.osk, n.osv)):
        at = slice((i + 1) * rows, (i + 2) * rows)
        n.z2[at, pl.ds(pl.multiple_of(a * cols, cols), cols)] = sq_send[a, i].astype(F32)
        for k in range(1, nd):
            n.z2[at, pl.ds(pl.multiple_of(apos(k) * cols, cols), cols)] = n.CQ[k - 1, i].astype(F32)
        outs.append(load(n.z2.at[at], target))
    for w, target in ((3, n.oco), (2, n.ocv), (1, n.ock), (0, n.ocq)):
        total = cross_back_z[w].total()
        at = slice(w * rows, (w + 1) * rows)
        n.ga[at] = total
        outs.append(load(n.ga.at[at], target))
    gain_hops[2][1]()
    outs.append(load(n.dg, n.ggain))
    for g in ([cross_z, gains_z, gains_dp, final_dp, dm1, sq_z, so_z, gq_sib, go_sib, gq_z, go_z,
               cu1_dp, cu2_dp, cq_dp, gu1_sib, gd1_sib, gu1_z, gd1_z]
              + gains_sib + cross_dp + sq_sib + so_sib + core_dp + list(cross_xy.values()) + list(cross_back_z.values())
              + [g for line in cross_sib for g in line]):
        sent(g)
    arrived(outs)


def layer_norm(value, gain):
    center = value - jnp.mean(value, axis=-1, keepdims=True)
    spread = jnp.mean(center * center, axis=-1, keepdims=True)
    return center * lax.rsqrt(spread + EPS) * gain


def activate(value):
    return jax.nn.gelu(value, approximate=True)


def product(left, right):
    return jnp.dot(left, right, preferred_element_type=jnp.float32)


def weight_grad(left, right):
    return lax.dot_general(
        left, right, (((0,), (0,)), ((), ())), preferred_element_type=jnp.float32
    )


def back_product(grad, weight):
    return lax.dot_general(
        grad, weight, (((1,), (1,)), ((), ())), preferred_element_type=jnp.float32
    )


def plain_norm_back(value, gain, grad):
    _, pull = jax.vjp(layer_norm, value, gain)
    return pull(grad)


def activate_back(value, grad):
    _, pull = jax.vjp(activate, value)
    return pull(grad)[0]


def split_heads(value, groups):
    return value.reshape(groups, -1, HEADS, value.shape[-1] // HEADS)


def merge_heads(value):
    return value.reshape(-1, value.shape[2] * value.shape[3])


def masked_scores(query, key, valid):
    scale = query.shape[-1] ** (-0.5)
    scores = jnp.einsum("gqhd,gkhd->ghqk", query, key, preferred_element_type=jnp.float32) * scale
    return jnp.where(valid[:, None, None, :], scores, NEG)


def attend_forward(query, key, value, valid):
    scores = masked_scores(query, key, valid)
    top = jnp.max(scores, axis=-1, keepdims=True)
    expo = jnp.exp(scores - top)
    denom = jnp.sum(expo, axis=-1, keepdims=True)
    weights = (expo / denom).astype(jnp.bfloat16)
    mixed = jnp.einsum("ghqk,gkhd->gqhd", weights, value, preferred_element_type=jnp.float32)
    return (merge_heads(mixed).astype(jnp.bfloat16), top + jnp.log(denom))


def plain_attend_back(query, key, value, valid, logsum, grad_mixed):
    scale = query.shape[-1] ** (-0.5)
    probs = jnp.exp(masked_scores(query, key, valid) - logsum)
    grad_probs = jnp.einsum(
        "gqhd,gkhd->ghqk", grad_mixed, value, preferred_element_type=jnp.float32
    )
    inner = jnp.sum(probs * grad_probs, axis=-1, keepdims=True)
    grad_scores = (probs * (grad_probs - inner)).astype(jnp.bfloat16)
    weights = probs.astype(jnp.bfloat16)
    grad_query = (
        jnp.einsum("ghqk,gkhd->gqhd", grad_scores, key, preferred_element_type=jnp.float32) * scale
    )
    grad_key = (
        jnp.einsum("ghqk,gqhd->gkhd", grad_scores, query, preferred_element_type=jnp.float32)
        * scale
    )
    grad_value = jnp.einsum(
        "ghqk,gqhd->gkhd", weights, grad_mixed, preferred_element_type=jnp.float32
    )
    return (
        merge_heads(grad_query).astype(jnp.bfloat16),
        merge_heads(grad_key).astype(jnp.bfloat16),
        merge_heads(grad_value).astype(jnp.bfloat16),
    )


def feed_forward(resid, gain, w_up, w_down):
    normed = layer_norm(resid, gain.astype(jnp.float32)).astype(jnp.bfloat16)
    before = product(normed, w_up)
    hidden = activate(before).astype(jnp.bfloat16)
    return (resid + product(hidden, w_down), (normed, before, hidden))


def plain_feed_back(grad, resid, gain, saved, w_up, w_down):
    normed, before, hidden = saved
    grad_low = grad.astype(jnp.bfloat16)
    grad_down = weight_grad(hidden, grad_low)
    grad_before = activate_back(before, back_product(grad_low, w_down)).astype(jnp.bfloat16)
    grad_up = weight_grad(normed, grad_before)
    grad_resid, grad_gain = plain_norm_back(
        resid, gain.astype(jnp.float32), back_product(grad_before, w_up)
    )
    return (grad + grad_resid, grad_gain, grad_up, grad_down)


def project_back(grad, mixed, w_out, query, key, value, valid, logsum, groups):
    grad_low = grad.astype(jnp.bfloat16)
    grad_out = weight_grad(mixed, grad_low)
    grad_mixed = back_product(grad_low, w_out).astype(jnp.bfloat16)
    grad_query, grad_key, grad_value = plain_attend_back(
        split_heads(query, groups),
        split_heads(key, groups),
        split_heads(value, groups),
        valid,
        logsum,
        split_heads(grad_mixed, groups),
    )
    return (grad_out, grad_query, grad_key, grad_value)


def plain_layer(
    latents,
    inputs,
    frames,
    norm_latent,
    norm_input,
    cross_query,
    cross_key,
    cross_value,
    cross_output,
    norm_first,
    first_up,
    first_down,
    norm_self,
    self_query,
    self_key,
    self_value,
    self_output,
    norm_second,
    second_up,
    second_down,
    cotangent,
    mesh_size,
):
    groups, lat_rows, width = latents.shape
    span = inputs.shape[1]
    hidden_width = first_up.shape[1]
    low_type = jnp.bfloat16
    parts = mesh_size
    gains = (norm_latent, norm_input, norm_first, norm_self, norm_second)
    mats = (cross_query, cross_key, cross_value, cross_output, first_up, first_down,
            self_query, self_key, self_value, self_output, second_up, second_down)
    blocks = []
    for mat in mats:
        for start in range(0, mat.shape[1], width):
            blocks.append(mat[:, start:start + width])
    gain_row = jnp.concatenate([jnp.concatenate(gains), jnp.zeros((width - 5 * gains[0].shape[0],), jnp.float32)])
    gain_rows = jnp.concatenate([gain_row[None], jnp.zeros((15, width), jnp.float32)])
    packed = jnp.concatenate([gain_rows] + blocks).astype(low_type)
    whole = lax.all_gather(packed, ("dp", "fsdp"), axis=0, tiled=False)
    per = gains[0].shape[0]
    gathered_gains = [whole[:, 0, i * per:(i + 1) * per].reshape(width) for i in range(5)]
    gain_lat, gain_inp, gain_first, gain_self, gain_second = gathered_gains
    at = 16
    full = []
    for mat in mats:
        columns = []
        for start in range(0, mat.shape[1], width):
            columns.append(whole[:, at:at + mat.shape[0]].reshape(parts * mat.shape[0], width))
            at += mat.shape[0]
        full.append(columns[0] if len(columns) == 1 else jnp.concatenate(columns, axis=1))
    w_query, w_key, w_value, w_out, up_one, down_one, s_query, s_key, s_value, s_out, up_two, down_two = full
    positions = jnp.arange(span, dtype=jnp.int32)
    valid = positions[None, :] < (frames * FRAME_TOK)[:, None]
    every = jnp.ones((groups, lat_rows), dtype=bool)
    latent_rows = latents.reshape(groups * lat_rows, width).astype(jnp.float32)
    input_rows = inputs.reshape(groups * span, width).astype(jnp.float32)
    normed_lat = layer_norm(latent_rows, gain_lat.astype(jnp.float32)).astype(low_type)
    normed_inp = layer_norm(input_rows, gain_inp.astype(jnp.float32)).astype(low_type)
    query_one = product(normed_lat, w_query).astype(low_type)
    key_one = product(normed_inp, w_key).astype(low_type)
    value_one = product(normed_inp, w_value).astype(low_type)
    mixed_one, logsum_one = attend_forward(
        split_heads(query_one, groups),
        split_heads(key_one, groups),
        split_heads(value_one, groups),
        valid,
    )
    first_resid = latent_rows + product(mixed_one, w_out)
    second_resid, saved_one = feed_forward(first_resid, gain_first, up_one, down_one)
    normed_self = layer_norm(second_resid, gain_self.astype(jnp.float32)).astype(low_type)
    query_two = product(normed_self, s_query).astype(low_type)
    key_two = product(normed_self, s_key).astype(low_type)
    value_two = product(normed_self, s_value).astype(low_type)
    mixed_two, logsum_two = attend_forward(
        split_heads(query_two, groups),
        split_heads(key_two, groups),
        split_heads(value_two, groups),
        every,
    )
    third_resid = second_resid + product(mixed_two, s_out)
    final_resid, saved_two = feed_forward(third_resid, gain_second, up_two, down_two)
    result = final_resid.reshape(groups, lat_rows, width).astype(low_type)
    grad_final = cotangent.reshape(groups * lat_rows, width).astype(jnp.float32)
    grad_third, grad_gain_second, grad_up_two, grad_down_two = plain_feed_back(
        grad_final, third_resid, gain_second, saved_two, up_two, down_two
    )
    grad_s_out, grad_query_two, grad_key_two, grad_value_two = project_back(
        grad_third, mixed_two, s_out, query_two, key_two, value_two, every, logsum_two, groups
    )
    grad_s_query = weight_grad(normed_self, grad_query_two)
    grad_s_key = weight_grad(normed_self, grad_key_two)
    grad_s_value = weight_grad(normed_self, grad_value_two)
    grad_normed_self = (
        back_product(grad_query_two, s_query)
        + back_product(grad_key_two, s_key)
        + back_product(grad_value_two, s_value)
    )
    grad_from_self, grad_gain_self = plain_norm_back(
        second_resid, gain_self.astype(jnp.float32), grad_normed_self
    )
    grad_second = grad_third + grad_from_self
    grad_first, grad_gain_first, grad_up_one, grad_down_one = plain_feed_back(
        grad_second, first_resid, gain_first, saved_one, up_one, down_one
    )
    grad_w_out, grad_query_one, grad_key_one, grad_value_one = project_back(
        grad_first, mixed_one, w_out, query_one, key_one, value_one, valid, logsum_one, groups
    )
    grad_w_query = weight_grad(normed_lat, grad_query_one)
    grad_w_key = weight_grad(normed_inp, grad_key_one)
    grad_w_value = weight_grad(normed_inp, grad_value_one)
    grad_from_lat, grad_gain_lat = plain_norm_back(
        latent_rows, gain_lat.astype(jnp.float32), back_product(grad_query_one, w_query)
    )
    grad_latent_rows = grad_first + grad_from_lat
    grad_normed_inp = back_product(grad_key_one, w_key) + back_product(grad_value_one, w_value)
    grad_input_rows, grad_gain_inp = plain_norm_back(
        input_rows, gain_inp.astype(jnp.float32), grad_normed_inp
    )
    grad_mats = (grad_w_query, grad_w_key, grad_w_value, grad_w_out, grad_up_one, grad_down_one,
                 grad_s_query, grad_s_key, grad_s_value, grad_s_out, grad_up_two, grad_down_two)
    gain_grads = jnp.stack([grad_gain_lat, grad_gain_inp, grad_gain_first, grad_gain_self, grad_gain_second])
    gain_grads = jnp.moveaxis(gain_grads.reshape(5, parts, per), 1, 0).reshape(parts, 1, 5 * per)
    gain_grads = jnp.pad(gain_grads, ((0, 0), (0, 15), (0, width - 5 * per)))
    pieces = [gain_grads.astype(low_type)]
    for grad in grad_mats:
        for start in range(0, grad.shape[1], width):
            pieces.append(grad[:, start:start + width].reshape(parts, -1, width).astype(low_type))
    summed = lax.psum_scatter(jnp.concatenate(pieces, axis=1), ("dp", "fsdp"), scatter_dimension=0, tiled=False)
    summed = summed.astype(jnp.float32)
    gain_out = [summed[0, i * per:(i + 1) * per] for i in range(5)]
    at = 16
    out = []
    for mat in mats:
        columns = []
        for start in range(0, mat.shape[1], width):
            columns.append(summed[at:at + mat.shape[0]])
            at += mat.shape[0]
        out.append(columns[0] if len(columns) == 1 else jnp.concatenate(columns, axis=1))
    grad_latents = grad_latent_rows.reshape(groups, lat_rows, width).astype(low_type)
    grad_inputs = grad_input_rows.reshape(groups, span, width).astype(low_type)
    return (
        result, grad_latents, grad_inputs,
        gain_out[0], gain_out[1], out[0], out[1], out[2], out[3],
        gain_out[2], out[4], out[5],
        gain_out[3], out[6], out[7], out[8], out[9],
        gain_out[4], out[10], out[11],
    )


def hand_over(count, *refs):
    copies = [pltpu.make_async_copy(refs[i], refs[count + i], refs[-1].at[i]) for i in range(count)]
    for copy in copies:
        copy.start()
    for copy in copies:
        copy.wait()


def fits(mesh, lat, span, width, hidden):
    nd, nf = mesh.shape["dp"], mesh.shape["fsdp"]
    return (nd == 4 and nf == 8 and HEADS % nd == 0 and hidden == nd * width
            and width % (32 * nd * nf) == 0 and span == HEADS * lat and width // HEADS % 128 == 0)


def local(latents, inputs, frames, *rest, mesh):
    nd, nf = mesh.shape["dp"], mesh.shape["fsdp"]
    groups, lat, width = latents.shape
    span = inputs.shape[1]
    if groups != 1 or not fits(mesh, lat, span, width, rest[7].shape[1]):
        return plain_layer(latents, inputs, frames, *rest, mesh_size=mesh.size)
    (norm_latent, norm_input, cross_query, cross_key, cross_value, cross_output, norm_first, first_up,
     first_down, norm_self, self_query, self_key, self_value, self_output, norm_second, second_up,
     second_down, cotangent) = rest
    rows = cross_query.shape[0]
    index = lax.axis_index("dp") * nf + lax.axis_index("fsdp")
    gains = jnp.stack([norm_latent, norm_input, norm_first, norm_self, norm_second])
    lanes = lax.broadcasted_iota(jnp.int32, (8, 128), 1)
    gains = jnp.where(lanes // rows == lax.rem(index, 128 // rows),
                      jnp.tile(jnp.pad(gains, ((0, 3), (0, 0))), (1, 128 // rows)), 0.0)
    scratch = scratch_list(nd, nf, rows, width, lat, span, HEADS)
    anywhere = pl.BlockSpec(memory_space=pl.ANY)
    out_shape = (
        [jax.ShapeDtypeStruct(latents.shape, BF16)] * 2 + [jax.ShapeDtypeStruct(inputs.shape, BF16)]
        + [jax.ShapeDtypeStruct((8, width), F32)]
        + [jax.ShapeDtypeStruct(w.shape, F32) for w in (
            cross_query, cross_key, cross_value, cross_output, first_up, first_down,
            self_query, self_key, self_value, self_output, second_up, second_down)])
    flops = 2 * 3 * (lat * width * width * 22 + span * width * width * 2)
    results = pl.pallas_call(
        functools.partial(layer_kernel, INPUTS + OUTPUTS + tuple(scratch), nd, nf, rows),
        out_shape=out_shape,
        in_specs=[pl.BlockSpec(memory_space=pltpu.SMEM), pl.BlockSpec(memory_space=pltpu.VMEM)]
        + [anywhere] * (len(INPUTS) - 2),
        out_specs=[anywhere] * len(OUTPUTS),
        scratch_shapes=list(scratch.values()),
        compiler_params=pltpu.CompilerParams(
            collective_id=0, has_side_effects=True, vmem_limit_bytes=64 * 1024 * 1024),
        cost_estimate=pl.CostEstimate(flops=flops, bytes_accessed=30_000_000, transcendentals=4_000_000),
        name="layer",
    )(frames, gains, latents, inputs, cotangent, cross_query, cross_key, cross_value, cross_output,
      first_up, first_down, self_query, self_key, self_value, self_output, second_up, second_down)
    (result, grad_latents, grad_inputs, gain_grads, g_cq, g_ck, g_cv, g_co, g_fu, g_fd,
     g_sq, g_sk, g_sv, g_so, g_gu, g_gd) = pl.pallas_call(
        functools.partial(hand_over, len(OUTPUTS)),
        out_shape=out_shape,
        in_specs=[anywhere] * len(OUTPUTS),
        out_specs=[pl.BlockSpec(memory_space=pltpu.VMEM)] * len(OUTPUTS),
        scratch_shapes=[pltpu.SemaphoreType.DMA((len(OUTPUTS),))],
        compiler_params=pltpu.CompilerParams(vmem_limit_bytes=64 * 1024 * 1024),
        cost_estimate=pl.CostEstimate(flops=0, bytes_accessed=12_000_000, transcendentals=0),
        name="hand_over",
    )(*results)
    own = lax.dynamic_slice(gain_grads, (0, index * rows), (8, rows))
    return (result, grad_latents, grad_inputs, own[0], own[1], g_cq, g_ck, g_cv, g_co, own[2], g_fu, g_fd,
            own[3], g_sq, g_sk, g_sv, g_so, own[4], g_gu, g_gd)


def solution(mesh):
    in_specs = (
        P(("dp", "fsdp"), None, None),
        P(("dp", "fsdp"), None, None),
        P(("dp", "fsdp")),
        P(("dp", "fsdp")),
        P(("dp", "fsdp")),
        P(("dp", "fsdp"), None),
        P(("dp", "fsdp"), None),
        P(("dp", "fsdp"), None),
        P(("dp", "fsdp"), None),
        P(("dp", "fsdp")),
        P(("dp", "fsdp"), None),
        P(("dp", "fsdp"), None),
        P(("dp", "fsdp")),
        P(("dp", "fsdp"), None),
        P(("dp", "fsdp"), None),
        P(("dp", "fsdp"), None),
        P(("dp", "fsdp"), None),
        P(("dp", "fsdp")),
        P(("dp", "fsdp"), None),
        P(("dp", "fsdp"), None),
        P(("dp", "fsdp"), None, None),
    )
    out_specs = (
        P(("dp", "fsdp"), None, None),
        P(("dp", "fsdp"), None, None),
        P(("dp", "fsdp"), None, None),
        P(("dp", "fsdp")),
        P(("dp", "fsdp")),
        P(("dp", "fsdp"), None),
        P(("dp", "fsdp"), None),
        P(("dp", "fsdp"), None),
        P(("dp", "fsdp"), None),
        P(("dp", "fsdp")),
        P(("dp", "fsdp"), None),
        P(("dp", "fsdp"), None),
        P(("dp", "fsdp")),
        P(("dp", "fsdp"), None),
        P(("dp", "fsdp"), None),
        P(("dp", "fsdp"), None),
        P(("dp", "fsdp"), None),
        P(("dp", "fsdp")),
        P(("dp", "fsdp"), None),
        P(("dp", "fsdp"), None),
    )
    return jax.shard_map(functools.partial(local, mesh=mesh), mesh=mesh, in_specs=in_specs, out_specs=out_specs,
                         check_vma=False)
```

```python
import functools

import jax
import jax.numpy as jnp
from jax import lax
from jax.experimental import pallas as pl
from jax.experimental.pallas import tpu as pltpu
from jax.sharding import PartitionSpec as P

HEADS = 8
FRAME_TOK = 64
EPS = 1e-05
NEG = -1000000000.0
F32 = jnp.float32
BF16 = jnp.bfloat16
MESH = pl.DeviceIdType.MESH
NN = (((1,), (0,)), ((), ()))
NT = (((1,), (1,)), ((), ()))
TN = (((0,), (0,)), ((), ()))
GC0 = 0.7978845608
GC1 = 0.044715


def dot(left, right, dims):
    return lax.dot_general(left, right, dims, preferred_element_type=F32)


def low(value):
    return value.astype(BF16)


def flip(value, mask, size):
    out = 0
    bit = 1
    while bit < size:
        one = lax.rem(lax.div(value, jnp.int32(bit)), jnp.int32(2))
        if isinstance(mask, int):
            other = jnp.int32((mask // bit) % 2)
        else:
            other = lax.rem(lax.div(mask, jnp.int32(bit)), jnp.int32(2))
        out = out + lax.rem(one + other, jnp.int32(2)) * bit
        bit *= 2
    return out


def norm_parts(value):
    center = value - jnp.mean(value, axis=-1, keepdims=True)
    spread = jnp.mean(center * center, axis=-1, keepdims=True)
    inv = lax.rsqrt(spread + EPS)
    return center * inv, inv


def norm(value, gain):
    hat, _ = norm_parts(value)
    return low(hat * gain)


def norm_back(value, gain, grad):
    hat, inv = norm_parts(value)
    scaled = grad * gain
    out = inv * (
        scaled
        - jnp.mean(scaled, axis=-1, keepdims=True)
        - hat * jnp.mean(scaled * hat, axis=-1, keepdims=True)
    )
    return out, jnp.sum(grad * hat, axis=0, keepdims=True)


def gelu_both(value):
    square = value * value
    tan = jnp.tanh(GC0 * value * (1.0 + GC1 * square))
    half = 0.5 * (1.0 + tan)
    slope = half + 0.5 * value * (1.0 - tan * tan) * (GC0 * (1.0 + 3.0 * GC1 * square))
    return value * half, slope


INPUTS = ("frames", "gains", "latents", "inputs", "cot",
          "cq", "ck", "cv", "co", "fu", "fd", "sq_", "sk_", "sv_", "so_", "gu_", "gd_")
OUTPUTS = ("out", "glat", "ginp", "ggain",
           "ocq", "ock", "ocv", "oco", "ofu", "ofd", "osq", "osk", "osv", "oso", "ogu", "ogd")


def scratch_list(nd, nf, rows, width, lat, span, heads):
    nz = nf // 2
    hd = width // heads
    tp_cols = width // nd
    four = (nd, nf, rows, width)
    act = (nd, nz, rows, width)
    three = (nd - 1, nz, rows, width)
    vm = pltpu.VMEM
    return {
        "wx": vm((4,) + four, BF16),
        "up1": vm(four, BF16), "dn1": vm(four, BF16),
        "up2": vm(four, BF16), "dn2": vm(four, BF16),
        "sq": vm((3, nd, nf, rows, tp_cols), BF16), "so": vm((nf, rows, width), BF16),
        "sqs": vm((nd, 3, rows, tp_cols), BF16),
        "xn": vm((span, width), BF16), "kk": vm((span, width), BF16), "vv": vm((span, width), BF16),
        "pp": vm((heads, lat, span), BF16),
        "ag1": vm(act, BF16), "u1": vm(act, BF16), "d1": vm(act, BF16), "bg": vm(act, BF16),
        "ag2": vm(act, BF16), "u2": vm(act, BF16), "d2": vm(act, BF16),
        "gg": vm(act, BF16), "ggs": vm(act, BF16),
        "q2": vm((nd, lat, tp_cols), BF16), "k2": vm((nd, lat, tp_cols), BF16),
        "v2": vm((nd, lat, tp_cols), BF16), "c2": vm((nd, lat, tp_cols), BF16),
        "p2": vm((nd, heads // nd, lat, lat), BF16),
        "ra": vm(three, BF16), "rb": vm(three, BF16), "sa": vm(three, BF16), "sc": vm(three, BF16),
        "xw": vm((4,) + three, BF16),
        "GU": vm((2, nz, nd, rows, width), BF16), "GD": vm((2, nz, nd, rows, width), BF16),
        "GQ": vm((2, nz, nd, 3, rows, tp_cols), BF16), "GO": vm((2, nz, rows, width), BF16),
        "SU": vm((nz, nd, rows, width), BF16), "SD": vm((nz, nd, rows, width), BF16),
        "SQ": vm((nz, nd, 3, rows, tp_cols), BF16), "SO": vm((nz, rows, width), BF16),
        "ZU": vm((nz, nd, rows, width), BF16), "ZD": vm((nz, nd, rows, width), BF16),
        "ZQ": vm((nz, nd, 3, rows, tp_cols), BF16), "ZO": vm((nz, rows, width), BF16),
        "CU1": vm((nd - 1, rows, width), BF16), "CU2": vm((nd - 1, rows, width), BF16),
        "CQ": vm((nd - 1, 3, rows, tp_cols), BF16),
        "z1": vm((lat, width), F32), "z2": vm((lat, width), F32), "z3": vm((lat, width), F32),
        "ga": vm((lat, width), F32), "own": vm((lat, width), F32), "st": vm((lat, width), F32),
        "lt": vm((lat, width), BF16), "an": vm((lat, width), BF16), "qq": vm((lat, width), BF16),
        "cc": vm((lat, width), BF16), "gb": vm((lat, width), BF16), "dc": vm((lat, width), BF16),
        "gn": vm((8, width), F32), "dg": vm((8, width), F32),
        "gr": vm((1 + nz - 1 + nd - 1, 8, width), F32), "gs": vm((nd, nf, 8, 128), F32),
        "ss": pltpu.SemaphoreType.DMA((SEMS,)), "rs": pltpu.SemaphoreType.DMA((SEMS,)),
        "ls": pltpu.SemaphoreType.DMA((64,)),
    }


SEMS = 320


def layer_kernel(names, nd, nf, rows, *refs):
    r = dict(zip(names, refs))

    class Space:
        pass

    n = Space()
    for key, ref in r.items():
        setattr(n, key, ref)
    nz = nf // 2
    width = n.lt.shape[1]
    lat = n.lt.shape[0]
    span = n.xn.shape[0]
    hd = width // HEADS
    cols = width // nd
    local_heads = HEADS // nd
    scale = hd ** (-0.5)
    a = lax.axis_index("dp")
    b = lax.axis_index("fsdp")
    z = lax.div(b, jnp.int32(2))
    c = lax.rem(b, jnp.int32(2))
    sib = (a, z * 2 + 1 - c)

    def apos(k):
        return flip(a, k, nd)

    def zpos(m):
        return flip(z, m, nz)

    def bpos(m):
        return zpos(m) * 2 + c

    taken = [0, 0]

    def group(count, make):
        base = taken[0]
        taken[0] += count
        assert taken[0] <= SEMS

        def desc(i):
            src, dst, peer, *where = make(i)
            return pltpu.make_async_remote_copy(
                src_ref=src, dst_ref=dst, send_sem=n.ss.at[base + i],
                recv_sem=n.rs.at[base + (where[0] if where else i)],
                device_id=peer, device_id_type=MESH)

        desc.count = count
        return desc

    def start(g):
        for i in range(g.count):
            g(i).start()

    def recv(g):
        for i in range(g.count):
            g(i).wait_recv()

    def sent(g):
        if hasattr(g, "sent"):
            g.sent()
            return
        for i in range(g.count):
            g(i).wait_send()

    def load(src, dst):
        i = taken[1]
        taken[1] += 1
        copy = pltpu.make_async_copy(src, dst, n.ls.at[i])
        copy.start()
        return copy

    def dp_group(src, dst):
        return group(nd - 1, lambda i: (src(i + 1), dst(i + 1), (apos(i + 1), b)))

    inner = lax.rem(z, jnp.int32(3)) != 0
    outer = jnp.logical_not(inner)

    class Gather:
        def __init__(self, block):
            self.g = group(4, lambda i: (
                (block(b), block(b), (a, bpos(i + 1))) if i < 3
                else (block(bpos(2)), block(bpos(2)), (a, bpos(1)), 2)))

        def start(self):
            self.g(1).start()
            self.g(0).start()
            pl.when(inner)(lambda: self.g(2).start())

        def relay(self):
            @pl.when(inner)
            def _():
                self.g(1).wait_recv()
                self.g(3).start()

        def recv(self, m):
            if m == 2:
                pl.when(outer)(lambda: self.g(1).wait_recv())
            else:
                self.g(m - 1).wait_recv()

        def sent(self):
            self.g(0).wait_send()
            self.g(1).wait_send()

            @pl.when(inner)
            def _():
                self.g(2).wait_send()
                self.g(3).wait_send()

    class Reduce:
        def __init__(self, part, slots):
            self.part, self.slots = part, slots
            self.g = group(4, lambda i: (
                (part(zpos(i + 1)), slots.at[i], (a, bpos(i + 1))) if i < 3
                else (part(zpos(3)), slots.at[3], (a, bpos(1)))))

        def start(self):
            @pl.when(outer)
            def _():
                self.g(3).start()
                self.g(1).start()

            pl.when(inner)(lambda: self.g(2).start())
            self.g(0).start()

        def combine(self):
            @pl.when(inner)
            def _():
                self.g(3).wait_recv()
                ref = self.part(zpos(2))
                ref[...] = low(ref[...].astype(F32) + self.slots[3].astype(F32))
                self.g(1).start()

        def total(self):
            self.g(0).wait_recv()
            self.g(1).wait_recv()
            ref = self.part(z)

            @pl.when(inner)
            def _():
                self.g(2).wait_recv()
                ref[...] = low(ref[...].astype(F32) + self.slots[2].astype(F32))

            return ref[...].astype(F32) + self.slots[0].astype(F32) + self.slots[1].astype(F32)

        def sent(self):
            self.g(0).wait_send()
            self.g(1).wait_send()
            pl.when(outer)(lambda: self.g(3).wait_send())
            pl.when(inner)(lambda: self.g(2).wait_send())

    class Share:
        def __init__(self, one, two, three):
            def make(i):
                if i in (0, 2):
                    return one(i // 2) + ((apos(1), b),)
                if i in (1, 3):
                    return two(1 - i // 2) + ((apos(2), b),)
                return three(i - 4) + ((apos(2 - (i - 4)), b),)

            self.g = group(6, make)

        def start(self):
            for i in range(4):
                self.g(i).start()

        def relay(self):
            for i in range(2):
                self.g(i).wait_recv()
                self.g(4 + i).start()

        def recv(self, k):
            if isinstance(k, int):
                for i in ((2,), (3,), (4, 5))[k - 1]:
                    self.g(i).wait_recv()
                return
            for j in (1, 2, 3):
                pl.when(k == j)(lambda j=j: self.recv(j))

        def sent(self):
            for i in range(6):
                self.g(i).wait_send()

    def sib_group(src, dst):
        return group(1, lambda i: (src, dst, sib))

    class Merge:
        def __init__(self, part, slots):
            self.part, self.slots = part, slots

            def make(i):
                k, h, slot, peer = ((3, 0, 2, 2), (3, 1, 2, 1), (1, 1, 0, 1), (2, 0, 1, 2),
                                    (1, 0, 0, 1), (2, 1, 1, 2))[i]
                return part(k, h), slots.at[slot, halves[h]], (apos(peer), b)

            self.g = group(6, make)

        def push(self, k):
            if isinstance(k, int):
                for i in ((2,), (3,), (0, 1))[k - 1]:
                    self.g(i).start()
                return
            for j in (1, 2, 3):
                pl.when(k == j)(lambda j=j: self.push(j))

        def combine(self):
            for i, k, h in ((0, 1, 0), (1, 2, 1)):
                self.g(i).wait_recv()
                ref = self.part(k, h)
                ref[...] = low(ref[...].astype(F32) + self.slots[2, halves[h]].astype(F32))
                self.g(4 + i).start()

        def total(self, own):
            for i in (2, 3, 4, 5):
                self.g(i).wait_recv()
            return own + self.slots[0].reshape(own.shape).astype(F32) + self.slots[1].reshape(own.shape).astype(F32)

        def sent(self):
            for i in range(6):
                self.g(i).wait_send()

    mid = nz // 2
    halves = (slice(0, mid), slice(mid, nz))

    def stage(refs, dst):
        return [load(ref, dst.at[pl.ds(i * rows, rows)]) for i, ref in enumerate(refs)]

    blocks = [pl.ds(j * width, width) for j in range(nd)]
    in_cross = stage((n.cq, n.ck, n.cv, n.co), n.z1)
    in_up1 = stage([n.fu.at[:, s] for s in blocks], n.z2)
    in_dn1 = [load(n.fd, n.z3)]
    in_lat = [load(n.latents.at[0], n.lt)]
    in_x = [load(n.inputs.at[0], n.xn)]
    in_self = stage((n.sq_, n.sk_, n.sv_, n.so_), n.ga)
    in_up2 = stage([n.gu_.at[:, s] for s in blocks], n.own)
    in_dn2 = [load(n.gd_, n.st)]
    in_cot = [load(n.cot.at[0], n.gb)]

    def arrived(copies):
        for copy in copies:
            copy.wait()

    peers = [(apos(k), b) for k in range(1, nd)] + [(a, bpos(m)) for m in range(1, nz)] + [sib]
    barrier = pltpu.get_barrier_semaphore()
    for peer in peers:
        pl.semaphore_signal(barrier, inc=1, device_id=peer, device_id_type=MESH)

    def small_sum(buf):
        slots = n.gr
        hops = (group(1, lambda i: (buf, slots.at[0], sib)),
                group(nd - 1, lambda i: (buf, slots.at[1 + i], (apos(i + 1), b))),
                group(nz - 1, lambda i: (buf, slots.at[nd + i], (a, bpos(i + 1)))))
        phases = []
        first = 0
        for g in hops:
            def finish(g=g, first=first):
                recv(g)
                sent(g)
                total = buf[...]
                for i in range(g.count):
                    total = total + slots[first + i]
                buf[...] = total

            phases.append((functools.partial(start, g), finish))
            first += g.count
        return phases

    pl.semaphore_wait(barrier, len(peers))
    n.gs[a, b] = low(n.gains[...]).astype(F32)
    gains_z = Gather(lambda bi: n.gs.at[a, bi])
    gains_sib = [sib_group(n.gs.at[a, bpos(m)], n.gs.at[a, bpos(m)]) for m in range(nz)]
    gains_dp = dp_group(lambda k: n.gs.at[a], lambda k: n.gs.at[a])
    gains_z.start()
    start(gains_sib[0])
    arrived(in_cross)
    for i in range(4):
        n.wx[i, a, b] = low(n.z1[i * rows:(i + 1) * rows])

    def wx_at(ai, bi):
        return n.wx.at[:, ai, bi]

    cross_z = Gather(lambda bi: n.wx.at[:, a, bi])
    cross_dp = []
    for m in range(nz):
        def direct(h, m=m):
            at = n.wx.at[2 * h:2 * h + 2, a, bpos(m)]
            return at, at

        def relayed(h, m=m):
            at = n.wx.at[2 * h:2 * h + 2, apos(1 + h), bpos(m)]
            return at, at

        cross_dp.append(Share(direct, direct, relayed))
    cross_sib = [[sib_group(wx_at(apos(k), bpos(m)), wx_at(apos(k), bpos(m))) for m in range(nz)]
                 for k in range(nd)]
    cross_z.start()
    cross_dp[0].start()
    start(cross_sib[0][0])

    su1, su2 = n.xw.at[3, 0], n.xw.at[3, 1]

    def put_up(staged, sends, up):
        for j in range(nd):
            sends[j] = low(staged[j * rows:(j + 1) * rows])
        up[a, b] = sends[a]

    def put_dn(staged, dn):
        dn[lax.div(b * nd, jnp.int32(nf)), pl.ds(lax.rem(b * nd, jnp.int32(nf)), nd)] = (
            low(staged[...]).reshape(nd, rows, width))

    def dn_at(dn, bi):
        return dn.at[lax.div(bi * nd, jnp.int32(nf)), pl.ds(lax.rem(bi * nd, jnp.int32(nf)), nd)]

    arrived(in_up1)
    put_up(n.z2, su1, n.up1)
    up1_dp = dp_group(lambda k: su1.at[apos(k)], lambda k: n.up1.at[a, b])
    start(up1_dp)
    arrived(in_dn1)
    put_dn(n.z3, n.dn1)
    arrived(in_self)
    for i in range(3):
        for j in range(nd):
            n.sqs[j, i] = low(n.ga[i * rows:(i + 1) * rows, j * cols:(j + 1) * cols])
    for i in range(3):
        n.sq[i, a, b] = n.sqs[a, i]
    n.so[b] = low(n.ga[3 * rows:4 * rows])
    arrived(in_up2)
    put_up(n.own, su2, n.up2)
    arrived(in_dn2)
    put_dn(n.st, n.dn2)
    arrived(in_cot)
    act_rows = (nz, rows, width)

    def up_z(up):
        return Gather(lambda bi: up.at[:, bi])

    def up_sib(up):
        return [sib_group(up.at[:, bpos(m)], up.at[:, bpos(m)]) for m in range(nz)]

    def dn_z(dn):
        return Gather(lambda bi: dn_at(dn, bi))

    def dn_sib(dn):
        return [sib_group(dn_at(dn, bpos(m)), dn_at(dn, bpos(m))) for m in range(nz)]

    gain = [n.gn.at[i:i + 1] for i in range(5)]

    arrived(in_lat)
    arrived(in_x)
    gains_z.relay()
    for m in (1, 2, 3):
        gains_z.recv(m)
        start(gains_sib[m])
    for g in gains_sib:
        recv(g)
    start(gains_dp)
    cross_z.relay()
    for m in (1, 2, 3):
        cross_z.recv(m)
        cross_dp[m].start()
        start(cross_sib[0][m])
        if m == 1:
            cross_dp[0].relay()
    up1_z, up1_sib, dn1_z, dn1_sib = up_z(n.up1), up_sib(n.up1), dn_z(n.dn1), dn_sib(n.dn1)
    recv(up1_dp)
    up1_z.start()
    dn1_z.start()
    cross_dp[1].relay()
    cross_dp[2].relay()
    recv(gains_dp)
    per = 128 // rows
    for j in range(width // 128):
        tile = 0.0
        for i in range(j * per, (j + 1) * per):
            tile = tile + n.gs[i // nf, i % nf]
        n.gn[:, j * 128:(j + 1) * 128] = tile

    block = lat
    big = 1

    def token_norm(i, _):
        at = pl.ds(pl.multiple_of(i * block, block), block)
        n.xn[at] = norm(n.xn[at].astype(F32), gain[1][...])
        return 0

    n.an[...] = norm(n.lt[...].astype(F32), gain[0][...])
    lax.fori_loop(0, span // block, token_norm, 0)

    cross_dp[3].relay()
    for m in range(nz):
        for k in range(1, nd):
            cross_dp[m].recv(k)
            start(cross_sib[k][m])
        if m == 1:
            up1_z.relay()
    up2_dp = dp_group(lambda k: su2.at[apos(k)], lambda k: n.up2.at[a, b])
    sq_dp = dp_group(lambda k: n.sqs.at[apos(k)], lambda k: n.sq.at[:, a, b])
    start(sq_dp)
    start(up2_dp)
    for k in range(nd):
        for m in range(nz):
            recv(cross_sib[k][m])

    def rows_of(ref, k):
        return ref[k].reshape(lat, width)

    def spread(buf, value):
        buf[0] = value.reshape(act_rows)
        g = Share(lambda h: (buf.at[0, halves[h]], buf.at[1, halves[h]]),
                  lambda h: (buf.at[0, halves[h]], buf.at[2, halves[h]]),
                  lambda h: (buf.at[1 + h, halves[h]], buf.at[3, halves[h]]))
        g.start()
        return g

    cot_dp = spread(n.gg, n.gb[...])
    def wcols(i, at):
        return n.wx[i, :, :, :, at].reshape(width, at.size)

    def full(ref):
        return ref[...].reshape(width, width)

    n.qq[...] = low(dot(n.an[...], n.wx[0].reshape(width, width), NN))
    wide = 256

    def token_proj(i, _):
        at = pl.ds(pl.multiple_of(i * wide, wide), wide)
        n.kk[:, at] = low(dot(n.xn[...], wcols(1, at), NN))
        n.vv[:, at] = low(dot(n.xn[...], wcols(2, at), NN))
        return 0

    lax.fori_loop(0, width // wide, token_proj, 0)
    dn1_z.relay()
    recv(sq_dp)
    sq_z = Gather(lambda bi: n.sq.at[:, :, bi])
    so_z = Gather(lambda bi: n.so.at[bi])
    sq_sib = [sib_group(n.sq.at[:, :, bpos(m)], n.sq.at[:, :, bpos(m)]) for m in range(nz)]
    so_sib = [sib_group(n.so.at[bpos(m)], n.so.at[bpos(m)]) for m in range(nz)]
    sq_z.start()
    so_z.start()
    cot_dp.relay()
    valid = lax.broadcasted_iota(jnp.int32, (lat, span), 1) < n.frames[0] * FRAME_TOK

    def softmax(scores):
        expo = jnp.exp(scores - jnp.max(scores, axis=-1, keepdims=True))
        return low(expo / jnp.sum(expo, axis=-1, keepdims=True))

    def cross_head(h, _):
        at = pl.ds(pl.multiple_of(h * hd, hd), hd)
        scores = jnp.where(valid, dot(n.qq[:, at], n.kk[:, at], NT) * scale, NEG)
        probs = softmax(scores)
        n.pp[h] = probs
        n.cc[:, at] = low(dot(probs, n.vv[:, at], NN))
        return 0

    lax.fori_loop(0, HEADS, cross_head, 0, unroll=2)
    z1 = n.lt[...].astype(F32) + dot(n.cc[...], n.wx[3].reshape(width, width), NN)
    n.z1[...] = z1

    def collect(make, gathered, sends, slots, previous):
        if previous is not None:
            sent(previous)
        back = Merge(lambda k, h: sends.at[k - 1, halves[h]], slots)
        back.gathered = gathered
        n.own[...] = make(0)
        gathered.relay()

        def step(i, _):
            gathered.recv(i + 1)
            sends[i] = low(make(i + 1)).reshape(act_rows)
            back.push(i + 1)
            return 0

        lax.fori_loop(0, nd - 1, step, 0)
        return back

    def gather_sum(back, slots):
        if back.gathered is not None:
            sent(back.gathered)
        return back.total(n.own[...])

    def feed_hidden(ag, u, d, up):
        def make(k):
            value, slope = gelu_both(dot(rows_of(ag, k), full(up), NN))
            hidden = low(value)
            u[k] = hidden.reshape(act_rows)
            d[k] = low(slope).reshape(act_rows)
            return hidden

        return make

    def feed_make(ag, u, d, up, dn):
        hide = feed_hidden(ag, u, d, up)

        def make(k):
            return dot(hide(k), full(dn), NN)

        return make

    ag1_dp = spread(n.ag1, norm(z1, gain[2][...]))
    recv(up2_dp)
    up2_z, up2_sib, dn2_z, dn2_sib = up_z(n.up2), up_sib(n.up2), dn_z(n.dn2), dn_sib(n.dn2)
    for m in range(nz):
        for g, line in ((up1_z, up1_sib), (dn1_z, dn1_sib)):
            if m > 0:
                g.recv(m)
            start(line[m])
    sq_z.relay()
    so_z.relay()
    up2_z.start()
    dn2_z.start()
    for m in range(nz):
        recv(up1_sib[m])
        recv(dn1_sib[m])
    out1 = collect(feed_make(n.ag1, n.u1, n.d1, n.up1, n.dn1), ag1_dp, n.sa, n.ra, None)
    out1.combine()
    z2 = n.z1[...] + gather_sum(out1, n.ra)
    n.z2[...] = z2

    bg_dp = spread(n.bg, norm(z2, gain[3][...]))
    for m in range(nz):
        for g, line in ((sq_z, sq_sib), (so_z, so_sib)):
            if m > 0:
                g.recv(m)
            start(line[m])
    up2_z.relay()
    for m in range(nz):
        recv(sq_sib[m])
        recv(so_sib[m])

    def self_make(k):
        normed = rows_of(n.bg, k)
        for i, ref in enumerate((n.q2, n.k2, n.v2)):
            ref[k] = low(dot(normed, n.sq[i].reshape(width, cols), NN))
        for h in range(local_heads):
            at = slice(h * hd, (h + 1) * hd)
            probs = softmax(dot(n.q2[k, :, at], n.k2[k, :, at], NT) * scale)
            n.p2[k, h] = probs
            n.c2[k, :, at] = low(dot(probs, n.v2[k, :, at], NN))
        return dot(n.c2[k], n.so[...].reshape(cols, width), NN)

    out_self = collect(self_make, bg_dp, n.sa, n.rb, out1)
    out_self.combine()
    dn2_z.relay()
    z3 = n.z2[...] + gather_sum(out_self, n.rb)
    n.z3[...] = z3

    ag2_dp = spread(n.ag2, norm(z3, gain[4][...]))
    for m in range(nz):
        if m > 0:
            up2_z.recv(m)
        start(up2_sib[m])
    for m in range(nz):
        recv(up2_sib[m])

    sc, rc = n.sc, n.rb

    def feed_back(g, d, up, dn):
        def make(k):
            grad = dot(rows_of(g, k), full(dn), NT)
            grad_low = low(rows_of(d, k).astype(F32) * grad)
            d[k] = grad_low.reshape(act_rows)
            return dot(grad_low, full(up), NT)

        return make

    hide2 = feed_hidden(n.ag2, n.u2, n.d2, n.up2)
    back2 = feed_back(n.gg, n.d2, n.up2, n.dn2)
    final_dp = Merge(lambda k, h: sc.at[k - 1, halves[h]], rc)
    sent(up1_dp)
    sent(up2_dp)
    hide2(0)
    ag2_dp.relay()

    def hide_step(i, _):
        ag2_dp.recv(i + 1)
        hide2(i + 1)
        return 0

    lax.fori_loop(0, nd - 1, hide_step, 0)

    def put_grad(value, ref, first):
        for i in range(value.shape[0] // rows):
            ai, bi = divmod(first + i, nf)
            zi, ci = divmod(bi, 2)
            ref[ci, zi, ai] = value[i * rows:(i + 1) * rows]

    def put_down(value, ref, first):
        for i in range(value.shape[0] // rows):
            bi, ai = divmod(first + i, nd)
            zi, ci = divmod(bi, 2)
            ref[ci, zi, ai] = value[i * rows:(i + 1) * rows]

    tall = 256

    def every_row(ref, at=slice(None)):
        value = ref[:, :, :, at]
        return value.reshape(value.shape[0] * value.shape[1] * value.shape[2], value.shape[3])

    def up_grad(ag, d):
        for i in range(width // tall):
            at = slice(i * tall, (i + 1) * tall)
            put_grad(low(dot(every_row(ag, at), every_row(d), TN)), n.GU, i * tall // rows)

    def down_grad(u, g):
        for i in range(width // tall):
            at = slice(i * tall, (i + 1) * tall)
            put_down(low(dot(every_row(u, at), every_row(g), TN)), n.GD, i * tall // rows)

    def core_sum(grad, other):
        for i in range(nz):
            grad[c, i] = low(grad[c, i].astype(F32) + other[i].astype(F32))

    def sib_grads(grad, other):
        g = sib_group(grad.at[1 - c], other)
        start(g)
        return g

    def z_grads(grad, slots):
        g = Reduce(lambda zi: grad.at[c, zi], slots)
        g.start()
        return g

    for k in range(1, nd):
        cot_dp.recv(k)
    down_grad(n.u2, n.gg)
    gd2_sib = sib_grads(n.GD, n.SD)
    for m in range(nz):
        if m > 0:
            dn2_z.recv(m)
        start(dn2_sib[m])
    for m in range(nz):
        recv(dn2_sib[m])
    sent(out_self)
    dm2 = Merge(lambda k, h: n.sa.at[k - 1, halves[h]], n.ra)
    dm2.gathered = None
    n.own[...] = back2(0)
    recv(gd2_sib)
    core_sum(n.GD, n.SD)
    gd2_z = z_grads(n.GD, n.ZD)

    def back_step(i, _):
        k = lax.rem(i + 2, 3) + 1
        n.sa[k - 1] = low(back2(k)).reshape(act_rows)
        dm2.push(k)
        return 0

    lax.fori_loop(0, nd - 1, back_step, 0)
    sent(ag2_dp)
    up_grad(n.ag2, n.d2)
    gu2_sib = sib_grads(n.GU, n.SU)
    dm2.combine()
    n.st[...] = n.z3[...] + dot(rows_of(n.u2, 0), full(n.dn2), NN)

    def out_step(i, _):
        sc[i] = low(dot(rows_of(n.u2, i + 1), full(n.dn2), NN)).reshape(act_rows)
        return 0

    lax.fori_loop(0, nd - 1, out_step, 0)
    recv(gu2_sib)
    core_sum(n.GU, n.SU)
    gu2_z = z_grads(n.GU, n.ZU)

    def set_gain(i, value):
        n.dg[i:i + 1] = value

    n.dg[...] = jnp.zeros_like(n.dg)
    back, gain_part = norm_back(n.z3[...], gain[4][...], gather_sum(dm2, n.ra))
    set_gain(4, gain_part)
    ga = rows_of(n.gg, 0).astype(F32) + back
    n.ga[...] = ga

    sent(cot_dp)

    gs_dp = spread(n.ggs, low(ga))
    gd2_z.combine()

    def attend_back(q, k, v, probs, grad):
        grad_probs = dot(grad, v, NT)
        wide_probs = probs.astype(F32)
        inner = jnp.sum(wide_probs * grad_probs, axis=-1, keepdims=True)
        scores = low(wide_probs * (grad_probs - inner))
        return (low(dot(scores, k, NN) * scale), low(dot(scores, q, TN) * scale),
                low(dot(probs, grad, TN)))

    def self_back(k):
        grad = low(dot(rows_of(n.ggs, k), n.so[...].reshape(cols, width), NT))
        for h in range(local_heads):
            at = slice(h * hd, (h + 1) * hd)
            dq, dk, dv = attend_back(n.q2[k, :, at], n.k2[k, :, at], n.v2[k, :, at],
                                     n.p2[k, h], grad[:, at])
            n.q2[k, :, at] = dq
            n.k2[k, :, at] = dk
            n.v2[k, :, at] = dv
        total = 0.0
        for i, ref in enumerate((n.q2, n.k2, n.v2)):
            total = total + dot(ref[k], n.sq[i].reshape(width, cols), NT)
        return total

    db = collect(self_back, gs_dp, n.sa, n.rb, dm2)
    for i, ref in enumerate((n.q2, n.k2, n.v2)):
        value = low(dot(every_row(n.bg), ref[...].reshape(nd * lat, cols), TN))
        for j in range(width // rows):
            ai, bi = divmod(j, nf)
            zi, ci = divmod(bi, 2)
            n.GQ[ci, zi, ai, i] = value[j * rows:(j + 1) * rows]
    value = low(dot(n.c2[...].reshape(nd * lat, cols), every_row(n.ggs), TN))
    for bi in range(nf):
        zi, ci = divmod(bi, 2)
        n.GO[ci, zi] = value[bi * rows:(bi + 1) * rows]
    gq_sib = sib_grads(n.GQ, n.SQ)
    go_sib = sib_grads(n.GO, n.SO)
    db.combine()
    recv(gq_sib)
    core_sum(n.GQ, n.SQ)
    gq_z = z_grads(n.GQ, n.ZQ)
    recv(go_sib)
    core_sum(n.GO, n.SO)
    go_z = z_grads(n.GO, n.ZO)
    gu2_z.combine()
    back, gain_part = norm_back(n.z2[...], gain[3][...], gather_sum(db, n.rb))
    set_gain(3, gain_part)
    ga = n.ga[...] + back
    n.ga[...] = ga

    outs = []
    gf_dp = spread(n.gg, low(ga))
    dm1 = collect(feed_back(n.gg, n.d1, n.up1, n.dn1), gf_dp, n.sa, n.ra, db)

    def out_rows(value, staged, target):
        staged[...] = value.reshape(staged.shape)
        return load(staged, target)

    gq_z.combine()
    go_z.combine()
    total = gd2_z.total()
    outs.append(out_rows(total, n.z3, n.ogd))
    total = gu2_z.total()

    def column_grads(total, sends, slots):
        sends[...] = low(total)
        return dp_group(lambda k: sends.at[apos(k)], lambda k: slots.at[k - 1])

    su3, su4 = n.d2.at[0], n.d2.at[1]
    cu2_dp = column_grads(total, su3, n.CU2)
    for g in (gu2_sib, gd2_sib, gu2_z, gd2_z):
        sent(g)
    down_grad(n.u1, n.gg)
    gd1_sib = sib_grads(n.GD, n.SD)
    dm1.combine()
    zu1, zd1 = n.ag2, n.u2
    recv(gd1_sib)
    core_sum(n.GD, n.SD)
    gd1_z = z_grads(n.GD, zd1)
    up_grad(n.ag1, n.d1)
    gu1_sib = sib_grads(n.GU, n.SU)
    recv(gu1_sib)
    core_sum(n.GU, n.SU)
    gu1_z = z_grads(n.GU, zu1)
    back, gain_part = norm_back(n.z1[...], gain[2][...], gather_sum(dm1, n.ra))
    set_gain(2, gain_part)
    ga = n.ga[...] + back
    n.ga[...] = ga

    n.gb[...] = low(ga)
    mats = (n.up2, n.dn2, n.up1, n.dn1)
    others = (n.u1, n.d1, n.ag1, n.bg)

    def put_cross(value, ref, first):
        for i in range(value.shape[0] // rows):
            ai, bi = divmod(first + i, nf)
            zi, ci = divmod(bi, 2)
            ref[ai, ci * nz + zi] = value[i * rows:(i + 1) * rows]

    def cross_grad(left, right, which):
        for i in range(width // tall):
            put_cross(low(dot(left[:, i * tall:(i + 1) * tall], right, TN)), mats[which],
                      i * tall // rows)

    def half(ref, ci):
        return ref.at[:, pl.ds(ci * nz, nz)]

    for g in up1_sib + dn1_sib + up2_sib + dn2_sib + [up1_z, dn1_z, up2_z, dn2_z]:
        sent(g)
    start(cu2_dp)
    cross_grad(n.cc, n.gb[...], 3)
    core_dp = [group(1, lambda i, w=w: (half(mats[w], 1 - c), others[w], sib)) for w in range(4)]
    start(core_dp[3])
    n.dc[...] = low(dot(n.gb[...], n.wx[3].reshape(width, width), NT))
    own_half = pl.ds(c * nz, nz)
    cross_xy, cross_back_z = {}, {}

    def over_dp(w):
        recv(core_dp[w])
        for ai in range(nd):
            mats[w][ai, own_half] = low(mats[w][ai, own_half].astype(F32) + others[w][ai].astype(F32))
        cross_xy[w] = Merge(lambda k, h, w=w: mats[w].at[apos(k), pl.ds(c * nz + h * mid, mid)], n.xw.at[w])
        for k in (3, 1, 2):
            cross_xy[w].push(k)

    def z_start(w, slots):
        mats[w][a, own_half] = low(cross_xy[w].total(mats[w][a, own_half].astype(F32)))
        cross_back_z[w] = Reduce(lambda zi: mats[w].at[a, c * nz + zi], slots)
        cross_back_z[w].start()

    over_dp(3)

    def cross_back(h, _):
        at = pl.ds(pl.multiple_of(h * hd, hd), hd)
        dq, dk, dv = attend_back(n.qq[:, at], n.kk[:, at], n.vv[:, at], n.pp[h], n.dc[:, at])
        n.qq[:, at] = dq
        n.kk[:, at] = dk
        n.vv[:, at] = dv
        return 0

    lax.fori_loop(0, HEADS, cross_back, 0, unroll=2)
    again = [load(n.inputs.at[0, pl.ds(i * block, block)], n.pp.at[i]) for i in range(span // block)]
    cross_xy[3].combine()
    cross_grad(n.xn, n.vv[...], 2)
    start(core_dp[2])
    cross_grad(n.xn, n.kk[...], 1)
    start(core_dp[1])
    over_dp(2)
    cross_grad(n.an, n.qq[...], 0)
    start(core_dp[0])
    over_dp(1)
    gd1_z.combine()
    cross_xy[2].combine()
    over_dp(0)
    for k in (3, 1, 2):
        final_dp.push(k)
    gu1_z.combine()

    back, gain_part = norm_back(n.lt[...].astype(F32), gain[0][...],
                                dot(n.qq[...], n.wx[0].reshape(width, width), NT))
    set_gain(0, gain_part)
    n.gb[...] = low(n.ga[...] + back)
    outs.append(load(n.gb, n.glat.at[0]))
    arrived(again)

    def token_back(i, total):
        at = pl.ds(pl.multiple_of(i * big * block, big * block), big * block)
        grad = (dot(n.kk[at], n.wx[1].reshape(width, width), NT)
                + dot(n.vv[at], n.wx[2].reshape(width, width), NT))
        tokens = n.pp[pl.ds(i * big, big)].reshape(big * block, width).astype(F32)
        back, gain_part = norm_back(tokens, gain[1][...], grad)
        n.pp[pl.ds(i * big, big)] = low(back).reshape(big, block, width)
        return total + gain_part

    steps = span // (big * block)
    total = lax.fori_loop(0, steps // 4, token_back, jnp.zeros((1, width), F32))
    cross_xy[1].combine()
    z_start(3, n.d2.at[2])
    total = lax.fori_loop(steps // 4, steps // 2, token_back, total)
    cross_xy[0].combine()
    z_start(2, n.d2.at[3])
    cross_back_z[3].combine()
    set_gain(1, lax.fori_loop(steps // 2, steps, token_back, total))
    for i in range(span // block):
        outs.append(load(n.pp.at[i], n.ginp.at[0, pl.ds(i * block, block)]))
    gain_hops = small_sum(n.dg)
    gain_hops[0][0]()

    total = gd1_z.total()
    outs.append(out_rows(total, n.z1, n.ofd))
    cu1_dp = column_grads(gu1_z.total(), su4, n.CU1)
    start(cu1_dp)
    gain_hops[0][1]()
    gain_hops[1][0]()
    z_start(1, n.ZU.at[1])
    cross_back_z[2].combine()
    total = go_z.total()
    n.z2[0:rows] = total
    outs.append(load(n.z2.at[0:rows], n.oso))
    total = gq_z.total()
    sq_send = n.sqs
    sent(sq_dp)
    sq_send[...] = low(total)
    cq_dp = dp_group(lambda k: sq_send.at[apos(k)], lambda k: n.CQ.at[k - 1])
    start(cq_dp)
    z_start(0, n.ZU.at[0])
    cross_back_z[1].combine()
    final_dp.combine()
    gain_hops[1][1]()
    gain_hops[2][0]()
    cross_back_z[0].combine()
    n.dc[...] = low(final_dp.total(n.st[...]))
    outs.append(load(n.dc, n.out.at[0]))

    def put_columns(g, own, slots, staged, target):
        staged[0:rows] = own
        copies = [load(staged.at[0:rows], target.at[:, pl.ds(pl.multiple_of(a * width, width), width)])]
        for i in range(nd - 1):
            g(i).wait_recv()
            staged[(i + 1) * rows:(i + 2) * rows] = slots[i].astype(F32)
            copies.append(load(staged.at[(i + 1) * rows:(i + 2) * rows],
                               target.at[:, pl.ds(pl.multiple_of(apos(i + 1) * width, width), width)]))
        return copies

    outs += put_columns(cu2_dp, su3[a].astype(F32), n.CU2, n.st, n.ogu)
    outs += put_columns(cu1_dp, su4[a].astype(F32), n.CU1, n.own, n.ofu)
    recv(cq_dp)
    for i, target in enumerate((n.osq, n.osk, n.osv)):
        at = slice((i + 1) * rows, (i + 2) * rows)
        n.z2[at, pl.ds(pl.multiple_of(a * cols, cols), cols)] = sq_send[a, i].astype(F32)
        for k in range(1, nd):
            n.z2[at, pl.ds(pl.multiple_of(apos(k) * cols, cols), cols)] = n.CQ[k - 1, i].astype(F32)
        outs.append(load(n.z2.at[at], target))
    for w, target in ((3, n.oco), (2, n.ocv), (1, n.ock), (0, n.ocq)):
        total = cross_back_z[w].total()
        at = slice(w * rows, (w + 1) * rows)
        n.ga[at] = total
        outs.append(load(n.ga.at[at], target))
    gain_hops[2][1]()
    outs.append(load(n.dg, n.ggain))
    for g in ([cross_z, gains_z, gains_dp, final_dp, dm1, sq_z, so_z, gq_sib, go_sib, gq_z, go_z,
               cu1_dp, cu2_dp, cq_dp, gu1_sib, gd1_sib, gu1_z, gd1_z]
              + gains_sib + cross_dp + sq_sib + so_sib + core_dp + list(cross_xy.values()) + list(cross_back_z.values())
              + [g for line in cross_sib for g in line]):
        sent(g)
    arrived(outs)


def layer_norm(value, gain):
    center = value - jnp.mean(value, axis=-1, keepdims=True)
    spread = jnp.mean(center * center, axis=-1, keepdims=True)
    return center * lax.rsqrt(spread + EPS) * gain


def activate(value):
    return jax.nn.gelu(value, approximate=True)


def product(left, right):
    return jnp.dot(left, right, preferred_element_type=jnp.float32)


def weight_grad(left, right):
    return lax.dot_general(
        left, right, (((0,), (0,)), ((), ())), preferred_element_type=jnp.float32
    )


def back_product(grad, weight):
    return lax.dot_general(
        grad, weight, (((1,), (1,)), ((), ())), preferred_element_type=jnp.float32
    )


def plain_norm_back(value, gain, grad):
    _, pull = jax.vjp(layer_norm, value, gain)
    return pull(grad)


def activate_back(value, grad):
    _, pull = jax.vjp(activate, value)
    return pull(grad)[0]


def split_heads(value, groups):
    return value.reshape(groups, -1, HEADS, value.shape[-1] // HEADS)


def merge_heads(value):
    return value.reshape(-1, value.shape[2] * value.shape[3])


def masked_scores(query, key, valid):
    scale = query.shape[-1] ** (-0.5)
    scores = jnp.einsum("gqhd,gkhd->ghqk", query, key, preferred_element_type=jnp.float32) * scale
    return jnp.where(valid[:, None, None, :], scores, NEG)


def attend_forward(query, key, value, valid):
    scores = masked_scores(query, key, valid)
    top = jnp.max(scores, axis=-1, keepdims=True)
    expo = jnp.exp(scores - top)
    denom = jnp.sum(expo, axis=-1, keepdims=True)
    weights = (expo / denom).astype(jnp.bfloat16)
    mixed = jnp.einsum("ghqk,gkhd->gqhd", weights, value, preferred_element_type=jnp.float32)
    return (merge_heads(mixed).astype(jnp.bfloat16), top + jnp.log(denom))


def plain_attend_back(query, key, value, valid, logsum, grad_mixed):
    scale = query.shape[-1] ** (-0.5)
    probs = jnp.exp(masked_scores(query, key, valid) - logsum)
    grad_probs = jnp.einsum(
        "gqhd,gkhd->ghqk", grad_mixed, value, preferred_element_type=jnp.float32
    )
    inner = jnp.sum(probs * grad_probs, axis=-1, keepdims=True)
    grad_scores = (probs * (grad_probs - inner)).astype(jnp.bfloat16)
    weights = probs.astype(jnp.bfloat16)
    grad_query = (
        jnp.einsum("ghqk,gkhd->gqhd", grad_scores, key, preferred_element_type=jnp.float32) * scale
    )
    grad_key = (
        jnp.einsum("ghqk,gqhd->gkhd", grad_scores, query, preferred_element_type=jnp.float32)
        * scale
    )
    grad_value = jnp.einsum(
        "ghqk,gqhd->gkhd", weights, grad_mixed, preferred_element_type=jnp.float32
    )
    return (
        merge_heads(grad_query).astype(jnp.bfloat16),
        merge_heads(grad_key).astype(jnp.bfloat16),
        merge_heads(grad_value).astype(jnp.bfloat16),
    )


def feed_forward(resid, gain, w_up, w_down):
    normed = layer_norm(resid, gain.astype(jnp.float32)).astype(jnp.bfloat16)
    before = product(normed, w_up)
    hidden = activate(before).astype(jnp.bfloat16)
    return (resid + product(hidden, w_down), (normed, before, hidden))


def plain_feed_back(grad, resid, gain, saved, w_up, w_down):
    normed, before, hidden = saved
    grad_low = grad.astype(jnp.bfloat16)
    grad_down = weight_grad(hidden, grad_low)
    grad_before = activate_back(before, back_product(grad_low, w_down)).astype(jnp.bfloat16)
    grad_up = weight_grad(normed, grad_before)
    grad_resid, grad_gain = plain_norm_back(
        resid, gain.astype(jnp.float32), back_product(grad_before, w_up)
    )
    return (grad + grad_resid, grad_gain, grad_up, grad_down)


def project_back(grad, mixed, w_out, query, key, value, valid, logsum, groups):
    grad_low = grad.astype(jnp.bfloat16)
    grad_out = weight_grad(mixed, grad_low)
    grad_mixed = back_product(grad_low, w_out).astype(jnp.bfloat16)
    grad_query, grad_key, grad_value = plain_attend_back(
        split_heads(query, groups),
        split_heads(key, groups),
        split_heads(value, groups),
        valid,
        logsum,
        split_heads(grad_mixed, groups),
    )
    return (grad_out, grad_query, grad_key, grad_value)


def plain_layer(
    latents,
    inputs,
    frames,
    norm_latent,
    norm_input,
    cross_query,
    cross_key,
    cross_value,
    cross_output,
    norm_first,
    first_up,
    first_down,
    norm_self,
    self_query,
    self_key,
    self_value,
    self_output,
    norm_second,
    second_up,
    second_down,
    cotangent,
    mesh_size,
):
    groups, lat_rows, width = latents.shape
    span = inputs.shape[1]
    hidden_width = first_up.shape[1]
    low_type = jnp.bfloat16
    parts = mesh_size
    gains = (norm_latent, norm_input, norm_first, norm_self, norm_second)
    mats = (cross_query, cross_key, cross_value, cross_output, first_up, first_down,
            self_query, self_key, self_value, self_output, second_up, second_down)
    blocks = []
    for mat in mats:
        for start in range(0, mat.shape[1], width):
            blocks.append(mat[:, start:start + width])
    gain_row = jnp.concatenate([jnp.concatenate(gains), jnp.zeros((width - 5 * gains[0].shape[0],), jnp.float32)])
    gain_rows = jnp.concatenate([gain_row[None], jnp.zeros((15, width), jnp.float32)])
    packed = jnp.concatenate([gain_rows] + blocks).astype(low_type)
    whole = lax.all_gather(packed, ("dp", "fsdp"), axis=0, tiled=False)
    per = gains[0].shape[0]
    gathered_gains = [whole[:, 0, i * per:(i + 1) * per].reshape(width) for i in range(5)]
    gain_lat, gain_inp, gain_first, gain_self, gain_second = gathered_gains
    at = 16
    full = []
    for mat in mats:
        columns = []
        for start in range(0, mat.shape[1], width):
            columns.append(whole[:, at:at + mat.shape[0]].reshape(parts * mat.shape[0], width))
            at += mat.shape[0]
        full.append(columns[0] if len(columns) == 1 else jnp.concatenate(columns, axis=1))
    w_query, w_key, w_value, w_out, up_one, down_one, s_query, s_key, s_value, s_out, up_two, down_two = full
    positions = jnp.arange(span, dtype=jnp.int32)
    valid = positions[None, :] < (frames * FRAME_TOK)[:, None]
    every = jnp.ones((groups, lat_rows), dtype=bool)
    latent_rows = latents.reshape(groups * lat_rows, width).astype(jnp.float32)
    input_rows = inputs.reshape(groups * span, width).astype(jnp.float32)
    normed_lat = layer_norm(latent_rows, gain_lat.astype(jnp.float32)).astype(low_type)
    normed_inp = layer_norm(input_rows, gain_inp.astype(jnp.float32)).astype(low_type)
    query_one = product(normed_lat, w_query).astype(low_type)
    key_one = product(normed_inp, w_key).astype(low_type)
    value_one = product(normed_inp, w_value).astype(low_type)
    mixed_one, logsum_one = attend_forward(
        split_heads(query_one, groups),
        split_heads(key_one, groups),
        split_heads(value_one, groups),
        valid,
    )
    first_resid = latent_rows + product(mixed_one, w_out)
    second_resid, saved_one = feed_forward(first_resid, gain_first, up_one, down_one)
    normed_self = layer_norm(second_resid, gain_self.astype(jnp.float32)).astype(low_type)
    query_two = product(normed_self, s_query).astype(low_type)
    key_two = product(normed_self, s_key).astype(low_type)
    value_two = product(normed_self, s_value).astype(low_type)
    mixed_two, logsum_two = attend_forward(
        split_heads(query_two, groups),
        split_heads(key_two, groups),
        split_heads(value_two, groups),
        every,
    )
    third_resid = second_resid + product(mixed_two, s_out)
    final_resid, saved_two = feed_forward(third_resid, gain_second, up_two, down_two)
    result = final_resid.reshape(groups, lat_rows, width).astype(low_type)
    grad_final = cotangent.reshape(groups * lat_rows, width).astype(jnp.float32)
    grad_third, grad_gain_second, grad_up_two, grad_down_two = plain_feed_back(
        grad_final, third_resid, gain_second, saved_two, up_two, down_two
    )
    grad_s_out, grad_query_two, grad_key_two, grad_value_two = project_back(
        grad_third, mixed_two, s_out, query_two, key_two, value_two, every, logsum_two, groups
    )
    grad_s_query = weight_grad(normed_self, grad_query_two)
    grad_s_key = weight_grad(normed_self, grad_key_two)
    grad_s_value = weight_grad(normed_self, grad_value_two)
    grad_normed_self = (
        back_product(grad_query_two, s_query)
        + back_product(grad_key_two, s_key)
        + back_product(grad_value_two, s_value)
    )
    grad_from_self, grad_gain_self = plain_norm_back(
        second_resid, gain_self.astype(jnp.float32), grad_normed_self
    )
    grad_second = grad_third + grad_from_self
    grad_first, grad_gain_first, grad_up_one, grad_down_one = plain_feed_back(
        grad_second, first_resid, gain_first, saved_one, up_one, down_one
    )
    grad_w_out, grad_query_one, grad_key_one, grad_value_one = project_back(
        grad_first, mixed_one, w_out, query_one, key_one, value_one, valid, logsum_one, groups
    )
    grad_w_query = weight_grad(normed_lat, grad_query_one)
    grad_w_key = weight_grad(normed_inp, grad_key_one)
    grad_w_value = weight_grad(normed_inp, grad_value_one)
    grad_from_lat, grad_gain_lat = plain_norm_back(
        latent_rows, gain_lat.astype(jnp.float32), back_product(grad_query_one, w_query)
    )
    grad_latent_rows = grad_first + grad_from_lat
    grad_normed_inp = back_product(grad_key_one, w_key) + back_product(grad_value_one, w_value)
    grad_input_rows, grad_gain_inp = plain_norm_back(
        input_rows, gain_inp.astype(jnp.float32), grad_normed_inp
    )
    grad_mats = (grad_w_query, grad_w_key, grad_w_value, grad_w_out, grad_up_one, grad_down_one,
                 grad_s_query, grad_s_key, grad_s_value, grad_s_out, grad_up_two, grad_down_two)
    gain_grads = jnp.stack([grad_gain_lat, grad_gain_inp, grad_gain_first, grad_gain_self, grad_gain_second])
    gain_grads = jnp.moveaxis(gain_grads.reshape(5, parts, per), 1, 0).reshape(parts, 1, 5 * per)
    gain_grads = jnp.pad(gain_grads, ((0, 0), (0, 15), (0, width - 5 * per)))
    pieces = [gain_grads.astype(low_type)]
    for grad in grad_mats:
        for start in range(0, grad.shape[1], width):
            pieces.append(grad[:, start:start + width].reshape(parts, -1, width).astype(low_type))
    summed = lax.psum_scatter(jnp.concatenate(pieces, axis=1), ("dp", "fsdp"), scatter_dimension=0, tiled=False)
    summed = summed.astype(jnp.float32)
    gain_out = [summed[0, i * per:(i + 1) * per] for i in range(5)]
    at = 16
    out = []
    for mat in mats:
        columns = []
        for start in range(0, mat.shape[1], width):
            columns.append(summed[at:at + mat.shape[0]])
            at += mat.shape[0]
        out.append(columns[0] if len(columns) == 1 else jnp.concatenate(columns, axis=1))
    grad_latents = grad_latent_rows.reshape(groups, lat_rows, width).astype(low_type)
    grad_inputs = grad_input_rows.reshape(groups, span, width).astype(low_type)
    return (
        result, grad_latents, grad_inputs,
        gain_out[0], gain_out[1], out[0], out[1], out[2], out[3],
        gain_out[2], out[4], out[5],
        gain_out[3], out[6], out[7], out[8], out[9],
        gain_out[4], out[10], out[11],
    )


def hand_over(count, *refs):
    copies = [pltpu.make_async_copy(refs[i], refs[count + i], refs[-1].at[i]) for i in range(count)]
    for copy in copies:
        copy.start()
    for copy in copies:
        copy.wait()


def fits(mesh, lat, span, width, hidden):
    nd, nf = mesh.shape["dp"], mesh.shape["fsdp"]
    return (nd == 4 and nf == 8 and HEADS % nd == 0 and hidden == nd * width
            and width % (32 * nd * nf) == 0 and span == HEADS * lat and width // HEADS % 128 == 0)


def local(latents, inputs, frames, *rest, mesh):
    nd, nf = mesh.shape["dp"], mesh.shape["fsdp"]
    groups, lat, width = latents.shape
    span = inputs.shape[1]
    if groups != 1 or not fits(mesh, lat, span, width, rest[7].shape[1]):
        return plain_layer(latents, inputs, frames, *rest, mesh_size=mesh.size)
    (norm_latent, norm_input, cross_query, cross_key, cross_value, cross_output, norm_first, first_up,
     first_down, norm_self, self_query, self_key, self_value, self_output, norm_second, second_up,
     second_down, cotangent) = rest
    rows = cross_query.shape[0]
    index = lax.axis_index("dp") * nf + lax.axis_index("fsdp")
    gains = jnp.stack([norm_latent, norm_input, norm_first, norm_self, norm_second])
    lanes = lax.broadcasted_iota(jnp.int32, (8, 128), 1)
    gains = jnp.where(lanes // rows == lax.rem(index, 128 // rows),
                      jnp.tile(jnp.pad(gains, ((0, 3), (0, 0))), (1, 128 // rows)), 0.0)
    scratch = scratch_list(nd, nf, rows, width, lat, span, HEADS)
    anywhere = pl.BlockSpec(memory_space=pl.ANY)
    out_shape = (
        [jax.ShapeDtypeStruct(latents.shape, BF16)] * 2 + [jax.ShapeDtypeStruct(inputs.shape, BF16)]
        + [jax.ShapeDtypeStruct((8, width), F32)]
        + [jax.ShapeDtypeStruct(w.shape, F32) for w in (
            cross_query, cross_key, cross_value, cross_output, first_up, first_down,
            self_query, self_key, self_value, self_output, second_up, second_down)])
    flops = 2 * 3 * (lat * width * width * 22 + span * width * width * 2)
    results = pl.pallas_call(
        functools.partial(layer_kernel, INPUTS + OUTPUTS + tuple(scratch), nd, nf, rows),
        out_shape=out_shape,
        in_specs=[pl.BlockSpec(memory_space=pltpu.SMEM), pl.BlockSpec(memory_space=pltpu.VMEM)]
        + [anywhere] * (len(INPUTS) - 2),
        out_specs=[anywhere] * len(OUTPUTS),
        scratch_shapes=list(scratch.values()),
        compiler_params=pltpu.CompilerParams(
            collective_id=0, has_side_effects=True, vmem_limit_bytes=64 * 1024 * 1024),
        cost_estimate=pl.CostEstimate(flops=flops, bytes_accessed=30_000_000, transcendentals=4_000_000),
        name="layer",
    )(frames, gains, latents, inputs, cotangent, cross_query, cross_key, cross_value, cross_output,
      first_up, first_down, self_query, self_key, self_value, self_output, second_up, second_down)
    (result, grad_latents, grad_inputs, gain_grads, g_cq, g_ck, g_cv, g_co, g_fu, g_fd,
     g_sq, g_sk, g_sv, g_so, g_gu, g_gd) = pl.pallas_call(
        functools.partial(hand_over, len(OUTPUTS)),
        out_shape=out_shape,
        in_specs=[anywhere] * len(OUTPUTS),
        out_specs=[pl.BlockSpec(memory_space=pltpu.VMEM)] * len(OUTPUTS),
        scratch_shapes=[pltpu.SemaphoreType.DMA((len(OUTPUTS),))],
        compiler_params=pltpu.CompilerParams(vmem_limit_bytes=64 * 1024 * 1024),
        cost_estimate=pl.CostEstimate(flops=0, bytes_accessed=12_000_000, transcendentals=0),
        name="hand_over",
    )(*results)
    own = lax.dynamic_slice(gain_grads, (0, index * rows), (8, rows))
    return (result, grad_latents, grad_inputs, own[0], own[1], g_cq, g_ck, g_cv, g_co, own[2], g_fu, g_fd,
            own[3], g_sq, g_sk, g_sv, g_so, own[4], g_gu, g_gd)


def solution(mesh):
    in_specs = (
        P(("dp", "fsdp"), None, None),
        P(("dp", "fsdp"), None, None),
        P(("dp", "fsdp")),
        P(("dp", "fsdp")),
        P(("dp", "fsdp")),
        P(("dp", "fsdp"), None),
        P(("dp", "fsdp"), None),
        P(("dp", "fsdp"), None),
        P(("dp", "fsdp"), None),
        P(("dp", "fsdp")),
        P(("dp", "fsdp"), None),
        P(("dp", "fsdp"), None),
        P(("dp", "fsdp")),
        P(("dp", "fsdp"), None),
        P(("dp", "fsdp"), None),
        P(("dp", "fsdp"), None),
        P(("dp", "fsdp"), None),
        P(("dp", "fsdp")),
        P(("dp", "fsdp"), None),
        P(("dp", "fsdp"), None),
        P(("dp", "fsdp"), None, None),
    )
    out_specs = (
        P(("dp", "fsdp"), None, None),
        P(("dp", "fsdp"), None, None),
        P(("dp", "fsdp"), None, None),
        P(("dp", "fsdp")),
        P(("dp", "fsdp")),
        P(("dp", "fsdp"), None),
        P(("dp", "fsdp"), None),
        P(("dp", "fsdp"), None),
        P(("dp", "fsdp"), None),
        P(("dp", "fsdp")),
        P(("dp", "fsdp"), None),
        P(("dp", "fsdp"), None),
        P(("dp", "fsdp")),
        P(("dp", "fsdp"), None),
        P(("dp", "fsdp"), None),
        P(("dp", "fsdp"), None),
        P(("dp", "fsdp"), None),
        P(("dp", "fsdp")),
        P(("dp", "fsdp"), None),
        P(("dp", "fsdp"), None),
    )
    return jax.shard_map(functools.partial(local, mesh=mesh), mesh=mesh, in_specs=in_specs, out_specs=out_specs,
                         check_vma=False)
```

```python
import functools

import jax
import jax.numpy as jnp
from jax import lax
from jax.experimental import pallas as pl
from jax.experimental.pallas import tpu as pltpu
from jax.sharding import PartitionSpec as P

HEADS = 8
FRAME_TOK = 64
EPS = 1e-05
NEG = -1000000000.0
F32 = jnp.float32
BF16 = jnp.bfloat16
MESH = pl.DeviceIdType.MESH
NN = (((1,), (0,)), ((), ()))
NT = (((1,), (1,)), ((), ()))
TN = (((0,), (0,)), ((), ()))
GC0 = 0.7978845608
GC1 = 0.044715


def dot(left, right, dims):
    return lax.dot_general(left, right, dims, preferred_element_type=F32)


def low(value):
    return value.astype(BF16)


def flip(value, mask, size):
    out = 0
    bit = 1
    while bit < size:
        one = lax.rem(lax.div(value, jnp.int32(bit)), jnp.int32(2))
        if isinstance(mask, int):
            other = jnp.int32((mask // bit) % 2)
        else:
            other = lax.rem(lax.div(mask, jnp.int32(bit)), jnp.int32(2))
        out = out + lax.rem(one + other, jnp.int32(2)) * bit
        bit *= 2
    return out


def norm_parts(value):
    center = value - jnp.mean(value, axis=-1, keepdims=True)
    spread = jnp.mean(center * center, axis=-1, keepdims=True)
    inv = lax.rsqrt(spread + EPS)
    return center * inv, inv


def norm(value, gain):
    hat, _ = norm_parts(value)
    return low(hat * gain)


def norm_back(value, gain, grad):
    hat, inv = norm_parts(value)
    scaled = grad * gain
    out = inv * (
        scaled
        - jnp.mean(scaled, axis=-1, keepdims=True)
        - hat * jnp.mean(scaled * hat, axis=-1, keepdims=True)
    )
    return out, jnp.sum(grad * hat, axis=0, keepdims=True)


def gelu_both(value):
    square = value * value
    tan = jnp.tanh(GC0 * value * (1.0 + GC1 * square))
    half = 0.5 * (1.0 + tan)
    slope = half + 0.5 * value * (1.0 - tan * tan) * (GC0 * (1.0 + 3.0 * GC1 * square))
    return value * half, slope


INPUTS = ("frames", "gains", "latents", "inputs", "cot",
          "cq", "ck", "cv", "co", "fu", "fd", "sq_", "sk_", "sv_", "so_", "gu_", "gd_")
OUTPUTS = ("out", "glat", "ginp", "ggain",
           "ocq", "ock", "ocv", "oco", "ofu", "ofd", "osq", "osk", "osv", "oso", "ogu", "ogd")


def scratch_list(nd, nf, rows, width, lat, span, heads):
    nz = nf // 2
    hd = width // heads
    tp_cols = width // nd
    four = (nd, nf, rows, width)
    act = (nd, nz, rows, width)
    three = (nd - 1, nz, rows, width)
    vm = pltpu.VMEM
    return {
        "wx": vm((4,) + four, BF16),
        "up1": vm(four, BF16), "dn1": vm(four, BF16),
        "up2": vm(four, BF16), "dn2": vm(four, BF16),
        "sq": vm((3, nd, nf, rows, tp_cols), BF16), "so": vm((nf, rows, width), BF16),
        "sqs": vm((nd, 3, rows, tp_cols), BF16),
        "xn": vm((span, width), BF16), "kk": vm((span, width), BF16), "vv": vm((span, width), BF16),
        "pp": vm((heads, lat, span), BF16),
        "ag1": vm(act, BF16), "u1": vm(act, BF16), "d1": vm(act, BF16), "bg": vm(act, BF16),
        "ag2": vm(act, BF16), "u2": vm(act, BF16), "d2": vm(act, BF16),
        "gg": vm(act, BF16), "ggs": vm(act, BF16),
        "q2": vm((nd, lat, tp_cols), BF16), "k2": vm((nd, lat, tp_cols), BF16),
        "v2": vm((nd, lat, tp_cols), BF16), "c2": vm((nd, lat, tp_cols), BF16),
        "p2": vm((nd, heads // nd, lat, lat), BF16),
        "ra": vm(three, BF16), "rb": vm(three, BF16), "sa": vm(three, BF16), "sc": vm(three, BF16),
        "xw": vm((4,) + three, BF16),
        "GU": vm((2, nz, nd, rows, width), BF16), "GD": vm((2, nz, nd, rows, width), BF16),
        "GQ": vm((2, nz, nd, 3, rows, tp_cols), BF16), "GO": vm((2, nz, rows, width), BF16),
        "SU": vm((nz, nd, rows, width), BF16), "SD": vm((nz, nd, rows, width), BF16),
        "SQ": vm((nz, nd, 3, rows, tp_cols), BF16), "SO": vm((nz, rows, width), BF16),
        "ZU": vm((nz, nd, rows, width), BF16), "ZD": vm((nz, nd, rows, width), BF16),
        "ZQ": vm((nz, nd, 3, rows, tp_cols), BF16), "ZO": vm((nz, rows, width), BF16),
        "CU1": vm((nd - 1, rows, width), BF16), "CU2": vm((nd - 1, rows, width), BF16),
        "CQ": vm((nd - 1, 3, rows, tp_cols), BF16),
        "z1": vm((lat, width), F32), "z2": vm((lat, width), F32), "z3": vm((lat, width), F32),
        "ga": vm((lat, width), F32), "own": vm((lat, width), F32), "st": vm((lat, width), F32),
        "lt": vm((lat, width), BF16), "an": vm((lat, width), BF16), "qq": vm((lat, width), BF16),
        "cc": vm((lat, width), BF16), "gb": vm((lat, width), BF16), "dc": vm((lat, width), BF16),
        "gn": vm((8, width), F32), "dg": vm((8, width), F32),
        "gr": vm((1 + nz - 1 + nd - 1, 8, width), F32), "gs": vm((nd, nf, 8, 128), F32),
        "ss": pltpu.SemaphoreType.DMA((SEMS,)), "rs": pltpu.SemaphoreType.DMA((SEMS,)),
        "ls": pltpu.SemaphoreType.DMA((40,)),
    }


SEMS = 164


def layer_kernel(names, nd, nf, rows, *refs):
    r = dict(zip(names, refs))

    class Space:
        pass

    n = Space()
    for key, ref in r.items():
        setattr(n, key, ref)
    nz = nf // 2
    width = n.lt.shape[1]
    lat = n.lt.shape[0]
    span = n.xn.shape[0]
    hd = width // HEADS
    cols = width // nd
    local_heads = HEADS // nd
    scale = hd ** (-0.5)
    a = lax.axis_index("dp")
    b = lax.axis_index("fsdp")
    z = lax.div(b, jnp.int32(2))
    c = lax.rem(b, jnp.int32(2))
    sib = (a, z * 2 + 1 - c)

    def apos(k):
        return flip(a, k, nd)

    def zpos(m):
        return flip(z, m, nz)

    def bpos(m):
        return zpos(m) * 2 + c

    taken = [0, 0]

    def group(count, make, after=None):
        if after is None:
            base = taken[0]
            taken[0] += count
            assert taken[0] <= SEMS
        else:
            base = after.base
            assert count <= after.count

        def desc(i):
            src, dst, peer, *where = make(i)
            return pltpu.make_async_remote_copy(
                src_ref=src, dst_ref=dst, send_sem=n.ss.at[base + i],
                recv_sem=n.rs.at[base + (where[0] if where else i)],
                device_id=peer, device_id_type=MESH)

        desc.count = count
        desc.base = base
        return desc

    def start(g):
        for i in range(g.count):
            g(i).start()

    def recv(g):
        for i in range(g.count):
            g(i).wait_recv()

    def sent(g):
        if hasattr(g, "sent"):
            g.sent()
            return
        for i in range(g.count):
            g(i).wait_send()

    def load(src, dst):
        i = taken[1]
        taken[1] += 1
        copy = pltpu.make_async_copy(src, dst, n.ls.at[i])
        copy.start()
        return copy

    def dp_group(src, dst):
        return group(nd - 1, lambda i: (src(i + 1), dst(i + 1), (apos(i + 1), b)))

    inner = lax.rem(z, jnp.int32(3)) != 0
    outer = jnp.logical_not(inner)

    class Gather:
        def __init__(self, block):
            self.g = group(4, lambda i: (
                (block(b), block(b), (a, bpos(i + 1))) if i < 3
                else (block(bpos(2)), block(bpos(2)), (a, bpos(1)), 2)))

        def start(self):
            self.g(1).start()
            self.g(0).start()
            pl.when(inner)(lambda: self.g(2).start())

        def relay(self):
            @pl.when(inner)
            def _():
                self.g(1).wait_recv()
                self.g(3).start()

        def recv(self, m):
            if m == 2:
                pl.when(outer)(lambda: self.g(1).wait_recv())
            else:
                self.g(m - 1).wait_recv()

        def sent(self):
            self.g(0).wait_send()
            self.g(1).wait_send()

            @pl.when(inner)
            def _():
                self.g(2).wait_send()
                self.g(3).wait_send()

    class Reduce:
        def __init__(self, part, slots, after):
            self.part, self.slots = part, slots
            self.g = group(4, lambda i: (
                (part(zpos(i + 1)), slots.at[i], (a, bpos(i + 1))) if i < 3
                else (part(zpos(3)), slots.at[3], (a, bpos(1)))), after.g)

        def start(self):
            @pl.when(outer)
            def _():
                self.g(3).start()
                self.g(1).start()

            pl.when(inner)(lambda: self.g(2).start())
            self.g(0).start()

        def combine(self):
            @pl.when(inner)
            def _():
                self.g(3).wait_recv()
                ref = self.part(zpos(2))
                ref[...] = low(ref[...].astype(F32) + self.slots[3].astype(F32))
                self.g(1).start()

        def total(self):
            self.g(0).wait_recv()
            self.g(1).wait_recv()
            ref = self.part(z)

            @pl.when(inner)
            def _():
                self.g(2).wait_recv()
                ref[...] = low(ref[...].astype(F32) + self.slots[2].astype(F32))

            return ref[...].astype(F32) + self.slots[0].astype(F32) + self.slots[1].astype(F32)

        def sent(self):
            self.g(0).wait_send()
            self.g(1).wait_send()
            pl.when(outer)(lambda: self.g(3).wait_send())
            pl.when(inner)(lambda: self.g(2).wait_send())

    class Share:
        def __init__(self, one, two, three, after=None):
            def make(i):
                if i in (0, 2):
                    return one(i // 2) + ((apos(1), b),)
                if i in (1, 3):
                    return two(1 - i // 2) + ((apos(2), b),)
                return three(i - 4) + ((apos(2 - (i - 4)), b),)

            self.g = group(6, make, after and after.g)

        def start(self):
            for i in range(4):
                self.g(i).start()

        def relay(self):
            for i in range(2):
                self.g(i).wait_recv()
                self.g(4 + i).start()

        def recv(self, k):
            if isinstance(k, int):
                for i in ((2,), (3,), (4, 5))[k - 1]:
                    self.g(i).wait_recv()
                return
            for j in (1, 2, 3):
                pl.when(k == j)(lambda j=j: self.recv(j))

        def sent(self):
            for i in range(6):
                self.g(i).wait_send()

    def sib_group(src, dst):
        return group(1, lambda i: (src, dst, sib))

    class Merge:
        def __init__(self, part, slots, after=None):
            self.part, self.slots = part, slots

            def make(i):
                k, h, slot, peer = ((3, 0, 2, 2), (3, 1, 2, 1), (1, 1, 0, 1), (2, 0, 1, 2),
                                    (1, 0, 0, 1), (2, 1, 1, 2))[i]
                return part(k, h), slots.at[slot, halves[h]], (apos(peer), b)

            self.g = group(6, make, after and after.g)

        def push(self, k):
            if isinstance(k, int):
                for i in ((2,), (3,), (0, 1))[k - 1]:
                    self.g(i).start()
                return
            for j in (1, 2, 3):
                pl.when(k == j)(lambda j=j: self.push(j))

        def combine(self):
            for i, k, h in ((0, 1, 0), (1, 2, 1)):
                self.g(i).wait_recv()
                ref = self.part(k, h)
                ref[...] = low(ref[...].astype(F32) + self.slots[2, halves[h]].astype(F32))
                self.g(4 + i).start()

        def total(self, own):
            for i in (2, 3, 4, 5):
                self.g(i).wait_recv()
            return own + self.slots[0].reshape(own.shape).astype(F32) + self.slots[1].reshape(own.shape).astype(F32)

        def sent(self):
            for i in range(6):
                self.g(i).wait_send()

    mid = nz // 2
    halves = (slice(0, mid), slice(mid, nz))

    def stage(refs, dst):
        return [load(ref, dst.at[pl.ds(i * rows, rows)]) for i, ref in enumerate(refs)]

    blocks = [pl.ds(j * width, width) for j in range(nd)]
    in_cross = stage((n.cq, n.ck, n.cv, n.co), n.z1)
    in_up1 = stage([n.fu.at[:, s] for s in blocks], n.z2)
    in_dn1 = [load(n.fd, n.z3)]
    in_lat = [load(n.latents.at[0], n.lt)]
    in_x = [load(n.inputs.at[0], n.xn)]
    in_self = stage((n.sq_, n.sk_, n.sv_, n.so_), n.ga)
    in_up2 = stage([n.gu_.at[:, s] for s in blocks], n.own)
    in_dn2 = [load(n.gd_, n.st)]
    in_cot = [load(n.cot.at[0], n.gb)]

    def arrived(copies):
        for copy in copies:
            copy.wait()

    peers = [(apos(k), b) for k in range(1, nd)] + [(a, bpos(m)) for m in range(1, nz)] + [sib]
    barrier = pltpu.get_barrier_semaphore()
    for peer in peers:
        pl.semaphore_signal(barrier, inc=1, device_id=peer, device_id_type=MESH)

    def small_sum(buf):
        slots = n.gr
        hops = (group(1, lambda i: (buf, slots.at[0], sib)),
                group(nd - 1, lambda i: (buf, slots.at[1 + i], (apos(i + 1), b))),
                group(nz - 1, lambda i: (buf, slots.at[nd + i], (a, bpos(i + 1)))))
        phases = []
        first = 0
        for g in hops:
            def finish(g=g, first=first):
                recv(g)
                sent(g)
                total = buf[...]
                for i in range(g.count):
                    total = total + slots[first + i]
                buf[...] = total

            phases.append((functools.partial(start, g), finish))
            first += g.count
        return phases

    pl.semaphore_wait(barrier, len(peers))
    n.gs[a, b] = low(n.gains[...]).astype(F32)
    gains_z = Gather(lambda bi: n.gs.at[a, bi])
    gains_sib = [sib_group(n.gs.at[a, bpos(m)], n.gs.at[a, bpos(m)]) for m in range(nz)]
    gains_dp = dp_group(lambda k: n.gs.at[a], lambda k: n.gs.at[a])
    gains_z.start()
    start(gains_sib[0])
    arrived(in_cross)
    for i in range(4):
        n.wx[i, a, b] = low(n.z1[i * rows:(i + 1) * rows])

    def wx_at(ai, bi):
        return n.wx.at[:, ai, bi]

    cross_z = Gather(lambda bi: n.wx.at[:, a, bi])
    cross_dp = []
    for m in range(nz):
        def direct(h, m=m):
            at = n.wx.at[2 * h:2 * h + 2, a, bpos(m)]
            return at, at

        def relayed(h, m=m):
            at = n.wx.at[2 * h:2 * h + 2, apos(1 + h), bpos(m)]
            return at, at

        cross_dp.append(Share(direct, direct, relayed))
    cross_sib = [[sib_group(wx_at(apos(k), bpos(m)), wx_at(apos(k), bpos(m))) for m in range(nz)]
                 for k in range(nd)]
    cross_z.start()
    cross_dp[0].start()
    start(cross_sib[0][0])

    su1, su2 = n.xw.at[3, 0], n.xw.at[3, 1]

    def put_up(staged, sends, up):
        for j in range(nd):
            sends[j] = low(staged[j * rows:(j + 1) * rows])
        up[a, b] = sends[a]

    def put_dn(staged, dn):
        dn[lax.div(b * nd, jnp.int32(nf)), pl.ds(lax.rem(b * nd, jnp.int32(nf)), nd)] = (
            low(staged[...]).reshape(nd, rows, width))

    def dn_at(dn, bi):
        return dn.at[lax.div(bi * nd, jnp.int32(nf)), pl.ds(lax.rem(bi * nd, jnp.int32(nf)), nd)]

    arrived(in_up1)
    put_up(n.z2, su1, n.up1)
    up1_dp = dp_group(lambda k: su1.at[apos(k)], lambda k: n.up1.at[a, b])
    start(up1_dp)
    arrived(in_dn1)
    put_dn(n.z3, n.dn1)
    arrived(in_self)
    for i in range(3):
        for j in range(nd):
            n.sqs[j, i] = low(n.ga[i * rows:(i + 1) * rows, j * cols:(j + 1) * cols])
    for i in range(3):
        n.sq[i, a, b] = n.sqs[a, i]
    n.so[b] = low(n.ga[3 * rows:4 * rows])
    arrived(in_up2)
    put_up(n.own, su2, n.up2)
    arrived(in_dn2)
    put_dn(n.st, n.dn2)
    arrived(in_cot)
    act_rows = (nz, rows, width)

    def up_z(up):
        return Gather(lambda bi: up.at[:, bi])

    def up_sib(up):
        return [sib_group(up.at[:, bpos(m)], up.at[:, bpos(m)]) for m in range(nz)]

    def dn_z(dn):
        return Gather(lambda bi: dn_at(dn, bi))

    def dn_sib(dn):
        return [sib_group(dn_at(dn, bpos(m)), dn_at(dn, bpos(m))) for m in range(nz)]

    gain = [n.gn.at[i:i + 1] for i in range(5)]

    arrived(in_lat)
    arrived(in_x)
    gains_z.relay()
    for m in (1, 2, 3):
        gains_z.recv(m)
        start(gains_sib[m])
    for g in gains_sib:
        recv(g)
    start(gains_dp)
    cross_z.relay()
    for m in (1, 2, 3):
        cross_z.recv(m)
        cross_dp[m].start()
        start(cross_sib[0][m])
        if m == 1:
            cross_dp[0].relay()
    up1_z, up1_sib, dn1_z, dn1_sib = up_z(n.up1), up_sib(n.up1), dn_z(n.dn1), dn_sib(n.dn1)
    recv(up1_dp)
    up1_z.start()
    dn1_z.start()
    cross_dp[1].relay()
    cross_dp[2].relay()
    recv(gains_dp)
    per = 128 // rows
    for j in range(width // 128):
        tile = 0.0
        for i in range(j * per, (j + 1) * per):
            tile = tile + n.gs[i // nf, i % nf]
        n.gn[:, j * 128:(j + 1) * 128] = tile

    block = lat
    big = 1

    def token_norm(i, _):
        at = pl.ds(pl.multiple_of(i * block, block), block)
        n.xn[at] = norm(n.xn[at].astype(F32), gain[1][...])
        return 0

    n.an[...] = norm(n.lt[...].astype(F32), gain[0][...])
    lax.fori_loop(0, span // block, token_norm, 0)

    cross_dp[3].relay()
    for m in range(nz):
        for k in range(1, nd):
            cross_dp[m].recv(k)
            start(cross_sib[k][m])
        if m == 1:
            up1_z.relay()
    up2_dp = dp_group(lambda k: su2.at[apos(k)], lambda k: n.up2.at[a, b])
    sq_dp = dp_group(lambda k: n.sqs.at[apos(k)], lambda k: n.sq.at[:, a, b])
    start(sq_dp)
    start(up2_dp)
    for k in range(nd):
        for m in range(nz):
            recv(cross_sib[k][m])

    def rows_of(ref, k):
        return ref[k].reshape(lat, width)

    def spread(buf, value, after=None):
        buf[0] = value.reshape(act_rows)
        g = Share(lambda h: (buf.at[0, halves[h]], buf.at[1, halves[h]]),
                  lambda h: (buf.at[0, halves[h]], buf.at[2, halves[h]]),
                  lambda h: (buf.at[1 + h, halves[h]], buf.at[3, halves[h]]), after)
        g.start()
        return g

    taken[1] = 0
    cot_dp = spread(n.gg, n.gb[...])
    def wcols(i, at):
        return n.wx[i, :, :, :, at].reshape(width, at.size)

    def full(ref):
        return ref[...].reshape(width, width)

    n.qq[...] = low(dot(n.an[...], n.wx[0].reshape(width, width), NN))
    wide = 256

    def token_proj(i, _):
        at = pl.ds(pl.multiple_of(i * wide, wide), wide)
        n.kk[:, at] = low(dot(n.xn[...], wcols(1, at), NN))
        n.vv[:, at] = low(dot(n.xn[...], wcols(2, at), NN))
        return 0

    lax.fori_loop(0, width // wide, token_proj, 0)
    dn1_z.relay()
    valid = lax.broadcasted_iota(jnp.int32, (lat, span), 1) < n.frames[0] * FRAME_TOK

    def softmax(scores):
        expo = jnp.exp(scores - jnp.max(scores, axis=-1, keepdims=True))
        return low(expo / jnp.sum(expo, axis=-1, keepdims=True))

    def cross_head(h, _):
        at = pl.ds(pl.multiple_of(h * hd, hd), hd)
        scores = jnp.where(valid, dot(n.qq[:, at], n.kk[:, at], NT) * scale, NEG)
        probs = softmax(scores)
        n.pp[h] = probs
        n.cc[:, at] = low(dot(probs, n.vv[:, at], NN))
        return 0

    lax.fori_loop(0, HEADS, cross_head, 0, unroll=2)
    recv(sq_dp)
    sq_z = Gather(lambda bi: n.sq.at[:, :, bi])
    so_z = Gather(lambda bi: n.so.at[bi])
    sq_sib = [sib_group(n.sq.at[:, :, bpos(m)], n.sq.at[:, :, bpos(m)]) for m in range(nz)]
    so_sib = [sib_group(n.so.at[bpos(m)], n.so.at[bpos(m)]) for m in range(nz)]
    sq_z.start()
    so_z.start()
    cot_dp.relay()
    z1 = n.lt[...].astype(F32) + dot(n.cc[...], n.wx[3].reshape(width, width), NN)
    n.z1[...] = z1

    acts = []

    def collect(make, gathered, sends, slots, previous):
        if previous is not None:
            sent(previous)
        back = Merge(lambda k, h: sends.at[k - 1, halves[h]], slots, acts[0] if acts else None)
        acts.append(back)
        back.gathered = gathered
        n.own[...] = make(0)
        gathered.relay()

        def step(i, _):
            gathered.recv(i + 1)
            sends[i] = low(make(i + 1)).reshape(act_rows)
            back.push(i + 1)
            return 0

        lax.fori_loop(0, nd - 1, step, 0)
        return back

    def gather_sum(back, slots):
        if back.gathered is not None:
            sent(back.gathered)
        return back.total(n.own[...])

    def feed_hidden(ag, u, d, up):
        def make(k):
            value, slope = gelu_both(dot(rows_of(ag, k), full(up), NN))
            hidden = low(value)
            u[k] = hidden.reshape(act_rows)
            d[k] = low(slope).reshape(act_rows)
            return hidden

        return make

    def feed_make(ag, u, d, up, dn):
        hide = feed_hidden(ag, u, d, up)

        def make(k):
            return dot(hide(k), full(dn), NN)

        return make

    ag1_dp = spread(n.ag1, norm(z1, gain[2][...]))
    recv(up2_dp)
    up2_z, up2_sib, dn2_z, dn2_sib = up_z(n.up2), up_sib(n.up2), dn_z(n.dn2), dn_sib(n.dn2)
    for m in range(nz):
        for g, line in ((up1_z, up1_sib), (dn1_z, dn1_sib)):
            if m > 0:
                g.recv(m)
            start(line[m])
    sq_z.relay()
    so_z.relay()
    up2_z.start()
    dn2_z.start()
    for m in range(nz):
        recv(up1_sib[m])
        recv(dn1_sib[m])
    out1 = collect(feed_make(n.ag1, n.u1, n.d1, n.up1, n.dn1), ag1_dp, n.sa, n.ra, None)
    out1.combine()
    for g in ([cross_z, gains_z, gains_dp, up1_z, dn1_z] + gains_sib + cross_dp
              + [g for line in cross_sib for g in line]):
        sent(g)
    z2 = n.z1[...] + gather_sum(out1, n.ra)
    n.z2[...] = z2

    bg_dp = spread(n.bg, norm(z2, gain[3][...]), ag1_dp)
    for m in range(nz):
        for g, line in ((sq_z, sq_sib), (so_z, so_sib)):
            if m > 0:
                g.recv(m)
            start(line[m])
    up2_z.relay()
    for m in range(nz):
        recv(sq_sib[m])
        recv(so_sib[m])

    def self_make(k):
        normed = rows_of(n.bg, k)
        for i, ref in enumerate((n.q2, n.k2, n.v2)):
            ref[k] = low(dot(normed, n.sq[i].reshape(width, cols), NN))
        for h in range(local_heads):
            at = slice(h * hd, (h + 1) * hd)
            probs = softmax(dot(n.q2[k, :, at], n.k2[k, :, at], NT) * scale)
            n.p2[k, h] = probs
            n.c2[k, :, at] = low(dot(probs, n.v2[k, :, at], NN))
        return dot(n.c2[k], n.so[...].reshape(cols, width), NN)

    out_self = collect(self_make, bg_dp, n.sa, n.rb, out1)
    out_self.combine()
    dn2_z.relay()
    z3 = n.z2[...] + gather_sum(out_self, n.rb)
    n.z3[...] = z3

    ag2_dp = spread(n.ag2, norm(z3, gain[4][...]), ag1_dp)
    for m in range(nz):
        if m > 0:
            up2_z.recv(m)
        start(up2_sib[m])
    for m in range(nz):
        recv(up2_sib[m])

    sc, rc = n.sc, n.rb

    def feed_back(g, d, up, dn):
        def make(k):
            grad = dot(rows_of(g, k), full(dn), NT)
            grad_low = low(rows_of(d, k).astype(F32) * grad)
            d[k] = grad_low.reshape(act_rows)
            return dot(grad_low, full(up), NT)

        return make

    hide2 = feed_hidden(n.ag2, n.u2, n.d2, n.up2)
    back2 = feed_back(n.gg, n.d2, n.up2, n.dn2)
    final_dp = Merge(lambda k, h: sc.at[k - 1, halves[h]], rc)
    sent(up1_dp)
    sent(up2_dp)
    hide2(0)
    ag2_dp.relay()

    def hide_step(i, _):
        ag2_dp.recv(i + 1)
        hide2(i + 1)
        return 0

    lax.fori_loop(0, nd - 1, hide_step, 0)

    def put_grad(value, ref, first):
        for i in range(value.shape[0] // rows):
            ai, bi = divmod(first + i, nf)
            zi, ci = divmod(bi, 2)
            ref[ci, zi, ai] = value[i * rows:(i + 1) * rows]

    def put_down(value, ref, first):
        for i in range(value.shape[0] // rows):
            bi, ai = divmod(first + i, nd)
            zi, ci = divmod(bi, 2)
            ref[ci, zi, ai] = value[i * rows:(i + 1) * rows]

    tall = 256

    def every_row(ref, at=slice(None)):
        value = ref[:, :, :, at]
        return value.reshape(value.shape[0] * value.shape[1] * value.shape[2], value.shape[3])

    def up_grad(ag, d):
        for i in range(width // tall):
            at = slice(i * tall, (i + 1) * tall)
            put_grad(low(dot(every_row(ag, at), every_row(d), TN)), n.GU, i * tall // rows)

    def down_grad(u, g):
        for i in range(width // tall):
            at = slice(i * tall, (i + 1) * tall)
            put_down(low(dot(every_row(u, at), every_row(g), TN)), n.GD, i * tall // rows)

    def core_sum(grad, other):
        for i in range(nz):
            grad[c, i] = low(grad[c, i].astype(F32) + other[i].astype(F32))

    def sib_grads(grad, other):
        g = sib_group(grad.at[1 - c], other)
        start(g)
        return g

    def z_grads(grad, slots, after):
        g = Reduce(lambda zi: grad.at[c, zi], slots, after)
        g.start()
        return g

    for k in range(1, nd):
        cot_dp.recv(k)
    down_grad(n.u2, n.gg)
    gd2_sib = sib_grads(n.GD, n.SD)
    for m in range(nz):
        if m > 0:
            dn2_z.recv(m)
        start(dn2_sib[m])
    for m in range(nz):
        recv(dn2_sib[m])
    sent(out_self)
    dm2 = Merge(lambda k, h: n.sa.at[k - 1, halves[h]], n.ra, out1)
    dm2.gathered = None
    n.own[...] = back2(0)
    recv(gd2_sib)
    core_sum(n.GD, n.SD)
    gd2_z = z_grads(n.GD, n.ZD, cross_z)

    def back_step(i, _):
        k = lax.rem(i + 2, 3) + 1
        n.sa[k - 1] = low(back2(k)).reshape(act_rows)
        dm2.push(k)
        return 0

    lax.fori_loop(0, nd - 1, back_step, 0)
    sent(ag2_dp)
    up_grad(n.ag2, n.d2)
    gu2_sib = sib_grads(n.GU, n.SU)
    dm2.combine()
    n.st[...] = n.z3[...] + dot(rows_of(n.u2, 0), full(n.dn2), NN)

    def out_step(i, _):
        sc[i] = low(dot(rows_of(n.u2, i + 1), full(n.dn2), NN)).reshape(act_rows)
        return 0

    lax.fori_loop(0, nd - 1, out_step, 0)
    recv(gu2_sib)
    core_sum(n.GU, n.SU)
    gu2_z = z_grads(n.GU, n.ZU, gains_z)

    def set_gain(i, value):
        n.dg[i:i + 1] = value

    n.dg[...] = jnp.zeros_like(n.dg)
    back, gain_part = norm_back(n.z3[...], gain[4][...], gather_sum(dm2, n.ra))
    set_gain(4, gain_part)
    ga = rows_of(n.gg, 0).astype(F32) + back
    n.ga[...] = ga

    sent(cot_dp)

    gs_dp = spread(n.ggs, low(ga), ag1_dp)
    gd2_z.combine()

    def attend_back(q, k, v, probs, grad):
        grad_probs = dot(grad, v, NT)
        wide_probs = probs.astype(F32)
        inner = jnp.sum(wide_probs * grad_probs, axis=-1, keepdims=True)
        scores = low(wide_probs * (grad_probs - inner))
        return (low(dot(scores, k, NN) * scale), low(dot(scores, q, TN) * scale),
                low(dot(probs, grad, TN)))

    def self_back(k):
        grad = low(dot(rows_of(n.ggs, k), n.so[...].reshape(cols, width), NT))
        for h in range(local_heads):
            at = slice(h * hd, (h + 1) * hd)
            dq, dk, dv = attend_back(n.q2[k, :, at], n.k2[k, :, at], n.v2[k, :, at],
                                     n.p2[k, h], grad[:, at])
            n.q2[k, :, at] = dq
            n.k2[k, :, at] = dk
            n.v2[k, :, at] = dv
        total = 0.0
        for i, ref in enumerate((n.q2, n.k2, n.v2)):
            total = total + dot(ref[k], n.sq[i].reshape(width, cols), NT)
        return total

    db = collect(self_back, gs_dp, n.sa, n.rb, dm2)
    for i, ref in enumerate((n.q2, n.k2, n.v2)):
        value = low(dot(every_row(n.bg), ref[...].reshape(nd * lat, cols), TN))
        for j in range(width // rows):
            ai, bi = divmod(j, nf)
            zi, ci = divmod(bi, 2)
            n.GQ[ci, zi, ai, i] = value[j * rows:(j + 1) * rows]
    value = low(dot(n.c2[...].reshape(nd * lat, cols), every_row(n.ggs), TN))
    for bi in range(nf):
        zi, ci = divmod(bi, 2)
        n.GO[ci, zi] = value[bi * rows:(bi + 1) * rows]
    gq_sib = sib_grads(n.GQ, n.SQ)
    go_sib = sib_grads(n.GO, n.SO)
    db.combine()
    gu2_z.combine()
    recv(gq_sib)
    core_sum(n.GQ, n.SQ)
    gq_z = z_grads(n.GQ, n.ZQ, up1_z)
    recv(go_sib)
    core_sum(n.GO, n.SO)
    go_z = z_grads(n.GO, n.ZO, dn1_z)
    back, gain_part = norm_back(n.z2[...], gain[3][...], gather_sum(db, n.rb))
    set_gain(3, gain_part)
    ga = n.ga[...] + back
    n.ga[...] = ga

    outs = []
    gf_dp = spread(n.gg, low(ga), ag1_dp)
    dm1 = collect(feed_back(n.gg, n.d1, n.up1, n.dn1), gf_dp, n.sa, n.ra, db)

    def out_rows(value, staged, target):
        staged[...] = value.reshape(staged.shape)
        return load(staged, target)

    gq_z.combine()
    go_z.combine()
    total = gd2_z.total()
    outs.append(out_rows(total, n.z3, n.ogd))
    total = gu2_z.total()

    def column_grads(total, sends, slots):
        sends[...] = low(total)
        return dp_group(lambda k: sends.at[apos(k)], lambda k: slots.at[k - 1])

    su3, su4 = n.d2.at[0], n.d2.at[1]
    cu2_dp = column_grads(total, su3, n.CU2)
    for g in (gu2_sib, gd2_sib, gu2_z, gd2_z):
        sent(g)
    down_grad(n.u1, n.gg)
    gd1_sib = sib_grads(n.GD, n.SD)
    dm1.combine()
    zu1, zd1 = n.ag2, n.u2
    for g in (up2_z, dn2_z, sq_z, so_z):
        sent(g)
    recv(gd1_sib)
    core_sum(n.GD, n.SD)
    gd1_z = z_grads(n.GD, zd1, up2_z)
    up_grad(n.ag1, n.d1)
    gu1_sib = sib_grads(n.GU, n.SU)
    recv(gu1_sib)
    core_sum(n.GU, n.SU)
    gu1_z = z_grads(n.GU, zu1, dn2_z)
    back, gain_part = norm_back(n.z1[...], gain[2][...], gather_sum(dm1, n.ra))
    set_gain(2, gain_part)
    ga = n.ga[...] + back
    n.ga[...] = ga

    n.gb[...] = low(ga)
    mats = (n.up2, n.dn2, n.up1, n.dn1)
    others = (n.u1, n.d1, n.ag1, n.bg)

    def put_cross(value, ref, first):
        for i in range(value.shape[0] // rows):
            ai, bi = divmod(first + i, nf)
            zi, ci = divmod(bi, 2)
            ref[ai, ci * nz + zi] = value[i * rows:(i + 1) * rows]

    def cross_grad(left, right, which):
        for i in range(width // tall):
            put_cross(low(dot(left[:, i * tall:(i + 1) * tall], right, TN)), mats[which],
                      i * tall // rows)

    def half(ref, ci):
        return ref.at[:, pl.ds(ci * nz, nz)]

    for g in up1_sib + dn1_sib + up2_sib + dn2_sib:
        sent(g)
    start(cu2_dp)
    cross_grad(n.cc, n.gb[...], 3)
    core_dp = [group(1, lambda i, w=w: (half(mats[w], 1 - c), others[w], sib)) for w in range(4)]
    start(core_dp[3])
    n.dc[...] = low(dot(n.gb[...], n.wx[3].reshape(width, width), NT))
    own_half = pl.ds(c * nz, nz)
    cross_xy, cross_back_z = {}, {}

    def over_dp(w):
        recv(core_dp[w])
        for ai in range(nd):
            mats[w][ai, own_half] = low(mats[w][ai, own_half].astype(F32) + others[w][ai].astype(F32))
        cross_xy[w] = Merge(lambda k, h, w=w: mats[w].at[apos(k), pl.ds(c * nz + h * mid, mid)], n.xw.at[w],
                            cross_dp[w])
        for k in (3, 1, 2):
            cross_xy[w].push(k)

    def z_start(w, slots, after):
        mats[w][a, own_half] = low(cross_xy[w].total(mats[w][a, own_half].astype(F32)))
        cross_back_z[w] = Reduce(lambda zi: mats[w].at[a, c * nz + zi], slots, after)
        cross_back_z[w].start()

    over_dp(3)

    def cross_back(h, _):
        at = pl.ds(pl.multiple_of(h * hd, hd), hd)
        dq, dk, dv = attend_back(n.qq[:, at], n.kk[:, at], n.vv[:, at], n.pp[h], n.dc[:, at])
        n.qq[:, at] = dq
        n.kk[:, at] = dk
        n.vv[:, at] = dv
        return 0

    lax.fori_loop(0, HEADS, cross_back, 0, unroll=2)
    again = [load(n.inputs.at[0, pl.ds(i * block, block)], n.pp.at[i]) for i in range(span // block)]
    cross_xy[3].combine()
    cross_grad(n.xn, n.vv[...], 2)
    start(core_dp[2])
    cross_grad(n.xn, n.kk[...], 1)
    start(core_dp[1])
    over_dp(2)
    cross_grad(n.an, n.qq[...], 0)
    start(core_dp[0])
    over_dp(1)
    gd1_z.combine()
    cross_xy[2].combine()
    over_dp(0)
    for k in (3, 1, 2):
        final_dp.push(k)
    gu1_z.combine()

    back, gain_part = norm_back(n.lt[...].astype(F32), gain[0][...],
                                dot(n.qq[...], n.wx[0].reshape(width, width), NT))
    set_gain(0, gain_part)
    n.gb[...] = low(n.ga[...] + back)
    outs.append(load(n.gb, n.glat.at[0]))
    arrived(again)

    def token_back(i, total):
        at = pl.ds(pl.multiple_of(i * big * block, big * block), big * block)
        grad = (dot(n.kk[at], n.wx[1].reshape(width, width), NT)
                + dot(n.vv[at], n.wx[2].reshape(width, width), NT))
        tokens = n.pp[pl.ds(i * big, big)].reshape(big * block, width).astype(F32)
        back, gain_part = norm_back(tokens, gain[1][...], grad)
        n.pp[pl.ds(i * big, big)] = low(back).reshape(big, block, width)
        return total + gain_part

    steps = span // (big * block)
    total = lax.fori_loop(0, steps // 4, token_back, jnp.zeros((1, width), F32))
    cross_xy[1].combine()
    z_start(3, n.d2.at[2], sq_z)
    total = lax.fori_loop(steps // 4, steps // 2, token_back, total)
    cross_xy[0].combine()
    z_start(2, n.d2.at[3], so_z)
    cross_back_z[3].combine()
    set_gain(1, lax.fori_loop(steps // 2, steps, token_back, total))
    for i in range(span // block):
        outs.append(load(n.pp.at[i], n.ginp.at[0, pl.ds(i * block, block)]))
    gain_hops = small_sum(n.dg)
    gain_hops[0][0]()

    total = gd1_z.total()
    outs.append(out_rows(total, n.z1, n.ofd))
    cu1_dp = column_grads(gu1_z.total(), su4, n.CU1)
    start(cu1_dp)
    gain_hops[0][1]()
    gain_hops[1][0]()
    z_start(1, n.ZU.at[1], gd2_z)
    cross_back_z[2].combine()
    total = go_z.total()
    n.z2[0:rows] = total
    outs.append(load(n.z2.at[0:rows], n.oso))
    total = gq_z.total()
    sq_send = n.sqs
    sent(sq_dp)
    sq_send[...] = low(total)
    cq_dp = dp_group(lambda k: sq_send.at[apos(k)], lambda k: n.CQ.at[k - 1])
    start(cq_dp)
    z_start(0, n.ZU.at[0], gu2_z)
    cross_back_z[1].combine()
    final_dp.combine()
    gain_hops[1][1]()
    gain_hops[2][0]()
    cross_back_z[0].combine()
    n.dc[...] = low(final_dp.total(n.st[...]))
    outs.append(load(n.dc, n.out.at[0]))

    def put_columns(g, own, slots, staged, target):
        staged[0:rows] = own
        copies = [load(staged.at[0:rows], target.at[:, pl.ds(pl.multiple_of(a * width, width), width)])]
        for i in range(nd - 1):
            g(i).wait_recv()
            staged[(i + 1) * rows:(i + 2) * rows] = slots[i].astype(F32)
            copies.append(load(staged.at[(i + 1) * rows:(i + 2) * rows],
                               target.at[:, pl.ds(pl.multiple_of(apos(i + 1) * width, width), width)]))
        return copies

    outs += put_columns(cu2_dp, su3[a].astype(F32), n.CU2, n.st, n.ogu)
    outs += put_columns(cu1_dp, su4[a].astype(F32), n.CU1, n.own, n.ofu)
    recv(cq_dp)
    for i, target in enumerate((n.osq, n.osk, n.osv)):
        at = slice((i + 1) * rows, (i + 2) * rows)
        n.z2[at, pl.ds(pl.multiple_of(a * cols, cols), cols)] = sq_send[a, i].astype(F32)
        for k in range(1, nd):
            n.z2[at, pl.ds(pl.multiple_of(apos(k) * cols, cols), cols)] = n.CQ[k - 1, i].astype(F32)
        outs.append(load(n.z2.at[at], target))
    for w, target in ((3, n.oco), (2, n.ocv), (1, n.ock), (0, n.ocq)):
        total = cross_back_z[w].total()
        at = slice(w * rows, (w + 1) * rows)
        n.ga[at] = total
        outs.append(load(n.ga.at[at], target))
    gain_hops[2][1]()
    outs.append(load(n.dg, n.ggain))
    for g in ([final_dp, dm1, gq_sib, go_sib, gq_z, go_z, cu1_dp, cu2_dp, cq_dp, gu1_sib, gd1_sib, gu1_z, gd1_z]
              + sq_sib + so_sib + core_dp + list(cross_xy.values()) + list(cross_back_z.values())):
        sent(g)
    arrived(outs)


def layer_norm(value, gain):
    center = value - jnp.mean(value, axis=-1, keepdims=True)
    spread = jnp.mean(center * center, axis=-1, keepdims=True)
    return center * lax.rsqrt(spread + EPS) * gain


def activate(value):
    return jax.nn.gelu(value, approximate=True)


def product(left, right):
    return jnp.dot(left, right, preferred_element_type=jnp.float32)


def weight_grad(left, right):
    return lax.dot_general(
        left, right, (((0,), (0,)), ((), ())), preferred_element_type=jnp.float32
    )


def back_product(grad, weight):
    return lax.dot_general(
        grad, weight, (((1,), (1,)), ((), ())), preferred_element_type=jnp.float32
    )


def plain_norm_back(value, gain, grad):
    _, pull = jax.vjp(layer_norm, value, gain)
    return pull(grad)


def activate_back(value, grad):
    _, pull = jax.vjp(activate, value)
    return pull(grad)[0]


def split_heads(value, groups):
    return value.reshape(groups, -1, HEADS, value.shape[-1] // HEADS)


def merge_heads(value):
    return value.reshape(-1, value.shape[2] * value.shape[3])


def masked_scores(query, key, valid):
    scale = query.shape[-1] ** (-0.5)
    scores = jnp.einsum("gqhd,gkhd->ghqk", query, key, preferred_element_type=jnp.float32) * scale
    return jnp.where(valid[:, None, None, :], scores, NEG)


def attend_forward(query, key, value, valid):
    scores = masked_scores(query, key, valid)
    top = jnp.max(scores, axis=-1, keepdims=True)
    expo = jnp.exp(scores - top)
    denom = jnp.sum(expo, axis=-1, keepdims=True)
    weights = (expo / denom).astype(jnp.bfloat16)
    mixed = jnp.einsum("ghqk,gkhd->gqhd", weights, value, preferred_element_type=jnp.float32)
    return (merge_heads(mixed).astype(jnp.bfloat16), top + jnp.log(denom))


def plain_attend_back(query, key, value, valid, logsum, grad_mixed):
    scale = query.shape[-1] ** (-0.5)
    probs = jnp.exp(masked_scores(query, key, valid) - logsum)
    grad_probs = jnp.einsum(
        "gqhd,gkhd->ghqk", grad_mixed, value, preferred_element_type=jnp.float32
    )
    inner = jnp.sum(probs * grad_probs, axis=-1, keepdims=True)
    grad_scores = (probs * (grad_probs - inner)).astype(jnp.bfloat16)
    weights = probs.astype(jnp.bfloat16)
    grad_query = (
        jnp.einsum("ghqk,gkhd->gqhd", grad_scores, key, preferred_element_type=jnp.float32) * scale
    )
    grad_key = (
        jnp.einsum("ghqk,gqhd->gkhd", grad_scores, query, preferred_element_type=jnp.float32)
        * scale
    )
    grad_value = jnp.einsum(
        "ghqk,gqhd->gkhd", weights, grad_mixed, preferred_element_type=jnp.float32
    )
    return (
        merge_heads(grad_query).astype(jnp.bfloat16),
        merge_heads(grad_key).astype(jnp.bfloat16),
        merge_heads(grad_value).astype(jnp.bfloat16),
    )


def feed_forward(resid, gain, w_up, w_down):
    normed = layer_norm(resid, gain.astype(jnp.float32)).astype(jnp.bfloat16)
    before = product(normed, w_up)
    hidden = activate(before).astype(jnp.bfloat16)
    return (resid + product(hidden, w_down), (normed, before, hidden))


def plain_feed_back(grad, resid, gain, saved, w_up, w_down):
    normed, before, hidden = saved
    grad_low = grad.astype(jnp.bfloat16)
    grad_down = weight_grad(hidden, grad_low)
    grad_before = activate_back(before, back_product(grad_low, w_down)).astype(jnp.bfloat16)
    grad_up = weight_grad(normed, grad_before)
    grad_resid, grad_gain = plain_norm_back(
        resid, gain.astype(jnp.float32), back_product(grad_before, w_up)
    )
    return (grad + grad_resid, grad_gain, grad_up, grad_down)


def project_back(grad, mixed, w_out, query, key, value, valid, logsum, groups):
    grad_low = grad.astype(jnp.bfloat16)
    grad_out = weight_grad(mixed, grad_low)
    grad_mixed = back_product(grad_low, w_out).astype(jnp.bfloat16)
    grad_query, grad_key, grad_value = plain_attend_back(
        split_heads(query, groups),
        split_heads(key, groups),
        split_heads(value, groups),
        valid,
        logsum,
        split_heads(grad_mixed, groups),
    )
    return (grad_out, grad_query, grad_key, grad_value)


def plain_layer(
    latents,
    inputs,
    frames,
    norm_latent,
    norm_input,
    cross_query,
    cross_key,
    cross_value,
    cross_output,
    norm_first,
    first_up,
    first_down,
    norm_self,
    self_query,
    self_key,
    self_value,
    self_output,
    norm_second,
    second_up,
    second_down,
    cotangent,
    mesh_size,
):
    groups, lat_rows, width = latents.shape
    span = inputs.shape[1]
    hidden_width = first_up.shape[1]
    low_type = jnp.bfloat16
    parts = mesh_size
    gains = (norm_latent, norm_input, norm_first, norm_self, norm_second)
    mats = (cross_query, cross_key, cross_value, cross_output, first_up, first_down,
            self_query, self_key, self_value, self_output, second_up, second_down)
    blocks = []
    for mat in mats:
        for start in range(0, mat.shape[1], width):
            blocks.append(mat[:, start:start + width])
    gain_row = jnp.concatenate([jnp.concatenate(gains), jnp.zeros((width - 5 * gains[0].shape[0],), jnp.float32)])
    gain_rows = jnp.concatenate([gain_row[None], jnp.zeros((15, width), jnp.float32)])
    packed = jnp.concatenate([gain_rows] + blocks).astype(low_type)
    whole = lax.all_gather(packed, ("dp", "fsdp"), axis=0, tiled=False)
    per = gains[0].shape[0]
    gathered_gains = [whole[:, 0, i * per:(i + 1) * per].reshape(width) for i in range(5)]
    gain_lat, gain_inp, gain_first, gain_self, gain_second = gathered_gains
    at = 16
    full = []
    for mat in mats:
        columns = []
        for start in range(0, mat.shape[1], width):
            columns.append(whole[:, at:at + mat.shape[0]].reshape(parts * mat.shape[0], width))
            at += mat.shape[0]
        full.append(columns[0] if len(columns) == 1 else jnp.concatenate(columns, axis=1))
    w_query, w_key, w_value, w_out, up_one, down_one, s_query, s_key, s_value, s_out, up_two, down_two = full
    positions = jnp.arange(span, dtype=jnp.int32)
    valid = positions[None, :] < (frames * FRAME_TOK)[:, None]
    every = jnp.ones((groups, lat_rows), dtype=bool)
    latent_rows = latents.reshape(groups * lat_rows, width).astype(jnp.float32)
    input_rows = inputs.reshape(groups * span, width).astype(jnp.float32)
    normed_lat = layer_norm(latent_rows, gain_lat.astype(jnp.float32)).astype(low_type)
    normed_inp = layer_norm(input_rows, gain_inp.astype(jnp.float32)).astype(low_type)
    query_one = product(normed_lat, w_query).astype(low_type)
    key_one = product(normed_inp, w_key).astype(low_type)
    value_one = product(normed_inp, w_value).astype(low_type)
    mixed_one, logsum_one = attend_forward(
        split_heads(query_one, groups),
        split_heads(key_one, groups),
        split_heads(value_one, groups),
        valid,
    )
    first_resid = latent_rows + product(mixed_one, w_out)
    second_resid, saved_one = feed_forward(first_resid, gain_first, up_one, down_one)
    normed_self = layer_norm(second_resid, gain_self.astype(jnp.float32)).astype(low_type)
    query_two = product(normed_self, s_query).astype(low_type)
    key_two = product(normed_self, s_key).astype(low_type)
    value_two = product(normed_self, s_value).astype(low_type)
    mixed_two, logsum_two = attend_forward(
        split_heads(query_two, groups),
        split_heads(key_two, groups),
        split_heads(value_two, groups),
        every,
    )
    third_resid = second_resid + product(mixed_two, s_out)
    final_resid, saved_two = feed_forward(third_resid, gain_second, up_two, down_two)
    result = final_resid.reshape(groups, lat_rows, width).astype(low_type)
    grad_final = cotangent.reshape(groups * lat_rows, width).astype(jnp.float32)
    grad_third, grad_gain_second, grad_up_two, grad_down_two = plain_feed_back(
        grad_final, third_resid, gain_second, saved_two, up_two, down_two
    )
    grad_s_out, grad_query_two, grad_key_two, grad_value_two = project_back(
        grad_third, mixed_two, s_out, query_two, key_two, value_two, every, logsum_two, groups
    )
    grad_s_query = weight_grad(normed_self, grad_query_two)
    grad_s_key = weight_grad(normed_self, grad_key_two)
    grad_s_value = weight_grad(normed_self, grad_value_two)
    grad_normed_self = (
        back_product(grad_query_two, s_query)
        + back_product(grad_key_two, s_key)
        + back_product(grad_value_two, s_value)
    )
    grad_from_self, grad_gain_self = plain_norm_back(
        second_resid, gain_self.astype(jnp.float32), grad_normed_self
    )
    grad_second = grad_third + grad_from_self
    grad_first, grad_gain_first, grad_up_one, grad_down_one = plain_feed_back(
        grad_second, first_resid, gain_first, saved_one, up_one, down_one
    )
    grad_w_out, grad_query_one, grad_key_one, grad_value_one = project_back(
        grad_first, mixed_one, w_out, query_one, key_one, value_one, valid, logsum_one, groups
    )
    grad_w_query = weight_grad(normed_lat, grad_query_one)
    grad_w_key = weight_grad(normed_inp, grad_key_one)
    grad_w_value = weight_grad(normed_inp, grad_value_one)
    grad_from_lat, grad_gain_lat = plain_norm_back(
        latent_rows, gain_lat.astype(jnp.float32), back_product(grad_query_one, w_query)
    )
    grad_latent_rows = grad_first + grad_from_lat
    grad_normed_inp = back_product(grad_key_one, w_key) + back_product(grad_value_one, w_value)
    grad_input_rows, grad_gain_inp = plain_norm_back(
        input_rows, gain_inp.astype(jnp.float32), grad_normed_inp
    )
    grad_mats = (grad_w_query, grad_w_key, grad_w_value, grad_w_out, grad_up_one, grad_down_one,
                 grad_s_query, grad_s_key, grad_s_value, grad_s_out, grad_up_two, grad_down_two)
    gain_grads = jnp.stack([grad_gain_lat, grad_gain_inp, grad_gain_first, grad_gain_self, grad_gain_second])
    gain_grads = jnp.moveaxis(gain_grads.reshape(5, parts, per), 1, 0).reshape(parts, 1, 5 * per)
    gain_grads = jnp.pad(gain_grads, ((0, 0), (0, 15), (0, width - 5 * per)))
    pieces = [gain_grads.astype(low_type)]
    for grad in grad_mats:
        for start in range(0, grad.shape[1], width):
            pieces.append(grad[:, start:start + width].reshape(parts, -1, width).astype(low_type))
    summed = lax.psum_scatter(jnp.concatenate(pieces, axis=1), ("dp", "fsdp"), scatter_dimension=0, tiled=False)
    summed = summed.astype(jnp.float32)
    gain_out = [summed[0, i * per:(i + 1) * per] for i in range(5)]
    at = 16
    out = []
    for mat in mats:
        columns = []
        for start in range(0, mat.shape[1], width):
            columns.append(summed[at:at + mat.shape[0]])
            at += mat.shape[0]
        out.append(columns[0] if len(columns) == 1 else jnp.concatenate(columns, axis=1))
    grad_latents = grad_latent_rows.reshape(groups, lat_rows, width).astype(low_type)
    grad_inputs = grad_input_rows.reshape(groups, span, width).astype(low_type)
    return (
        result, grad_latents, grad_inputs,
        gain_out[0], gain_out[1], out[0], out[1], out[2], out[3],
        gain_out[2], out[4], out[5],
        gain_out[3], out[6], out[7], out[8], out[9],
        gain_out[4], out[10], out[11],
    )


def hand_over(count, *refs):
    ins, outs, held, sems = refs[:count], refs[count:2 * count], refs[2 * count:3 * count], refs[-1]
    first = [pltpu.make_async_copy(ins[i], held[i], sems.at[i]) for i in range(count)]
    second = [pltpu.make_async_copy(held[i], outs[i], sems.at[count + i]) for i in range(count)]
    for copy in first:
        copy.start()
    for one, two in zip(first, second):
        one.wait()
        two.start()
    for copy in second:
        copy.wait()


def fits(mesh, lat, span, width, hidden):
    nd, nf = mesh.shape["dp"], mesh.shape["fsdp"]
    return (nd == 4 and nf == 8 and HEADS % nd == 0 and hidden == nd * width
            and width % (32 * nd * nf) == 0 and span == HEADS * lat and width // HEADS % 128 == 0)


def local(latents, inputs, frames, *rest, mesh):
    nd, nf = mesh.shape["dp"], mesh.shape["fsdp"]
    groups, lat, width = latents.shape
    span = inputs.shape[1]
    if groups != 1 or not fits(mesh, lat, span, width, rest[7].shape[1]):
        return plain_layer(latents, inputs, frames, *rest, mesh_size=mesh.size)
    (norm_latent, norm_input, cross_query, cross_key, cross_value, cross_output, norm_first, first_up,
     first_down, norm_self, self_query, self_key, self_value, self_output, norm_second, second_up,
     second_down, cotangent) = rest
    rows = cross_query.shape[0]
    index = lax.axis_index("dp") * nf + lax.axis_index("fsdp")
    gains = jnp.stack([norm_latent, norm_input, norm_first, norm_self, norm_second])
    lanes = lax.broadcasted_iota(jnp.int32, (8, 128), 1)
    gains = jnp.where(lanes // rows == lax.rem(index, 128 // rows),
                      jnp.tile(jnp.pad(gains, ((0, 3), (0, 0))), (1, 128 // rows)), 0.0)
    scratch = scratch_list(nd, nf, rows, width, lat, span, HEADS)
    anywhere = pl.BlockSpec(memory_space=pl.ANY)
    out_shape = (
        [jax.ShapeDtypeStruct(latents.shape, BF16)] * 2 + [jax.ShapeDtypeStruct(inputs.shape, BF16)]
        + [jax.ShapeDtypeStruct((8, width), F32)]
        + [jax.ShapeDtypeStruct(w.shape, F32) for w in (
            cross_query, cross_key, cross_value, cross_output, first_up, first_down,
            self_query, self_key, self_value, self_output, second_up, second_down)])
    flops = 2 * 3 * (lat * width * width * 22 + span * width * width * 2)
    results = pl.pallas_call(
        functools.partial(layer_kernel, INPUTS + OUTPUTS + tuple(scratch), nd, nf, rows),
        out_shape=out_shape,
        in_specs=[pl.BlockSpec(memory_space=pltpu.SMEM), pl.BlockSpec(memory_space=pltpu.VMEM)]
        + [anywhere] * (len(INPUTS) - 2),
        out_specs=[anywhere] * len(OUTPUTS),
        scratch_shapes=list(scratch.values()),
        compiler_params=pltpu.CompilerParams(
            collective_id=0, has_side_effects=True, vmem_limit_bytes=64 * 1024 * 1024),
        cost_estimate=pl.CostEstimate(flops=flops, bytes_accessed=30_000_000, transcendentals=4_000_000),
        name="layer",
    )(frames, gains, latents, inputs, cotangent, cross_query, cross_key, cross_value, cross_output,
      first_up, first_down, self_query, self_key, self_value, self_output, second_up, second_down)
    (result, grad_latents, grad_inputs, gain_grads, g_cq, g_ck, g_cv, g_co, g_fu, g_fd,
     g_sq, g_sk, g_sv, g_so, g_gu, g_gd) = pl.pallas_call(
        functools.partial(hand_over, len(OUTPUTS)),
        out_shape=out_shape,
        in_specs=[anywhere] * len(OUTPUTS),
        out_specs=[anywhere] * len(OUTPUTS),
        scratch_shapes=[pltpu.VMEM(o.shape, o.dtype) for o in out_shape]
        + [pltpu.SemaphoreType.DMA((2 * len(OUTPUTS),))],
        compiler_params=pltpu.CompilerParams(vmem_limit_bytes=64 * 1024 * 1024),
        cost_estimate=pl.CostEstimate(flops=0, bytes_accessed=12_000_000, transcendentals=0),
        name="hand_over",
    )(*results)
    own = lax.dynamic_slice(gain_grads, (0, index * rows), (8, rows))
    return (result, grad_latents, grad_inputs, own[0], own[1], g_cq, g_ck, g_cv, g_co, own[2], g_fu, g_fd,
            own[3], g_sq, g_sk, g_sv, g_so, own[4], g_gu, g_gd)


def solution(mesh):
    in_specs = (
        P(("dp", "fsdp"), None, None),
        P(("dp", "fsdp"), None, None),
        P(("dp", "fsdp")),
        P(("dp", "fsdp")),
        P(("dp", "fsdp")),
        P(("dp", "fsdp"), None),
        P(("dp", "fsdp"), None),
        P(("dp", "fsdp"), None),
        P(("dp", "fsdp"), None),
        P(("dp", "fsdp")),
        P(("dp", "fsdp"), None),
        P(("dp", "fsdp"), None),
        P(("dp", "fsdp")),
        P(("dp", "fsdp"), None),
        P(("dp", "fsdp"), None),
        P(("dp", "fsdp"), None),
        P(("dp", "fsdp"), None),
        P(("dp", "fsdp")),
        P(("dp", "fsdp"), None),
        P(("dp", "fsdp"), None),
        P(("dp", "fsdp"), None, None),
    )
    out_specs = (
        P(("dp", "fsdp"), None, None),
        P(("dp", "fsdp"), None, None),
        P(("dp", "fsdp"), None, None),
        P(("dp", "fsdp")),
        P(("dp", "fsdp")),
        P(("dp", "fsdp"), None),
        P(("dp", "fsdp"), None),
        P(("dp", "fsdp"), None),
        P(("dp", "fsdp"), None),
        P(("dp", "fsdp")),
        P(("dp", "fsdp"), None),
        P(("dp", "fsdp"), None),
        P(("dp", "fsdp")),
        P(("dp", "fsdp"), None),
        P(("dp", "fsdp"), None),
        P(("dp", "fsdp"), None),
        P(("dp", "fsdp"), None),
        P(("dp", "fsdp")),
        P(("dp", "fsdp"), None),
        P(("dp", "fsdp"), None),
    )
    return jax.shard_map(functools.partial(local, mesh=mesh), mesh=mesh, in_specs=in_specs, out_specs=out_specs,
                         check_vma=False)
```

```python
import functools

import jax
import jax.numpy as jnp
from jax import lax
from jax.experimental import pallas as pl
from jax.experimental.pallas import tpu as pltpu
from jax.sharding import PartitionSpec as P

HEADS = 8
FRAME_TOK = 64
EPS = 1e-05
NEG = -1000000000.0
F32 = jnp.float32
BF16 = jnp.bfloat16
MESH = pl.DeviceIdType.MESH
NN = (((1,), (0,)), ((), ()))
NT = (((1,), (1,)), ((), ()))
TN = (((0,), (0,)), ((), ()))
GC0 = 0.7978845608
GC1 = 0.044715


def dot(left, right, dims):
    return lax.dot_general(left, right, dims, preferred_element_type=F32)


def low(value):
    return value.astype(BF16)


def flip(value, mask, size):
    out = 0
    bit = 1
    while bit < size:
        one = lax.rem(lax.div(value, jnp.int32(bit)), jnp.int32(2))
        if isinstance(mask, int):
            other = jnp.int32((mask // bit) % 2)
        else:
            other = lax.rem(lax.div(mask, jnp.int32(bit)), jnp.int32(2))
        out = out + lax.rem(one + other, jnp.int32(2)) * bit
        bit *= 2
    return out


def norm_parts(value):
    center = value - jnp.mean(value, axis=-1, keepdims=True)
    spread = jnp.mean(center * center, axis=-1, keepdims=True)
    inv = lax.rsqrt(spread + EPS)
    return center * inv, inv


def norm(value, gain):
    hat, _ = norm_parts(value)
    return low(hat * gain)


def norm_back(value, gain, grad):
    hat, inv = norm_parts(value)
    scaled = grad * gain
    out = inv * (
        scaled
        - jnp.mean(scaled, axis=-1, keepdims=True)
        - hat * jnp.mean(scaled * hat, axis=-1, keepdims=True)
    )
    return out, jnp.sum(grad * hat, axis=0, keepdims=True)


def gelu_both(value):
    square = value * value
    tan = jnp.tanh(GC0 * value * (1.0 + GC1 * square))
    half = 0.5 * (1.0 + tan)
    slope = half + 0.5 * value * (1.0 - tan * tan) * (GC0 * (1.0 + 3.0 * GC1 * square))
    return value * half, slope


INPUTS = ("frames", "gains", "latents", "inputs", "cot",
          "cq", "ck", "cv", "co", "fu", "fd", "sq_", "sk_", "sv_", "so_", "gu_", "gd_")
OUTPUTS = ("out", "glat", "ginp", "ggain",
           "ocq", "ock", "ocv", "oco", "ofu", "ofd", "osq", "osk", "osv", "oso", "ogu", "ogd")


def scratch_list(nd, nf, rows, width, lat, span, heads):
    nz = nf // 2
    hd = width // heads
    tp_cols = width // nd
    four = (nd, nf, rows, width)
    act = (nd, nz, rows, width)
    three = (nd - 1, nz, rows, width)
    vm = pltpu.VMEM
    return {
        "wx": vm((4,) + four, BF16),
        "up1": vm(four, BF16), "dn1": vm(four, BF16),
        "up2": vm(four, BF16), "dn2": vm(four, BF16),
        "sq": vm((3, nd, nf, rows, tp_cols), BF16), "so": vm((nf, rows, width), BF16),
        "sqs": vm((nd, 3, rows, tp_cols), BF16),
        "xn": vm((span, width), BF16), "kk": vm((span, width), BF16), "vv": vm((span, width), BF16),
        "pp": vm((heads, lat, span), BF16),
        "ag1": vm(act, BF16), "u1": vm(act, BF16), "d1": vm(act, BF16), "bg": vm(act, BF16),
        "ag2": vm(act, BF16), "u2": vm(act, BF16), "d2": vm(act, BF16),
        "gg": vm(act, BF16), "ggs": vm(act, BF16),
        "q2": vm((nd, lat, tp_cols), BF16), "k2": vm((nd, lat, tp_cols), BF16),
        "v2": vm((nd, lat, tp_cols), BF16), "c2": vm((nd, lat, tp_cols), BF16),
        "p2": vm((nd, heads // nd, lat, lat), BF16),
        "ra": vm(three, BF16), "rb": vm(three, BF16), "sa": vm(three, BF16), "sc": vm(three, BF16),
        "xw": vm((4,) + three, BF16),
        "GU": vm((2, nz, nd, rows, width), BF16), "GD": vm((2, nz, nd, rows, width), BF16),
        "GQ": vm((2, nz, nd, 3, rows, tp_cols), BF16), "GO": vm((2, nz, rows, width), BF16),
        "SU": vm((nz, nd, rows, width), BF16), "SD": vm((nz, nd, rows, width), BF16),
        "SQ": vm((nz, nd, 3, rows, tp_cols), BF16), "SO": vm((nz, rows, width), BF16),
        "ZU": vm((nz, nd, rows, width), BF16), "ZD": vm((nz, nd, rows, width), BF16),
        "ZQ": vm((nz, nd, 3, rows, tp_cols), BF16), "ZO": vm((nz, rows, width), BF16),
        "CU1": vm((nd - 1, rows, width), BF16), "CU2": vm((nd - 1, rows, width), BF16),
        "CQ": vm((nd - 1, 3, rows, tp_cols), BF16),
        "z1": vm((lat, width), F32), "z2": vm((lat, width), F32), "z3": vm((lat, width), F32),
        "ga": vm((lat, width), F32), "own": vm((lat, width), F32),
        "ob": vm((lat, width), BF16),
        "lt": vm((lat, width), BF16), "an": vm((lat, width), BF16), "qq": vm((lat, width), BF16),
        "cc": vm((lat, width), BF16), "gb": vm((lat, width), BF16), "dc": vm((lat, width), BF16),
        "gn": vm((8, width), F32), "dg": vm((8, width), F32),
        "gr": vm((1 + nz - 1 + nd - 1, 8, width), F32), "gs": vm((nd, nf, 8, 128), F32),
        "ss": pltpu.SemaphoreType.DMA((SEMS,)), "rs": pltpu.SemaphoreType.DMA((SEMS,)),
        "ls": pltpu.SemaphoreType.DMA((40,)),
    }


SEMS = 164


def layer_kernel(names, nd, nf, rows, *refs):
    r = dict(zip(names, refs))

    class Space:
        pass

    n = Space()
    for key, ref in r.items():
        setattr(n, key, ref)
    nz = nf // 2
    width = n.lt.shape[1]
    lat = n.lt.shape[0]
    span = n.xn.shape[0]
    hd = width // HEADS
    cols = width // nd
    local_heads = HEADS // nd
    scale = hd ** (-0.5)
    a = lax.axis_index("dp")
    b = lax.axis_index("fsdp")
    z = lax.div(b, jnp.int32(2))
    c = lax.rem(b, jnp.int32(2))
    sib = (a, z * 2 + 1 - c)

    def apos(k):
        return flip(a, k, nd)

    def zpos(m):
        return flip(z, m, nz)

    def bpos(m):
        return zpos(m) * 2 + c

    taken = [0, 0]

    def group(count, make, after=None):
        if after is None:
            base = taken[0]
            taken[0] += count
            assert taken[0] <= SEMS
        else:
            base = after.base
            assert count <= after.count

        def desc(i):
            src, dst, peer, *where = make(i)
            return pltpu.make_async_remote_copy(
                src_ref=src, dst_ref=dst, send_sem=n.ss.at[base + i],
                recv_sem=n.rs.at[base + (where[0] if where else i)],
                device_id=peer, device_id_type=MESH)

        desc.count = count
        desc.base = base
        return desc

    def start(g):
        for i in range(g.count):
            g(i).start()

    def recv(g):
        for i in range(g.count):
            g(i).wait_recv()

    def sent(g):
        if hasattr(g, "sent"):
            g.sent()
            return
        for i in range(g.count):
            g(i).wait_send()

    def load(src, dst):
        i = taken[1]
        taken[1] += 1
        copy = pltpu.make_async_copy(src, dst, n.ls.at[i])
        copy.start()
        return copy

    def dp_group(src, dst):
        return group(nd - 1, lambda i: (src(i + 1), dst(i + 1), (apos(i + 1), b)))

    inner = lax.rem(z, jnp.int32(3)) != 0
    outer = jnp.logical_not(inner)

    class Gather:
        def __init__(self, block):
            self.g = group(4, lambda i: (
                (block(b), block(b), (a, bpos(i + 1))) if i < 3
                else (block(bpos(2)), block(bpos(2)), (a, bpos(1)), 2)))

        def start(self):
            self.g(1).start()
            self.g(0).start()
            pl.when(inner)(lambda: self.g(2).start())

        def relay(self):
            @pl.when(inner)
            def _():
                self.g(1).wait_recv()
                self.g(3).start()

        def recv(self, m):
            if m == 2:
                pl.when(outer)(lambda: self.g(1).wait_recv())
            else:
                self.g(m - 1).wait_recv()

        def sent(self):
            self.g(0).wait_send()
            self.g(1).wait_send()

            @pl.when(inner)
            def _():
                self.g(2).wait_send()
                self.g(3).wait_send()

    class Reduce:
        def __init__(self, part, slots, after):
            self.part, self.slots = part, slots
            self.g = group(4, lambda i: (
                (part(zpos(i + 1)), slots.at[i], (a, bpos(i + 1))) if i < 3
                else (part(zpos(3)), slots.at[3], (a, bpos(1)))), after.g)

        def start(self):
            @pl.when(outer)
            def _():
                self.g(3).start()
                self.g(1).start()

            pl.when(inner)(lambda: self.g(2).start())
            self.g(0).start()

        def combine(self):
            @pl.when(inner)
            def _():
                self.g(3).wait_recv()
                ref = self.part(zpos(2))
                ref[...] = low(ref[...].astype(F32) + self.slots[3].astype(F32))
                self.g(1).start()

        def total(self):
            self.g(0).wait_recv()
            self.g(1).wait_recv()
            ref = self.part(z)

            @pl.when(inner)
            def _():
                self.g(2).wait_recv()
                ref[...] = low(ref[...].astype(F32) + self.slots[2].astype(F32))

            return ref[...].astype(F32) + self.slots[0].astype(F32) + self.slots[1].astype(F32)

        def sent(self):
            self.g(0).wait_send()
            self.g(1).wait_send()
            pl.when(outer)(lambda: self.g(3).wait_send())
            pl.when(inner)(lambda: self.g(2).wait_send())

    class Share:
        def __init__(self, one, two, three, after=None):
            def make(i):
                if i in (0, 2):
                    return one(i // 2) + ((apos(1), b),)
                if i in (1, 3):
                    return two(1 - i // 2) + ((apos(2), b),)
                return three(i - 4) + ((apos(2 - (i - 4)), b),)

            self.g = group(6, make, after and after.g)

        def start(self):
            for i in range(4):
                self.g(i).start()

        def relay(self):
            for i in range(2):
                self.g(i).wait_recv()
                self.g(4 + i).start()

        def recv(self, k):
            if isinstance(k, int):
                for i in ((2,), (3,), (4, 5))[k - 1]:
                    self.g(i).wait_recv()
                return
            for j in (1, 2, 3):
                pl.when(k == j)(lambda j=j: self.recv(j))

        def sent(self):
            for i in range(6):
                self.g(i).wait_send()

    def sib_group(src, dst):
        return group(1, lambda i: (src, dst, sib))

    class Merge:
        def __init__(self, part, slots, after=None):
            self.part, self.slots = part, slots

            def make(i):
                k, h, slot, peer = ((3, 0, 2, 2), (3, 1, 2, 1), (1, 1, 0, 1), (2, 0, 1, 2),
                                    (1, 0, 0, 1), (2, 1, 1, 2))[i]
                return part(k, h), slots.at[slot, halves[h]], (apos(peer), b)

            self.g = group(6, make, after and after.g)

        def push(self, k):
            if isinstance(k, int):
                for i in ((2,), (3,), (0, 1))[k - 1]:
                    self.g(i).start()
                return
            for j in (1, 2, 3):
                pl.when(k == j)(lambda j=j: self.push(j))

        def combine(self):
            for i, k, h in ((0, 1, 0), (1, 2, 1)):
                self.g(i).wait_recv()
                ref = self.part(k, h)
                ref[...] = low(ref[...].astype(F32) + self.slots[2, halves[h]].astype(F32))
                self.g(4 + i).start()

        def total(self, own):
            for i in (2, 3, 4, 5):
                self.g(i).wait_recv()
            return own + self.slots[0].reshape(own.shape).astype(F32) + self.slots[1].reshape(own.shape).astype(F32)

        def sent(self):
            for i in range(6):
                self.g(i).wait_send()

    mid = nz // 2
    halves = (slice(0, mid), slice(mid, nz))

    def stage(refs, dst):
        return [load(ref, dst.at[pl.ds(i * rows, rows)]) for i, ref in enumerate(refs)]

    blocks = [pl.ds(j * width, width) for j in range(nd)]
    in_cross = stage((n.cq, n.ck, n.cv, n.co), n.z1)
    in_up1 = stage([n.fu.at[:, s] for s in blocks], n.z2)
    in_dn1 = [load(n.fd, n.z3)]
    in_lat = [load(n.latents.at[0], n.lt)]
    in_x = [load(n.inputs.at[0], n.xn)]
    in_self = stage((n.sq_, n.sk_, n.sv_, n.so_), n.ga)
    in_up2 = stage([n.gu_.at[:, s] for s in blocks], n.own)
    in_cot = [load(n.cot.at[0], n.gb)]

    def arrived(copies):
        for copy in copies:
            copy.wait()

    peers = [(apos(k), b) for k in range(1, nd)] + [(a, bpos(m)) for m in range(1, nz)] + [sib]
    barrier = pltpu.get_barrier_semaphore()
    for peer in peers:
        pl.semaphore_signal(barrier, inc=1, device_id=peer, device_id_type=MESH)

    def small_sum(buf):
        slots = n.gr
        hops = (group(1, lambda i: (buf, slots.at[0], sib)),
                group(nd - 1, lambda i: (buf, slots.at[1 + i], (apos(i + 1), b))),
                group(nz - 1, lambda i: (buf, slots.at[nd + i], (a, bpos(i + 1)))))
        phases = []
        first = 0
        for g in hops:
            def finish(g=g, first=first):
                recv(g)
                sent(g)
                total = buf[...]
                for i in range(g.count):
                    total = total + slots[first + i]
                buf[...] = total

            phases.append((functools.partial(start, g), finish))
            first += g.count
        return phases

    pl.semaphore_wait(barrier, len(peers))
    n.gs[a, b] = low(n.gains[...]).astype(F32)
    gains_z = Gather(lambda bi: n.gs.at[a, bi])
    gains_sib = [sib_group(n.gs.at[a, bpos(m)], n.gs.at[a, bpos(m)]) for m in range(nz)]
    gains_dp = dp_group(lambda k: n.gs.at[a], lambda k: n.gs.at[a])
    gains_z.start()
    start(gains_sib[0])
    arrived(in_cross)
    for i in range(4):
        n.wx[i, a, b] = low(n.z1[i * rows:(i + 1) * rows])
    in_dn2 = [load(n.gd_, n.z1)]

    def wx_at(ai, bi):
        return n.wx.at[:, ai, bi]

    cross_z = Gather(lambda bi: n.wx.at[:, a, bi])
    cross_dp = []
    for m in range(nz):
        def direct(h, m=m):
            at = n.wx.at[2 * h:2 * h + 2, a, bpos(m)]
            return at, at

        def relayed(h, m=m):
            at = n.wx.at[2 * h:2 * h + 2, apos(1 + h), bpos(m)]
            return at, at

        cross_dp.append(Share(direct, direct, relayed))
    cross_sib = [[sib_group(wx_at(apos(k), bpos(m)), wx_at(apos(k), bpos(m))) for m in range(nz)]
                 for k in range(nd)]
    cross_z.start()
    cross_dp[0].start()
    start(cross_sib[0][0])

    su1, su2 = n.xw.at[3, 0], n.xw.at[3, 1]

    def put_up(staged, sends, up):
        for j in range(nd):
            sends[j] = low(staged[j * rows:(j + 1) * rows])
        up[a, b] = sends[a]

    def put_dn(staged, dn):
        dn[lax.div(b * nd, jnp.int32(nf)), pl.ds(lax.rem(b * nd, jnp.int32(nf)), nd)] = (
            low(staged[...]).reshape(nd, rows, width))

    def dn_at(dn, bi):
        return dn.at[lax.div(bi * nd, jnp.int32(nf)), pl.ds(lax.rem(bi * nd, jnp.int32(nf)), nd)]

    arrived(in_up1)
    put_up(n.z2, su1, n.up1)
    up1_dp = dp_group(lambda k: su1.at[apos(k)], lambda k: n.up1.at[a, b])
    start(up1_dp)
    arrived(in_dn1)
    put_dn(n.z3, n.dn1)
    arrived(in_self)
    for i in range(3):
        for j in range(nd):
            n.sqs[j, i] = low(n.ga[i * rows:(i + 1) * rows, j * cols:(j + 1) * cols])
    for i in range(3):
        n.sq[i, a, b] = n.sqs[a, i]
    n.so[b] = low(n.ga[3 * rows:4 * rows])
    arrived(in_up2)
    put_up(n.own, su2, n.up2)
    arrived(in_dn2)
    put_dn(n.z1, n.dn2)
    arrived(in_cot)
    act_rows = (nz, rows, width)

    def up_z(up):
        return Gather(lambda bi: up.at[:, bi])

    def up_sib(up):
        return [sib_group(up.at[:, bpos(m)], up.at[:, bpos(m)]) for m in range(nz)]

    def dn_z(dn):
        return Gather(lambda bi: dn_at(dn, bi))

    def dn_sib(dn):
        return [sib_group(dn_at(dn, bpos(m)), dn_at(dn, bpos(m))) for m in range(nz)]

    gain = [n.gn.at[i:i + 1] for i in range(5)]

    arrived(in_lat)
    arrived(in_x)
    gains_z.relay()
    for m in (1, 2, 3):
        gains_z.recv(m)
        start(gains_sib[m])
    for g in gains_sib:
        recv(g)
    start(gains_dp)
    cross_z.relay()
    for m in (1, 2, 3):
        cross_z.recv(m)
        cross_dp[m].start()
        start(cross_sib[0][m])
        if m == 1:
            cross_dp[0].relay()
    up1_z, up1_sib, dn1_z, dn1_sib = up_z(n.up1), up_sib(n.up1), dn_z(n.dn1), dn_sib(n.dn1)
    recv(up1_dp)
    up1_z.start()
    dn1_z.start()
    cross_dp[1].relay()
    cross_dp[2].relay()
    recv(gains_dp)
    per = 128 // rows
    for j in range(width // 128):
        tile = 0.0
        for i in range(j * per, (j + 1) * per):
            tile = tile + n.gs[i // nf, i % nf]
        n.gn[:, j * 128:(j + 1) * 128] = tile

    block = lat

    def token_norm(i, _):
        at = pl.ds(pl.multiple_of(i * block, block), block)
        n.xn[at] = norm(n.xn[at].astype(F32), gain[1][...])
        return 0

    n.an[...] = norm(n.lt[...].astype(F32), gain[0][...])
    lax.fori_loop(0, span // block, token_norm, 0)

    cross_dp[3].relay()
    for m in range(nz):
        for k in range(1, nd):
            cross_dp[m].recv(k)
            start(cross_sib[k][m])
        if m == 1:
            up1_z.relay()
    up2_dp = dp_group(lambda k: su2.at[apos(k)], lambda k: n.up2.at[a, b])
    sq_dp = dp_group(lambda k: n.sqs.at[apos(k)], lambda k: n.sq.at[:, a, b])
    start(sq_dp)
    start(up2_dp)
    for k in range(nd):
        for m in range(nz):
            recv(cross_sib[k][m])

    def rows_of(ref, k):
        return ref[k].reshape(lat, width)

    def spread(buf, value, after=None):
        buf[0] = value.reshape(act_rows)
        g = Share(lambda h: (buf.at[0, halves[h]], buf.at[1, halves[h]]),
                  lambda h: (buf.at[0, halves[h]], buf.at[2, halves[h]]),
                  lambda h: (buf.at[1 + h, halves[h]], buf.at[3, halves[h]]), after)
        g.start()
        return g

    taken[1] = 0
    cot_dp = spread(n.gg, n.gb[...])
    def wcols(i, at):
        return n.wx[i, :, :, :, at].reshape(width, at.size)

    def full(ref):
        return ref[...].reshape(width, width)

    n.qq[...] = low(dot(n.an[...], n.wx[0].reshape(width, width), NN))
    wide = 256

    def token_proj(i, _):
        at = pl.ds(pl.multiple_of(i * wide, wide), wide)
        n.kk[:, at] = low(dot(n.xn[...], wcols(1, at), NN))
        n.vv[:, at] = low(dot(n.xn[...], wcols(2, at), NN))
        return 0

    lax.fori_loop(0, width // wide, token_proj, 0)
    dn1_z.relay()
    valid = lax.broadcasted_iota(jnp.int32, (lat, span), 1) < n.frames[0] * FRAME_TOK

    def softmax(scores):
        expo = jnp.exp(scores - jnp.max(scores, axis=-1, keepdims=True))
        return low(expo / jnp.sum(expo, axis=-1, keepdims=True))

    def cross_head(h, _):
        at = pl.ds(pl.multiple_of(h * hd, hd), hd)
        scores = jnp.where(valid, dot(n.qq[:, at], n.kk[:, at], NT) * scale, NEG)
        probs = softmax(scores)
        n.pp[h] = probs
        n.cc[:, at] = low(dot(probs, n.vv[:, at], NN))
        return 0

    lax.fori_loop(0, HEADS, cross_head, 0, unroll=2)
    recv(sq_dp)
    sq_z = Gather(lambda bi: n.sq.at[:, :, bi])
    so_z = Gather(lambda bi: n.so.at[bi])
    sq_sib = [sib_group(n.sq.at[:, :, bpos(m)], n.sq.at[:, :, bpos(m)]) for m in range(nz)]
    so_sib = [sib_group(n.so.at[bpos(m)], n.so.at[bpos(m)]) for m in range(nz)]
    sq_z.start()
    so_z.start()
    cot_dp.relay()
    z1 = n.lt[...].astype(F32) + dot(n.cc[...], n.wx[3].reshape(width, width), NN)
    n.z1[...] = z1

    acts = []

    def collect(make, gathered, sends, slots, previous, aside=None):
        if previous is not None:
            sent(previous)
        back = Merge(lambda k, h: sends.at[k - 1, halves[h]], slots, acts[0] if acts else None)
        acts.append(back)
        back.gathered = gathered
        n.own[...] = make(0)
        gathered.relay()
        if aside is not None:
            aside()

        def step(i, _):
            gathered.recv(i + 1)
            sends[i] = low(make(i + 1)).reshape(act_rows)
            back.push(i + 1)
            return 0

        lax.fori_loop(0, nd - 1, step, 0)
        return back

    def gather_sum(back, slots):
        if back.gathered is not None:
            sent(back.gathered)
        return back.total(n.own[...])

    def feed_hidden(ag, u, d, up):
        def make(k):
            value, slope = gelu_both(dot(rows_of(ag, k), full(up), NN))
            hidden = low(value)
            u[k] = hidden.reshape(act_rows)
            d[k] = low(slope).reshape(act_rows)
            return hidden

        return make

    def feed_make(ag, u, d, up, dn):
        hide = feed_hidden(ag, u, d, up)

        def make(k):
            return dot(hide(k), full(dn), NN)

        return make

    ag1_dp = spread(n.ag1, norm(z1, gain[2][...]))
    recv(up2_dp)
    up2_z, up2_sib, dn2_z, dn2_sib = up_z(n.up2), up_sib(n.up2), dn_z(n.dn2), dn_sib(n.dn2)
    for m in range(nz):
        for g, line in ((up1_z, up1_sib), (dn1_z, dn1_sib)):
            if m > 0:
                g.recv(m)
            start(line[m])
    for m in range(nz):
        recv(up1_sib[m])
        recv(dn1_sib[m])

    def later_weights():
        sq_z.relay()
        so_z.relay()
        up2_z.start()

    out1 = collect(feed_make(n.ag1, n.u1, n.d1, n.up1, n.dn1), ag1_dp, n.sa, n.ra, None, later_weights)
    out1.combine()
    for g in ([cross_z, gains_z, gains_dp, up1_z, dn1_z] + gains_sib + cross_dp
              + [g for line in cross_sib for g in line]):
        sent(g)
    z2 = n.z1[...] + gather_sum(out1, n.ra)
    n.z2[...] = z2

    bg_dp = spread(n.bg, norm(z2, gain[3][...]), ag1_dp)
    for m in range(nz):
        for g, line in ((sq_z, sq_sib), (so_z, so_sib)):
            if m > 0:
                g.recv(m)
            start(line[m])
    up2_z.relay()
    dn2_z.start()
    for m in range(nz):
        recv(sq_sib[m])
        recv(so_sib[m])

    def self_make(k):
        normed = rows_of(n.bg, k)
        for i, ref in enumerate((n.q2, n.k2, n.v2)):
            ref[k] = low(dot(normed, n.sq[i].reshape(width, cols), NN))
        for h in range(local_heads):
            at = slice(h * hd, (h + 1) * hd)
            probs = softmax(dot(n.q2[k, :, at], n.k2[k, :, at], NT) * scale)
            n.p2[k, h] = probs
            n.c2[k, :, at] = low(dot(probs, n.v2[k, :, at], NN))
        return dot(n.c2[k], n.so[...].reshape(cols, width), NN)

    out_self = collect(self_make, bg_dp, n.sa, n.rb, out1)
    out_self.combine()
    dn2_z.relay()
    z3 = n.z2[...] + gather_sum(out_self, n.rb)
    n.z3[...] = z3

    ag2_dp = spread(n.ag2, norm(z3, gain[4][...]), ag1_dp)
    for m in range(nz):
        if m > 0:
            up2_z.recv(m)
        start(up2_sib[m])
    for m in range(nz):
        recv(up2_sib[m])

    sc, rc = n.sc, n.rb

    def feed_back(ks, g, d, up, dn, sends):
        def rows_together(ref):
            parts = [rows_of(ref, k) for k in ks]
            return parts[0] if len(parts) == 1 else jnp.concatenate(parts, axis=0)

        step = width // nd
        left = rows_together(g)
        for i in range(nd):
            at = slice(i * step, (i + 1) * step)
            grad = dot(left, dn[i].reshape(step, width), NT)
            for j, k in enumerate(ks):
                slope = d[k, :, :, at].reshape(lat, step).astype(F32)
                d[k, :, :, at] = low(slope * grad[j * lat:(j + 1) * lat]).reshape(nz, rows, step)
        left = rows_together(d)
        for i in range(nd):
            at = slice(i * step, (i + 1) * step)
            value = dot(left, up[i].reshape(step, width), NT)
            for j, k in enumerate(ks):
                part = value[j * lat:(j + 1) * lat]
                if k == 0:
                    n.own[:, at] = part
                else:
                    sends[k - 1, :, :, at] = low(part).reshape(nz, rows, step)

    hide2 = feed_hidden(n.ag2, n.u2, n.d2, n.up2)
    final_dp = Merge(lambda k, h: sc.at[k - 1, halves[h]], rc)
    sent(up1_dp)
    sent(up2_dp)
    hide2(0)
    ag2_dp.relay()

    def hide_step(i, _):
        ag2_dp.recv(i + 1)
        hide2(i + 1)
        return 0

    lax.fori_loop(0, nd - 1, hide_step, 0)

    def put_grad(value, ref, first):
        for i in range(value.shape[0] // rows):
            ai, bi = divmod(first + i, nf)
            zi, ci = divmod(bi, 2)
            ref[ci, zi, ai] = value[i * rows:(i + 1) * rows]

    def put_down(value, ref, first):
        for i in range(value.shape[0] // rows):
            bi, ai = divmod(first + i, nd)
            zi, ci = divmod(bi, 2)
            ref[ci, zi, ai] = value[i * rows:(i + 1) * rows]

    tall = 256

    def every_row(ref, at=slice(None)):
        value = ref[:, :, :, at]
        return value.reshape(value.shape[0] * value.shape[1] * value.shape[2], value.shape[3])

    def up_grad(ag, d):
        for i in range(width // tall):
            at = slice(i * tall, (i + 1) * tall)
            put_grad(low(dot(every_row(ag, at), every_row(d), TN)), n.GU, i * tall // rows)

    def down_grad(u, g):
        for i in range(width // tall):
            at = slice(i * tall, (i + 1) * tall)
            put_down(low(dot(every_row(u, at), every_row(g), TN)), n.GD, i * tall // rows)

    def core_sum(grad, other):
        for i in range(nz):
            grad[c, i] = low(grad[c, i].astype(F32) + other[i].astype(F32))

    def sib_grads(grad, other):
        g = sib_group(grad.at[1 - c], other)
        start(g)
        return g

    def z_grads(grad, slots, after):
        g = Reduce(lambda zi: grad.at[c, zi], slots, after)
        g.start()
        return g

    for k in range(1, nd):
        cot_dp.recv(k)
    down_grad(n.u2, n.gg)
    gd2_sib = sib_grads(n.GD, n.SD)
    for m in range(nz):
        if m > 0:
            dn2_z.recv(m)
        start(dn2_sib[m])
    for m in range(nz):
        recv(dn2_sib[m])
    sent(out_self)
    dm2 = Merge(lambda k, h: n.sa.at[k - 1, halves[h]], n.ra, out1)
    dm2.gathered = None
    recv(gd2_sib)
    core_sum(n.GD, n.SD)
    gd2_z = z_grads(n.GD, n.ZD, cross_z)
    feed_back((3, 0), n.gg, n.d2, n.up2, n.dn2, n.sa)
    dm2.push(3)
    feed_back((1, 2), n.gg, n.d2, n.up2, n.dn2, n.sa)
    dm2.push(1)
    dm2.push(2)
    sent(ag2_dp)
    up_grad(n.ag2, n.d2)
    gu2_sib = sib_grads(n.GU, n.SU)
    dm2.combine()
    n.ob[...] = low(dot(rows_of(n.u2, 0), full(n.dn2), NN))

    def out_step(i, _):
        sc[i] = low(dot(rows_of(n.u2, i + 1), full(n.dn2), NN)).reshape(act_rows)
        return 0

    lax.fori_loop(0, nd - 1, out_step, 0)
    recv(gu2_sib)
    core_sum(n.GU, n.SU)
    gu2_z = z_grads(n.GU, n.ZU, gains_z)

    def set_gain(i, value):
        n.dg[i:i + 1] = value

    n.dg[...] = jnp.zeros_like(n.dg)
    back, gain_part = norm_back(n.z3[...], gain[4][...], gather_sum(dm2, n.ra))
    set_gain(4, gain_part)
    ga = rows_of(n.gg, 0).astype(F32) + back
    n.ga[...] = ga

    sent(cot_dp)

    gs_dp = spread(n.ggs, low(ga), ag1_dp)
    gd2_z.combine()

    def attend_back(q, k, v, probs, grad):
        grad_probs = dot(grad, v, NT)
        wide_probs = probs.astype(F32)
        inner = jnp.sum(wide_probs * grad_probs, axis=-1, keepdims=True)
        scores = low(wide_probs * (grad_probs - inner))
        return (low(dot(scores, k, NN) * scale), low(dot(scores, q, TN) * scale),
                low(dot(probs, grad, TN)))

    def self_back(k):
        grad = low(dot(rows_of(n.ggs, k), n.so[...].reshape(cols, width), NT))
        for h in range(local_heads):
            at = slice(h * hd, (h + 1) * hd)
            dq, dk, dv = attend_back(n.q2[k, :, at], n.k2[k, :, at], n.v2[k, :, at],
                                     n.p2[k, h], grad[:, at])
            n.q2[k, :, at] = dq
            n.k2[k, :, at] = dk
            n.v2[k, :, at] = dv
        total = 0.0
        for i, ref in enumerate((n.q2, n.k2, n.v2)):
            total = total + dot(ref[k], n.sq[i].reshape(width, cols), NT)
        return total

    db = collect(self_back, gs_dp, n.sa, n.rb, dm2)
    for i, ref in enumerate((n.q2, n.k2, n.v2)):
        value = low(dot(every_row(n.bg), ref[...].reshape(nd * lat, cols), TN))
        for j in range(width // rows):
            ai, bi = divmod(j, nf)
            zi, ci = divmod(bi, 2)
            n.GQ[ci, zi, ai, i] = value[j * rows:(j + 1) * rows]
    value = low(dot(n.c2[...].reshape(nd * lat, cols), every_row(n.ggs), TN))
    for bi in range(nf):
        zi, ci = divmod(bi, 2)
        n.GO[ci, zi] = value[bi * rows:(bi + 1) * rows]
    gq_sib = sib_grads(n.GQ, n.SQ)
    go_sib = sib_grads(n.GO, n.SO)
    db.combine()
    gu2_z.combine()
    recv(gq_sib)
    core_sum(n.GQ, n.SQ)
    gq_z = z_grads(n.GQ, n.ZQ, up1_z)
    recv(go_sib)
    core_sum(n.GO, n.SO)
    go_z = z_grads(n.GO, n.ZO, dn1_z)
    back, gain_part = norm_back(n.z2[...], gain[3][...], gather_sum(db, n.rb))
    set_gain(3, gain_part)
    ga = n.ga[...] + back
    n.ga[...] = ga

    outs = []
    gf_dp = spread(n.gg, low(ga), ag1_dp)
    sent(db)
    dm1 = Merge(lambda k, h: n.sa.at[k - 1, halves[h]], n.ra, out1)
    dm1.gathered = gf_dp
    feed_back((0,), n.gg, n.d1, n.up1, n.dn1, n.sa)
    gf_dp.relay()
    gf_dp.recv(1)
    gf_dp.recv(2)
    feed_back((1, 2), n.gg, n.d1, n.up1, n.dn1, n.sa)
    dm1.push(1)
    dm1.push(2)
    gf_dp.recv(3)
    feed_back((3,), n.gg, n.d1, n.up1, n.dn1, n.sa)
    dm1.push(3)

    def out_rows(value, staged, target):
        staged[...] = value.reshape(staged.shape)
        return load(staged, target)

    gq_z.combine()
    go_z.combine()
    total = gd2_z.total()
    down_out = out_rows(total, n.z2, n.ogd)
    total = gu2_z.total()

    def column_grads(total, sends, slots):
        sends[...] = low(total)
        return dp_group(lambda k: sends.at[apos(k)], lambda k: slots.at[k - 1])

    su3, su4 = n.d2.at[0], n.d2.at[1]
    cu2_dp = column_grads(total, su3, n.CU2)
    for g in (gu2_sib, gd2_sib, gu2_z, gd2_z):
        sent(g)
    down_grad(n.u1, n.gg)
    gd1_sib = sib_grads(n.GD, n.SD)
    dm1.combine()
    zu1, zd1 = n.ag2, n.u2
    for g in (up2_z, dn2_z, sq_z, so_z):
        sent(g)
    recv(gd1_sib)
    core_sum(n.GD, n.SD)
    gd1_z = z_grads(n.GD, zd1, up2_z)
    up_grad(n.ag1, n.d1)
    gu1_sib = sib_grads(n.GU, n.SU)
    recv(gu1_sib)
    core_sum(n.GU, n.SU)
    gu1_z = z_grads(n.GU, zu1, dn2_z)
    back, gain_part = norm_back(n.z1[...], gain[2][...], gather_sum(dm1, n.ra))
    set_gain(2, gain_part)
    ga = n.ga[...] + back
    n.ga[...] = ga

    n.gb[...] = low(ga)
    mats = (n.up2, n.dn2, n.up1, n.dn1)
    others = (n.u1, n.d1, n.ag1, n.bg)

    def put_cross(value, ref, first):
        for i in range(value.shape[0] // rows):
            ai, bi = divmod(first + i, nf)
            zi, ci = divmod(bi, 2)
            ref[ai, ci * nz + zi] = value[i * rows:(i + 1) * rows]

    def cross_grad(left, right, which):
        short = tall // 2
        for i in range(width // short):
            put_cross(low(dot(left[:, i * short:(i + 1) * short], right, TN)), mats[which],
                      i * short // rows)

    def half(ref, ci):
        return ref.at[:, pl.ds(ci * nz, nz)]

    for g in up1_sib + dn1_sib + up2_sib + dn2_sib:
        sent(g)
    for k in (3, 1, 2):
        final_dp.push(k)
    cross_grad(n.cc, n.gb[...], 3)
    core_dp = [group(1, lambda i, w=w: (half(mats[w], 1 - c), others[w], sib)) for w in range(4)]
    start(core_dp[3])
    n.dc[...] = low(dot(n.gb[...], n.wx[3].reshape(width, width), NT))
    own_half = pl.ds(c * nz, nz)
    cross_xy, cross_back_z = {}, {}

    def over_dp(w):
        recv(core_dp[w])
        for ai in range(nd):
            mats[w][ai, own_half] = low(mats[w][ai, own_half].astype(F32) + others[w][ai].astype(F32))
        cross_xy[w] = Merge(lambda k, h, w=w: mats[w].at[apos(k), pl.ds(c * nz + h * mid, mid)], n.xw.at[w],
                            cross_dp[w])
        for k in (3, 1, 2):
            cross_xy[w].push(k)

    def z_start(w, slots, after):
        mats[w][a, own_half] = low(cross_xy[w].total(mats[w][a, own_half].astype(F32)))
        cross_back_z[w] = Reduce(lambda zi: mats[w].at[a, c * nz + zi], slots, after)
        cross_back_z[w].start()

    over_dp(3)

    def cross_back(h, _):
        at = pl.ds(pl.multiple_of(h * hd, hd), hd)
        dq, dk, dv = attend_back(n.qq[:, at], n.kk[:, at], n.vv[:, at], n.pp[h], n.dc[:, at])
        n.qq[:, at] = dq
        n.kk[:, at] = dk
        n.vv[:, at] = dv
        return 0

    lax.fori_loop(0, HEADS, cross_back, 0, unroll=2)
    again = [load(n.inputs.at[0, pl.ds(i * block, block)], n.pp.at[i]) for i in range(span // block)]
    final_dp.combine()
    cross_xy[3].combine()
    cross_grad(n.xn, n.vv[...], 2)
    start(core_dp[2])
    cross_grad(n.xn, n.kk[...], 1)
    start(core_dp[1])
    over_dp(2)
    cross_grad(n.an, n.qq[...], 0)
    start(core_dp[0])
    over_dp(1)
    gd1_z.combine()
    cross_xy[2].combine()
    over_dp(0)
    start(cu2_dp)
    gu1_z.combine()

    back, gain_part = norm_back(n.lt[...].astype(F32), gain[0][...],
                                dot(n.qq[...], n.wx[0].reshape(width, width), NT))
    set_gain(0, gain_part)
    n.gb[...] = low(n.ga[...] + back)
    outs.append(load(n.gb, n.glat.at[0]))
    arrived(again)

    def token_back(i, total):
        at = pl.ds(pl.multiple_of(i * 2 * block, 2 * block), 2 * block)
        step = width // nd
        for j in range(nd):
            to = slice(j * step, (j + 1) * step)
            grad = (dot(n.kk[at], n.wx[1, j].reshape(step, width), NT)
                    + dot(n.vv[at], n.wx[2, j].reshape(step, width), NT))
            n.z1[:, to] = grad[:block]
            n.own[:, to] = grad[block:]
        for j, ref in enumerate((n.z1, n.own)):
            back, gain_part = norm_back(n.pp[2 * i + j].astype(F32), gain[1][...], ref[...])
            n.pp[2 * i + j] = low(back)
            total = total + gain_part
        return total

    steps = span // (2 * block)
    total = lax.fori_loop(0, steps // 4, token_back, jnp.zeros((1, width), F32))
    cross_xy[1].combine()
    z_start(3, n.d2.at[2], sq_z)
    total = lax.fori_loop(steps // 4, steps // 2, token_back, total)
    cross_xy[0].combine()
    z_start(2, n.d2.at[3], so_z)
    cross_back_z[3].combine()
    set_gain(1, lax.fori_loop(steps // 2, steps, token_back, total))
    for i in range(span // block):
        outs.append(load(n.pp.at[i], n.ginp.at[0, pl.ds(i * block, block)]))
    gain_hops = small_sum(n.dg)
    gain_hops[0][0]()

    total = gd1_z.total()
    outs.append(out_rows(total, n.z1, n.ofd))
    cu1_dp = column_grads(gu1_z.total(), su4, n.CU1)
    start(cu1_dp)
    gain_hops[0][1]()
    gain_hops[1][0]()
    z_start(1, n.ZU.at[1], gd2_z)
    cross_back_z[2].combine()
    total = go_z.total()
    down_out.wait()
    n.z2[0:rows] = total
    outs.append(load(n.z2.at[0:rows], n.oso))
    total = gq_z.total()
    sq_send = n.sqs
    sent(sq_dp)
    sq_send[...] = low(total)
    cq_dp = dp_group(lambda k: sq_send.at[apos(k)], lambda k: n.CQ.at[k - 1])
    start(cq_dp)
    z_start(0, n.ZU.at[0], gu2_z)
    cross_back_z[1].combine()
    gain_hops[1][1]()
    gain_hops[2][0]()
    cross_back_z[0].combine()
    n.dc[...] = low(final_dp.total(n.z3[...] + n.ob[...].astype(F32)))
    outs.append(load(n.dc, n.out.at[0]))

    def put_columns(g, own, slots, staged, target):
        staged[0:rows] = own
        copies = [load(staged.at[0:rows], target.at[:, pl.ds(pl.multiple_of(a * width, width), width)])]
        for i in range(nd - 1):
            g(i).wait_recv()
            staged[(i + 1) * rows:(i + 2) * rows] = slots[i].astype(F32)
            copies.append(load(staged.at[(i + 1) * rows:(i + 2) * rows],
                               target.at[:, pl.ds(pl.multiple_of(apos(i + 1) * width, width), width)]))
        return copies

    outs += put_columns(cu2_dp, su3[a].astype(F32), n.CU2, n.z3, n.ogu)
    outs += put_columns(cu1_dp, su4[a].astype(F32), n.CU1, n.own, n.ofu)
    recv(cq_dp)
    for i, target in enumerate((n.osq, n.osk, n.osv)):
        at = slice((i + 1) * rows, (i + 2) * rows)
        n.z2[at, pl.ds(pl.multiple_of(a * cols, cols), cols)] = sq_send[a, i].astype(F32)
        for k in range(1, nd):
            n.z2[at, pl.ds(pl.multiple_of(apos(k) * cols, cols), cols)] = n.CQ[k - 1, i].astype(F32)
        outs.append(load(n.z2.at[at], target))
    for w, target in ((3, n.oco), (2, n.ocv), (1, n.ock), (0, n.ocq)):
        total = cross_back_z[w].total()
        at = slice(w * rows, (w + 1) * rows)
        n.ga[at] = total
        outs.append(load(n.ga.at[at], target))
    gain_hops[2][1]()
    outs.append(load(n.dg, n.ggain))
    for g in ([final_dp, dm1, gq_sib, go_sib, gq_z, go_z, cu1_dp, cu2_dp, cq_dp, gu1_sib, gd1_sib, gu1_z, gd1_z]
              + sq_sib + so_sib + core_dp + list(cross_xy.values()) + list(cross_back_z.values())):
        sent(g)
    arrived(outs)


def layer_norm(value, gain):
    center = value - jnp.mean(value, axis=-1, keepdims=True)
    spread = jnp.mean(center * center, axis=-1, keepdims=True)
    return center * lax.rsqrt(spread + EPS) * gain


def activate(value):
    return jax.nn.gelu(value, approximate=True)


def product(left, right):
    return jnp.dot(left, right, preferred_element_type=jnp.float32)


def weight_grad(left, right):
    return lax.dot_general(
        left, right, (((0,), (0,)), ((), ())), preferred_element_type=jnp.float32
    )


def back_product(grad, weight):
    return lax.dot_general(
        grad, weight, (((1,), (1,)), ((), ())), preferred_element_type=jnp.float32
    )


def plain_norm_back(value, gain, grad):
    _, pull = jax.vjp(layer_norm, value, gain)
    return pull(grad)


def activate_back(value, grad):
    _, pull = jax.vjp(activate, value)
    return pull(grad)[0]


def split_heads(value, groups):
    return value.reshape(groups, -1, HEADS, value.shape[-1] // HEADS)


def merge_heads(value):
    return value.reshape(-1, value.shape[2] * value.shape[3])


def masked_scores(query, key, valid):
    scale = query.shape[-1] ** (-0.5)
    scores = jnp.einsum("gqhd,gkhd->ghqk", query, key, preferred_element_type=jnp.float32) * scale
    return jnp.where(valid[:, None, None, :], scores, NEG)


def attend_forward(query, key, value, valid):
    scores = masked_scores(query, key, valid)
    top = jnp.max(scores, axis=-1, keepdims=True)
    expo = jnp.exp(scores - top)
    denom = jnp.sum(expo, axis=-1, keepdims=True)
    weights = (expo / denom).astype(jnp.bfloat16)
    mixed = jnp.einsum("ghqk,gkhd->gqhd", weights, value, preferred_element_type=jnp.float32)
    return (merge_heads(mixed).astype(jnp.bfloat16), top + jnp.log(denom))


def plain_attend_back(query, key, value, valid, logsum, grad_mixed):
    scale = query.shape[-1] ** (-0.5)
    probs = jnp.exp(masked_scores(query, key, valid) - logsum)
    grad_probs = jnp.einsum(
        "gqhd,gkhd->ghqk", grad_mixed, value, preferred_element_type=jnp.float32
    )
    inner = jnp.sum(probs * grad_probs, axis=-1, keepdims=True)
    grad_scores = (probs * (grad_probs - inner)).astype(jnp.bfloat16)
    weights = probs.astype(jnp.bfloat16)
    grad_query = (
        jnp.einsum("ghqk,gkhd->gqhd", grad_scores, key, preferred_element_type=jnp.float32) * scale
    )
    grad_key = (
        jnp.einsum("ghqk,gqhd->gkhd", grad_scores, query, preferred_element_type=jnp.float32)
        * scale
    )
    grad_value = jnp.einsum(
        "ghqk,gqhd->gkhd", weights, grad_mixed, preferred_element_type=jnp.float32
    )
    return (
        merge_heads(grad_query).astype(jnp.bfloat16),
        merge_heads(grad_key).astype(jnp.bfloat16),
        merge_heads(grad_value).astype(jnp.bfloat16),
    )


def feed_forward(resid, gain, w_up, w_down):
    normed = layer_norm(resid, gain.astype(jnp.float32)).astype(jnp.bfloat16)
    before = product(normed, w_up)
    hidden = activate(before).astype(jnp.bfloat16)
    return (resid + product(hidden, w_down), (normed, before, hidden))


def plain_feed_back(grad, resid, gain, saved, w_up, w_down):
    normed, before, hidden = saved
    grad_low = grad.astype(jnp.bfloat16)
    grad_down = weight_grad(hidden, grad_low)
    grad_before = activate_back(before, back_product(grad_low, w_down)).astype(jnp.bfloat16)
    grad_up = weight_grad(normed, grad_before)
    grad_resid, grad_gain = plain_norm_back(
        resid, gain.astype(jnp.float32), back_product(grad_before, w_up)
    )
    return (grad + grad_resid, grad_gain, grad_up, grad_down)


def project_back(grad, mixed, w_out, query, key, value, valid, logsum, groups):
    grad_low = grad.astype(jnp.bfloat16)
    grad_out = weight_grad(mixed, grad_low)
    grad_mixed = back_product(grad_low, w_out).astype(jnp.bfloat16)
    grad_query, grad_key, grad_value = plain_attend_back(
        split_heads(query, groups),
        split_heads(key, groups),
        split_heads(value, groups),
        valid,
        logsum,
        split_heads(grad_mixed, groups),
    )
    return (grad_out, grad_query, grad_key, grad_value)


def plain_layer(
    latents,
    inputs,
    frames,
    norm_latent,
    norm_input,
    cross_query,
    cross_key,
    cross_value,
    cross_output,
    norm_first,
    first_up,
    first_down,
    norm_self,
    self_query,
    self_key,
    self_value,
    self_output,
    norm_second,
    second_up,
    second_down,
    cotangent,
    mesh_size,
):
    groups, lat_rows, width = latents.shape
    span = inputs.shape[1]
    hidden_width = first_up.shape[1]
    low_type = jnp.bfloat16
    parts = mesh_size
    gains = (norm_latent, norm_input, norm_first, norm_self, norm_second)
    mats = (cross_query, cross_key, cross_value, cross_output, first_up, first_down,
            self_query, self_key, self_value, self_output, second_up, second_down)
    blocks = []
    for mat in mats:
        for start in range(0, mat.shape[1], width):
            blocks.append(mat[:, start:start + width])
    gain_row = jnp.concatenate([jnp.concatenate(gains), jnp.zeros((width - 5 * gains[0].shape[0],), jnp.float32)])
    gain_rows = jnp.concatenate([gain_row[None], jnp.zeros((15, width), jnp.float32)])
    packed = jnp.concatenate([gain_rows] + blocks).astype(low_type)
    whole = lax.all_gather(packed, ("dp", "fsdp"), axis=0, tiled=False)
    per = gains[0].shape[0]
    gathered_gains = [whole[:, 0, i * per:(i + 1) * per].reshape(width) for i in range(5)]
    gain_lat, gain_inp, gain_first, gain_self, gain_second = gathered_gains
    at = 16
    full = []
    for mat in mats:
        columns = []
        for start in range(0, mat.shape[1], width):
            columns.append(whole[:, at:at + mat.shape[0]].reshape(parts * mat.shape[0], width))
            at += mat.shape[0]
        full.append(columns[0] if len(columns) == 1 else jnp.concatenate(columns, axis=1))
    w_query, w_key, w_value, w_out, up_one, down_one, s_query, s_key, s_value, s_out, up_two, down_two = full
    positions = jnp.arange(span, dtype=jnp.int32)
    valid = positions[None, :] < (frames * FRAME_TOK)[:, None]
    every = jnp.ones((groups, lat_rows), dtype=bool)
    latent_rows = latents.reshape(groups * lat_rows, width).astype(jnp.float32)
    input_rows = inputs.reshape(groups * span, width).astype(jnp.float32)
    normed_lat = layer_norm(latent_rows, gain_lat.astype(jnp.float32)).astype(low_type)
    normed_inp = layer_norm(input_rows, gain_inp.astype(jnp.float32)).astype(low_type)
    query_one = product(normed_lat, w_query).astype(low_type)
    key_one = product(normed_inp, w_key).astype(low_type)
    value_one = product(normed_inp, w_value).astype(low_type)
    mixed_one, logsum_one = attend_forward(
        split_heads(query_one, groups),
        split_heads(key_one, groups),
        split_heads(value_one, groups),
        valid,
    )
    first_resid = latent_rows + product(mixed_one, w_out)
    second_resid, saved_one = feed_forward(first_resid, gain_first, up_one, down_one)
    normed_self = layer_norm(second_resid, gain_self.astype(jnp.float32)).astype(low_type)
    query_two = product(normed_self, s_query).astype(low_type)
    key_two = product(normed_self, s_key).astype(low_type)
    value_two = product(normed_self, s_value).astype(low_type)
    mixed_two, logsum_two = attend_forward(
        split_heads(query_two, groups),
        split_heads(key_two, groups),
        split_heads(value_two, groups),
        every,
    )
    third_resid = second_resid + product(mixed_two, s_out)
    final_resid, saved_two = feed_forward(third_resid, gain_second, up_two, down_two)
    result = final_resid.reshape(groups, lat_rows, width).astype(low_type)
    grad_final = cotangent.reshape(groups * lat_rows, width).astype(jnp.float32)
    grad_third, grad_gain_second, grad_up_two, grad_down_two = plain_feed_back(
        grad_final, third_resid, gain_second, saved_two, up_two, down_two
    )
    grad_s_out, grad_query_two, grad_key_two, grad_value_two = project_back(
        grad_third, mixed_two, s_out, query_two, key_two, value_two, every, logsum_two, groups
    )
    grad_s_query = weight_grad(normed_self, grad_query_two)
    grad_s_key = weight_grad(normed_self, grad_key_two)
    grad_s_value = weight_grad(normed_self, grad_value_two)
    grad_normed_self = (
        back_product(grad_query_two, s_query)
        + back_product(grad_key_two, s_key)
        + back_product(grad_value_two, s_value)
    )
    grad_from_self, grad_gain_self = plain_norm_back(
        second_resid, gain_self.astype(jnp.float32), grad_normed_self
    )
    grad_second = grad_third + grad_from_self
    grad_first, grad_gain_first, grad_up_one, grad_down_one = plain_feed_back(
        grad_second, first_resid, gain_first, saved_one, up_one, down_one
    )
    grad_w_out, grad_query_one, grad_key_one, grad_value_one = project_back(
        grad_first, mixed_one, w_out, query_one, key_one, value_one, valid, logsum_one, groups
    )
    grad_w_query = weight_grad(normed_lat, grad_query_one)
    grad_w_key = weight_grad(normed_inp, grad_key_one)
    grad_w_value = weight_grad(normed_inp, grad_value_one)
    grad_from_lat, grad_gain_lat = plain_norm_back(
        latent_rows, gain_lat.astype(jnp.float32), back_product(grad_query_one, w_query)
    )
    grad_latent_rows = grad_first + grad_from_lat
    grad_normed_inp = back_product(grad_key_one, w_key) + back_product(grad_value_one, w_value)
    grad_input_rows, grad_gain_inp = plain_norm_back(
        input_rows, gain_inp.astype(jnp.float32), grad_normed_inp
    )
    grad_mats = (grad_w_query, grad_w_key, grad_w_value, grad_w_out, grad_up_one, grad_down_one,
                 grad_s_query, grad_s_key, grad_s_value, grad_s_out, grad_up_two, grad_down_two)
    gain_grads = jnp.stack([grad_gain_lat, grad_gain_inp, grad_gain_first, grad_gain_self, grad_gain_second])
    gain_grads = jnp.moveaxis(gain_grads.reshape(5, parts, per), 1, 0).reshape(parts, 1, 5 * per)
    gain_grads = jnp.pad(gain_grads, ((0, 0), (0, 15), (0, width - 5 * per)))
    pieces = [gain_grads.astype(low_type)]
    for grad in grad_mats:
        for start in range(0, grad.shape[1], width):
            pieces.append(grad[:, start:start + width].reshape(parts, -1, width).astype(low_type))
    summed = lax.psum_scatter(jnp.concatenate(pieces, axis=1), ("dp", "fsdp"), scatter_dimension=0, tiled=False)
    summed = summed.astype(jnp.float32)
    gain_out = [summed[0, i * per:(i + 1) * per] for i in range(5)]
    at = 16
    out = []
    for mat in mats:
        columns = []
        for start in range(0, mat.shape[1], width):
            columns.append(summed[at:at + mat.shape[0]])
            at += mat.shape[0]
        out.append(columns[0] if len(columns) == 1 else jnp.concatenate(columns, axis=1))
    grad_latents = grad_latent_rows.reshape(groups, lat_rows, width).astype(low_type)
    grad_inputs = grad_input_rows.reshape(groups, span, width).astype(low_type)
    return (
        result, grad_latents, grad_inputs,
        gain_out[0], gain_out[1], out[0], out[1], out[2], out[3],
        gain_out[2], out[4], out[5],
        gain_out[3], out[6], out[7], out[8], out[9],
        gain_out[4], out[10], out[11],
    )


def hand_over(count, *refs):
    ins, outs, held, sems = refs[:count], refs[count:2 * count], refs[2 * count:3 * count], refs[-1]
    first = [pltpu.make_async_copy(ins[i], held[i], sems.at[i]) for i in range(count)]
    second = [pltpu.make_async_copy(held[i], outs[i], sems.at[count + i]) for i in range(count)]
    for copy in first:
        copy.start()
    for one, two in zip(first, second):
        one.wait()
        two.start()
    for copy in second:
        copy.wait()


def fits(mesh, lat, span, width, hidden):
    nd, nf = mesh.shape["dp"], mesh.shape["fsdp"]
    return (nd == 4 and nf == 8 and HEADS % nd == 0 and hidden == nd * width
            and width % (32 * nd * nf) == 0 and span == HEADS * lat and width // HEADS % 128 == 0)


def local(latents, inputs, frames, *rest, mesh):
    nd, nf = mesh.shape["dp"], mesh.shape["fsdp"]
    groups, lat, width = latents.shape
    span = inputs.shape[1]
    if groups != 1 or not fits(mesh, lat, span, width, rest[7].shape[1]):
        return plain_layer(latents, inputs, frames, *rest, mesh_size=mesh.size)
    (norm_latent, norm_input, cross_query, cross_key, cross_value, cross_output, norm_first, first_up,
     first_down, norm_self, self_query, self_key, self_value, self_output, norm_second, second_up,
     second_down, cotangent) = rest
    rows = cross_query.shape[0]
    index = lax.axis_index("dp") * nf + lax.axis_index("fsdp")
    gains = jnp.stack([norm_latent, norm_input, norm_first, norm_self, norm_second])
    lanes = lax.broadcasted_iota(jnp.int32, (8, 128), 1)
    gains = jnp.where(lanes // rows == lax.rem(index, 128 // rows),
                      jnp.tile(jnp.pad(gains, ((0, 3), (0, 0))), (1, 128 // rows)), 0.0)
    scratch = scratch_list(nd, nf, rows, width, lat, span, HEADS)
    anywhere = pl.BlockSpec(memory_space=pl.ANY)
    out_shape = (
        [jax.ShapeDtypeStruct(latents.shape, BF16)] * 2 + [jax.ShapeDtypeStruct(inputs.shape, BF16)]
        + [jax.ShapeDtypeStruct((8, width), F32)]
        + [jax.ShapeDtypeStruct(w.shape, F32) for w in (
            cross_query, cross_key, cross_value, cross_output, first_up, first_down,
            self_query, self_key, self_value, self_output, second_up, second_down)])
    flops = 2 * 3 * (lat * width * width * 22 + span * width * width * 2)
    results = pl.pallas_call(
        functools.partial(layer_kernel, INPUTS + OUTPUTS + tuple(scratch), nd, nf, rows),
        out_shape=out_shape,
        in_specs=[pl.BlockSpec(memory_space=pltpu.SMEM), pl.BlockSpec(memory_space=pltpu.VMEM)]
        + [anywhere] * (len(INPUTS) - 2),
        out_specs=[anywhere] * len(OUTPUTS),
        scratch_shapes=list(scratch.values()),
        compiler_params=pltpu.CompilerParams(
            collective_id=0, has_side_effects=True, vmem_limit_bytes=64 * 1024 * 1024),
        cost_estimate=pl.CostEstimate(flops=flops, bytes_accessed=30_000_000, transcendentals=4_000_000),
        name="layer",
    )(frames, gains, latents, inputs, cotangent, cross_query, cross_key, cross_value, cross_output,
      first_up, first_down, self_query, self_key, self_value, self_output, second_up, second_down)
    (result, grad_latents, grad_inputs, gain_grads, g_cq, g_ck, g_cv, g_co, g_fu, g_fd,
     g_sq, g_sk, g_sv, g_so, g_gu, g_gd) = pl.pallas_call(
        functools.partial(hand_over, len(OUTPUTS)),
        out_shape=out_shape,
        in_specs=[anywhere] * len(OUTPUTS),
        out_specs=[anywhere] * len(OUTPUTS),
        scratch_shapes=[pltpu.VMEM(o.shape, o.dtype) for o in out_shape]
        + [pltpu.SemaphoreType.DMA((2 * len(OUTPUTS),))],
        compiler_params=pltpu.CompilerParams(vmem_limit_bytes=64 * 1024 * 1024),
        cost_estimate=pl.CostEstimate(flops=0, bytes_accessed=12_000_000, transcendentals=0),
        name="hand_over",
    )(*results)
    own = lax.dynamic_slice(gain_grads, (0, index * rows), (8, rows))
    return (result, grad_latents, grad_inputs, own[0], own[1], g_cq, g_ck, g_cv, g_co, own[2], g_fu, g_fd,
            own[3], g_sq, g_sk, g_sv, g_so, own[4], g_gu, g_gd)


def solution(mesh):
    in_specs = (
        P(("dp", "fsdp"), None, None),
        P(("dp", "fsdp"), None, None),
        P(("dp", "fsdp")),
        P(("dp", "fsdp")),
        P(("dp", "fsdp")),
        P(("dp", "fsdp"), None),
        P(("dp", "fsdp"), None),
        P(("dp", "fsdp"), None),
        P(("dp", "fsdp"), None),
        P(("dp", "fsdp")),
        P(("dp", "fsdp"), None),
        P(("dp", "fsdp"), None),
        P(("dp", "fsdp")),
        P(("dp", "fsdp"), None),
        P(("dp", "fsdp"), None),
        P(("dp", "fsdp"), None),
        P(("dp", "fsdp"), None),
        P(("dp", "fsdp")),
        P(("dp", "fsdp"), None),
        P(("dp", "fsdp"), None),
        P(("dp", "fsdp"), None, None),
    )
    out_specs = (
        P(("dp", "fsdp"), None, None),
        P(("dp", "fsdp"), None, None),
        P(("dp", "fsdp"), None, None),
        P(("dp", "fsdp")),
        P(("dp", "fsdp")),
        P(("dp", "fsdp"), None),
        P(("dp", "fsdp"), None),
        P(("dp", "fsdp"), None),
        P(("dp", "fsdp"), None),
        P(("dp", "fsdp")),
        P(("dp", "fsdp"), None),
        P(("dp", "fsdp"), None),
        P(("dp", "fsdp")),
        P(("dp", "fsdp"), None),
        P(("dp", "fsdp"), None),
        P(("dp", "fsdp"), None),
        P(("dp", "fsdp"), None),
        P(("dp", "fsdp")),
        P(("dp", "fsdp"), None),
        P(("dp", "fsdp"), None),
    )
    return jax.shard_map(functools.partial(local, mesh=mesh), mesh=mesh, in_specs=in_specs, out_specs=out_specs,
                         check_vma=False)
```

```python
import functools

import jax
import jax.numpy as jnp
from jax import lax
from jax.experimental import pallas as pl
from jax.experimental.pallas import tpu as pltpu
from jax.sharding import PartitionSpec as P

HEADS = 8
FRAME_TOK = 64
EPS = 1e-05
NEG = -1000000000.0
F32 = jnp.float32
BF16 = jnp.bfloat16
MESH = pl.DeviceIdType.MESH
NN = (((1,), (0,)), ((), ()))
NT = (((1,), (1,)), ((), ()))
TN = (((0,), (0,)), ((), ()))
GC0 = 0.7978845608
GC1 = 0.044715


def dot(left, right, dims):
    return lax.dot_general(left, right, dims, preferred_element_type=F32)


def low(value):
    return value.astype(BF16)


def flip(value, mask, size):
    out = 0
    bit = 1
    while bit < size:
        one = lax.rem(lax.div(value, jnp.int32(bit)), jnp.int32(2))
        if isinstance(mask, int):
            other = jnp.int32((mask // bit) % 2)
        else:
            other = lax.rem(lax.div(mask, jnp.int32(bit)), jnp.int32(2))
        out = out + lax.rem(one + other, jnp.int32(2)) * bit
        bit *= 2
    return out


def norm_parts(value):
    center = value - jnp.mean(value, axis=-1, keepdims=True)
    spread = jnp.mean(center * center, axis=-1, keepdims=True)
    inv = lax.rsqrt(spread + EPS)
    return center * inv, inv


def norm(value, gain):
    hat, _ = norm_parts(value)
    return low(hat * gain)


def norm_back(value, gain, grad):
    hat, inv = norm_parts(value)
    scaled = grad * gain
    out = inv * (
        scaled
        - jnp.mean(scaled, axis=-1, keepdims=True)
        - hat * jnp.mean(scaled * hat, axis=-1, keepdims=True)
    )
    return out, jnp.sum(grad * hat, axis=0, keepdims=True)


def gelu_both(value):
    square = value * value
    tan = jnp.tanh(GC0 * value * (1.0 + GC1 * square))
    half = 0.5 * (1.0 + tan)
    slope = half + 0.5 * value * (1.0 - tan * tan) * (GC0 * (1.0 + 3.0 * GC1 * square))
    return value * half, slope


INPUTS = ("frames", "gains", "latents", "inputs", "cot",
          "cq", "ck", "cv", "co", "fu", "fd", "sq_", "sk_", "sv_", "so_", "gu_", "gd_")
OUTPUTS = ("out", "glat", "ginp", "ggain",
           "ocq", "ock", "ocv", "oco", "ofu", "ofd", "osq", "osk", "osv", "oso", "ogu", "ogd")


def scratch_list(nd, nf, rows, width, lat, span, heads):
    nz = nf // 2
    hd = width // heads
    tp_cols = width // nd
    four = (nd, nf, rows, width)
    act = (nd, nz, rows, width)
    three = (nd - 1, nz, rows, width)
    vm = pltpu.VMEM
    return {
        "wx": vm((4,) + four, BF16),
        "up1": vm(four, BF16), "dn1": vm(four, BF16),
        "up2": vm(four, BF16), "dn2": vm(four, BF16),
        "sq": vm((3, nd, nf, rows, tp_cols), BF16), "so": vm((nf, rows, width), BF16),
        "sqs": vm((nd, 3, rows, tp_cols), BF16),
        "xn": vm((span, width), BF16), "kk": vm((span, width), BF16), "vv": vm((span, width), BF16),
        "pp": vm((heads, lat, span), BF16),
        "ag1": vm(act, BF16), "u1": vm(act, BF16), "d1": vm(act, BF16), "bg": vm(act, BF16),
        "ag2": vm(act, BF16), "u2": vm(act, BF16), "d2": vm(act, BF16),
        "gg": vm(act, BF16), "ggs": vm(act, BF16),
        "q2": vm((nd, lat, tp_cols), BF16), "k2": vm((nd, lat, tp_cols), BF16),
        "v2": vm((nd, lat, tp_cols), BF16), "c2": vm((nd, lat, tp_cols), BF16),
        "p2": vm((nd, heads // nd, lat, lat), BF16),
        "ra": vm(three, BF16), "rb": vm(three, BF16), "sa": vm(three, BF16), "sc": vm(three, BF16),
        "xw": vm((4,) + three, BF16),
        "GU": vm((2, nz, nd, rows, width), BF16), "GD": vm((2, nz, nd, rows, width), BF16),
        "GQ": vm((2, nz, nd, 3, rows, tp_cols), BF16), "GO": vm((2, nz, rows, width), BF16),
        "SU": vm((nz, nd, rows, width), BF16), "SD": vm((nz, nd, rows, width), BF16),
        "SQ": vm((nz, nd, 3, rows, tp_cols), BF16), "SO": vm((nz, rows, width), BF16),
        "ZU": vm((nz, nd, rows, width), BF16), "ZD": vm((nz, nd, rows, width), BF16),
        "ZQ": vm((nz, nd, 3, rows, tp_cols), BF16), "ZO": vm((nz, rows, width), BF16),
        "CU1": vm((nd - 1, rows, width), BF16), "CU2": vm((nd - 1, rows, width), BF16),
        "CQ": vm((nd - 1, 3, rows, tp_cols), BF16),
        "z1": vm((lat, width), F32), "z2": vm((lat, width), F32), "z3": vm((lat, width), F32),
        "ga": vm((lat, width), F32), "own": vm((lat, width), F32),
        "ob": vm((lat, width), BF16),
        "lt": vm((lat, width), BF16), "an": vm((lat, width), BF16), "qq": vm((lat, width), BF16),
        "cc": vm((lat, width), BF16), "gb": vm((lat, width), BF16), "dc": vm((lat, width), BF16),
        "gn": vm((8, width), F32), "dg": vm((8, width), F32),
        "gr": vm((1 + nz - 1 + nd - 1, 8, width), F32), "gs": vm((nd, nf, 8, 128), F32),
        "ss": pltpu.SemaphoreType.DMA((SEMS,)), "rs": pltpu.SemaphoreType.DMA((SEMS,)),
        "ls": pltpu.SemaphoreType.DMA((40,)),
    }


SEMS = 164


def layer_kernel(names, nd, nf, rows, *refs):
    r = dict(zip(names, refs))

    class Space:
        pass

    n = Space()
    for key, ref in r.items():
        setattr(n, key, ref)
    nz = nf // 2
    width = n.lt.shape[1]
    lat = n.lt.shape[0]
    span = n.xn.shape[0]
    hd = width // HEADS
    cols = width // nd
    local_heads = HEADS // nd
    scale = hd ** (-0.5)
    a = lax.axis_index("dp")
    b = lax.axis_index("fsdp")
    z = lax.div(b, jnp.int32(2))
    c = lax.rem(b, jnp.int32(2))
    sib = (a, z * 2 + 1 - c)

    def apos(k):
        return flip(a, k, nd)

    def zpos(m):
        return flip(z, m, nz)

    def bpos(m):
        return zpos(m) * 2 + c

    taken = [0, 0]

    def group(count, make, after=None):
        if after is None:
            base = taken[0]
            taken[0] += count
            assert taken[0] <= SEMS
        else:
            base = after.base
            assert count <= after.count

        def desc(i):
            src, dst, peer, *where = make(i)
            return pltpu.make_async_remote_copy(
                src_ref=src, dst_ref=dst, send_sem=n.ss.at[base + i],
                recv_sem=n.rs.at[base + (where[0] if where else i)],
                device_id=peer, device_id_type=MESH)

        desc.count = count
        desc.base = base
        return desc

    def start(g):
        for i in range(g.count):
            g(i).start()

    def recv(g):
        for i in range(g.count):
            g(i).wait_recv()

    def sent(g):
        if hasattr(g, "sent"):
            g.sent()
            return
        for i in range(g.count):
            g(i).wait_send()

    def load(src, dst):
        i = taken[1]
        taken[1] += 1
        copy = pltpu.make_async_copy(src, dst, n.ls.at[i])
        copy.start()
        return copy

    def dp_group(src, dst):
        return group(nd - 1, lambda i: (src(i + 1), dst(i + 1), (apos(i + 1), b)))

    inner = lax.rem(z, jnp.int32(3)) != 0
    outer = jnp.logical_not(inner)

    class Gather:
        def __init__(self, block):
            self.g = group(4, lambda i: (
                (block(b), block(b), (a, bpos(i + 1))) if i < 3
                else (block(bpos(2)), block(bpos(2)), (a, bpos(1)), 2)))

        def start(self):
            self.g(1).start()
            self.g(0).start()
            pl.when(inner)(lambda: self.g(2).start())

        def relay(self):
            @pl.when(inner)
            def _():
                self.g(1).wait_recv()
                self.g(3).start()

        def recv(self, m):
            if m == 2:
                pl.when(outer)(lambda: self.g(1).wait_recv())
            else:
                self.g(m - 1).wait_recv()

        def sent(self):
            self.g(0).wait_send()
            self.g(1).wait_send()

            @pl.when(inner)
            def _():
                self.g(2).wait_send()
                self.g(3).wait_send()

    class Reduce:
        def __init__(self, part, slots, after):
            self.part, self.slots = part, slots
            self.g = group(4, lambda i: (
                (part(zpos(i + 1)), slots.at[i], (a, bpos(i + 1))) if i < 3
                else (part(zpos(3)), slots.at[3], (a, bpos(1)))), after.g)

        def start(self):
            @pl.when(outer)
            def _():
                self.g(3).start()
                self.g(1).start()

            pl.when(inner)(lambda: self.g(2).start())
            self.g(0).start()

        def combine(self):
            @pl.when(inner)
            def _():
                self.g(3).wait_recv()
                ref = self.part(zpos(2))
                ref[...] = low(ref[...].astype(F32) + self.slots[3].astype(F32))
                self.g(1).start()

        def total(self):
            self.g(0).wait_recv()
            self.g(1).wait_recv()
            ref = self.part(z)

            @pl.when(inner)
            def _():
                self.g(2).wait_recv()
                ref[...] = low(ref[...].astype(F32) + self.slots[2].astype(F32))

            return ref[...].astype(F32) + self.slots[0].astype(F32) + self.slots[1].astype(F32)

        def sent(self):
            self.g(0).wait_send()
            self.g(1).wait_send()
            pl.when(outer)(lambda: self.g(3).wait_send())
            pl.when(inner)(lambda: self.g(2).wait_send())

    class Share:
        def __init__(self, one, two, three, after=None):
            def make(i):
                if i in (0, 2):
                    return one(i // 2) + ((apos(1), b),)
                if i in (1, 3):
                    return two(1 - i // 2) + ((apos(2), b),)
                return three(i - 4) + ((apos(2 - (i - 4)), b),)

            self.g = group(6, make, after and after.g)

        def start(self):
            for i in range(4):
                self.g(i).start()

        def relay(self):
            for i in range(2):
                self.g(i).wait_recv()
                self.g(4 + i).start()

        def recv(self, k):
            if isinstance(k, int):
                for i in ((2,), (3,), (4, 5))[k - 1]:
                    self.g(i).wait_recv()
                return
            for j in (1, 2, 3):
                pl.when(k == j)(lambda j=j: self.recv(j))

        def sent(self):
            for i in range(6):
                self.g(i).wait_send()

    def sib_group(src, dst):
        return group(1, lambda i: (src, dst, sib))

    class Merge:
        def __init__(self, part, slots, after=None):
            self.part, self.slots = part, slots

            def make(i):
                k, h, slot, peer = ((3, 0, 2, 2), (3, 1, 2, 1), (1, 1, 0, 1), (2, 0, 1, 2),
                                    (1, 0, 0, 1), (2, 1, 1, 2))[i]
                return part(k, h), slots.at[slot, halves[h]], (apos(peer), b)

            self.g = group(6, make, after and after.g)

        def push(self, k):
            if isinstance(k, int):
                for i in ((2,), (3,), (0, 1))[k - 1]:
                    self.g(i).start()
                return
            for j in (1, 2, 3):
                pl.when(k == j)(lambda j=j: self.push(j))

        def combine(self):
            for i, k, h in ((0, 1, 0), (1, 2, 1)):
                self.g(i).wait_recv()
                ref = self.part(k, h)
                ref[...] = low(ref[...].astype(F32) + self.slots[2, halves[h]].astype(F32))
                self.g(4 + i).start()

        def total(self, own):
            for i in (2, 3, 4, 5):
                self.g(i).wait_recv()
            return own + self.slots[0].reshape(own.shape).astype(F32) + self.slots[1].reshape(own.shape).astype(F32)

        def sent(self):
            for i in range(6):
                self.g(i).wait_send()

    mid = nz // 2
    halves = (slice(0, mid), slice(mid, nz))

    def stage(refs, dst):
        return [load(ref, dst.at[pl.ds(i * rows, rows)]) for i, ref in enumerate(refs)]

    blocks = [pl.ds(j * width, width) for j in range(nd)]
    in_cross = stage((n.cq, n.ck, n.cv, n.co), n.z1)
    in_up1 = stage([n.fu.at[:, s] for s in blocks], n.z2)
    in_dn1 = [load(n.fd, n.z3)]
    in_lat = [load(n.latents.at[0], n.lt)]
    in_x = [load(n.inputs.at[0], n.xn)]
    in_self = stage((n.sq_, n.sk_, n.sv_, n.so_), n.ga)
    in_up2 = stage([n.gu_.at[:, s] for s in blocks], n.own)
    in_cot = [load(n.cot.at[0], n.gb)]

    def arrived(copies):
        for copy in copies:
            copy.wait()

    peers = [(apos(k), b) for k in range(1, nd)] + [(a, bpos(m)) for m in range(1, nz)] + [sib]
    barrier = pltpu.get_barrier_semaphore()
    for peer in peers:
        pl.semaphore_signal(barrier, inc=1, device_id=peer, device_id_type=MESH)

    def small_sum(buf):
        slots = n.gr
        hops = (group(1, lambda i: (buf, slots.at[0], sib)),
                group(nd - 1, lambda i: (buf, slots.at[1 + i], (apos(i + 1), b))),
                group(nz - 1, lambda i: (buf, slots.at[nd + i], (a, bpos(i + 1)))))
        phases = []
        first = 0
        for g in hops:
            def finish(g=g, first=first):
                recv(g)
                sent(g)
                total = buf[...]
                for i in range(g.count):
                    total = total + slots[first + i]
                buf[...] = total

            phases.append((functools.partial(start, g), finish))
            first += g.count
        return phases

    pl.semaphore_wait(barrier, len(peers))
    n.gs[a, b] = low(n.gains[...]).astype(F32)
    gains_z = Gather(lambda bi: n.gs.at[a, bi])
    gains_sib = [sib_group(n.gs.at[a, bpos(m)], n.gs.at[a, bpos(m)]) for m in range(nz)]
    gains_dp = dp_group(lambda k: n.gs.at[a], lambda k: n.gs.at[a])
    gains_z.start()
    start(gains_sib[0])
    arrived(in_cross)
    for i in range(4):
        n.wx[i, a, b] = low(n.z1[i * rows:(i + 1) * rows])
    in_dn2 = [load(n.gd_, n.z1)]

    def wx_at(ai, bi):
        return n.wx.at[:, ai, bi]

    cross_z = Gather(lambda bi: n.wx.at[:, a, bi])
    cross_dp = []
    for m in range(nz):
        def direct(h, m=m):
            at = n.wx.at[2 * h:2 * h + 2, a, bpos(m)]
            return at, at

        def relayed(h, m=m):
            at = n.wx.at[2 * h:2 * h + 2, apos(1 + h), bpos(m)]
            return at, at

        cross_dp.append(Share(direct, direct, relayed))
    cross_sib = [[sib_group(wx_at(apos(k), bpos(m)), wx_at(apos(k), bpos(m))) for m in range(nz)]
                 for k in range(nd)]
    cross_z.start()
    cross_dp[0].start()
    start(cross_sib[0][0])

    su1, su2 = n.xw.at[3, 0], n.xw.at[3, 1]

    def put_up(staged, sends, up):
        for j in range(nd):
            sends[j] = low(staged[j * rows:(j + 1) * rows])
        up[a, b] = sends[a]

    def put_dn(staged, dn):
        dn[lax.div(b * nd, jnp.int32(nf)), pl.ds(lax.rem(b * nd, jnp.int32(nf)), nd)] = (
            low(staged[...]).reshape(nd, rows, width))

    def dn_at(dn, bi):
        return dn.at[lax.div(bi * nd, jnp.int32(nf)), pl.ds(lax.rem(bi * nd, jnp.int32(nf)), nd)]

    arrived(in_up1)
    put_up(n.z2, su1, n.up1)
    up1_dp = dp_group(lambda k: su1.at[apos(k)], lambda k: n.up1.at[a, b])
    start(up1_dp)
    arrived(in_dn1)
    put_dn(n.z3, n.dn1)
    arrived(in_self)
    for i in range(3):
        for j in range(nd):
            n.sqs[j, i] = low(n.ga[i * rows:(i + 1) * rows, j * cols:(j + 1) * cols])
    for i in range(3):
        n.sq[i, a, b] = n.sqs[a, i]
    n.so[b] = low(n.ga[3 * rows:4 * rows])
    arrived(in_up2)
    put_up(n.own, su2, n.up2)
    arrived(in_dn2)
    put_dn(n.z1, n.dn2)
    arrived(in_cot)
    act_rows = (nz, rows, width)

    def up_z(up):
        return Gather(lambda bi: up.at[:, bi])

    def up_sib(up):
        return [sib_group(up.at[:, bpos(m)], up.at[:, bpos(m)]) for m in range(nz)]

    def dn_z(dn):
        return Gather(lambda bi: dn_at(dn, bi))

    def dn_sib(dn):
        return [sib_group(dn_at(dn, bpos(m)), dn_at(dn, bpos(m))) for m in range(nz)]

    gain = [n.gn.at[i:i + 1] for i in range(5)]

    arrived(in_lat)
    arrived(in_x)
    gains_z.relay()
    for m in (1, 2, 3):
        gains_z.recv(m)
        start(gains_sib[m])
    for g in gains_sib:
        recv(g)
    start(gains_dp)
    cross_z.relay()
    for m in (1, 2, 3):
        cross_z.recv(m)
        cross_dp[m].start()
        start(cross_sib[0][m])
        if m == 1:
            cross_dp[0].relay()
    up1_z, up1_sib, dn1_z, dn1_sib = up_z(n.up1), up_sib(n.up1), dn_z(n.dn1), dn_sib(n.dn1)
    recv(up1_dp)
    up1_z.start()
    dn1_z.start()
    cross_dp[1].relay()
    cross_dp[2].relay()
    recv(gains_dp)
    per = 128 // rows
    for j in range(width // 128):
        tile = 0.0
        for i in range(j * per, (j + 1) * per):
            tile = tile + n.gs[i // nf, i % nf]
        n.gn[:, j * 128:(j + 1) * 128] = tile

    block = lat

    def token_norm(i, _):
        at = pl.ds(pl.multiple_of(i * block, block), block)
        n.xn[at] = norm(n.xn[at].astype(F32), gain[1][...])
        return 0

    n.an[...] = norm(n.lt[...].astype(F32), gain[0][...])
    lax.fori_loop(0, span // block, token_norm, 0)

    cross_dp[3].relay()
    for m in range(nz):
        for k in range(1, nd):
            cross_dp[m].recv(k)
            start(cross_sib[k][m])
        if m == 1:
            up1_z.relay()
    up2_dp = dp_group(lambda k: su2.at[apos(k)], lambda k: n.up2.at[a, b])
    sq_dp = dp_group(lambda k: n.sqs.at[apos(k)], lambda k: n.sq.at[:, a, b])
    start(sq_dp)
    start(up2_dp)
    dn1_z.relay()
    for k in range(nd):
        for m in range(nz):
            recv(cross_sib[k][m])

    def rows_of(ref, k):
        return ref[k].reshape(lat, width)

    def spread(buf, value, after=None):
        buf[0] = value.reshape(act_rows)
        g = Share(lambda h: (buf.at[0, halves[h]], buf.at[1, halves[h]]),
                  lambda h: (buf.at[0, halves[h]], buf.at[2, halves[h]]),
                  lambda h: (buf.at[1 + h, halves[h]], buf.at[3, halves[h]]), after)
        g.start()
        return g

    taken[1] = 0
    cot_dp = spread(n.gg, n.gb[...])
    def wcols(i, at):
        return n.wx[i, :, :, :, at].reshape(width, at.size)

    def full(ref):
        return ref[...].reshape(width, width)

    n.qq[...] = low(dot(n.an[...], n.wx[0].reshape(width, width), NN))
    wide = 256

    def token_proj(i, _):
        at = pl.ds(pl.multiple_of(i * wide, wide), wide)
        n.kk[:, at] = low(dot(n.xn[...], wcols(1, at), NN))
        n.vv[:, at] = low(dot(n.xn[...], wcols(2, at), NN))
        return 0

    lax.fori_loop(0, width // wide, token_proj, 0)
    valid = lax.broadcasted_iota(jnp.int32, (lat, span), 1) < n.frames[0] * FRAME_TOK

    def softmax(scores):
        expo = jnp.exp(scores - jnp.max(scores, axis=-1, keepdims=True))
        return low(expo / jnp.sum(expo, axis=-1, keepdims=True))

    def cross_head(h, _):
        at = pl.ds(pl.multiple_of(h * hd, hd), hd)
        scores = jnp.where(valid, dot(n.qq[:, at], n.kk[:, at], NT) * scale, NEG)
        probs = softmax(scores)
        n.pp[h] = probs
        n.cc[:, at] = low(dot(probs, n.vv[:, at], NN))
        return 0

    lax.fori_loop(0, HEADS, cross_head, 0, unroll=2)
    recv(sq_dp)
    sq_z = Gather(lambda bi: n.sq.at[:, :, bi])
    so_z = Gather(lambda bi: n.so.at[bi])
    sq_sib = [sib_group(n.sq.at[:, :, bpos(m)], n.sq.at[:, :, bpos(m)]) for m in range(nz)]
    so_sib = [sib_group(n.so.at[bpos(m)], n.so.at[bpos(m)]) for m in range(nz)]
    sq_z.start()
    so_z.start()
    cot_dp.relay()
    z1 = n.lt[...].astype(F32) + dot(n.cc[...], n.wx[3].reshape(width, width), NN)
    n.z1[...] = z1

    acts = []

    def collect(make, gathered, sends, slots, previous, aside=None):
        if previous is not None:
            sent(previous)
        back = Merge(lambda k, h: sends.at[k - 1, halves[h]], slots, acts[0] if acts else None)
        acts.append(back)
        back.gathered = gathered
        n.own[...] = make(0)
        gathered.relay()
        if aside is not None:
            aside()

        def step(i, _):
            gathered.recv(i + 1)
            sends[i] = low(make(i + 1)).reshape(act_rows)
            back.push(i + 1)
            return 0

        lax.fori_loop(0, nd - 1, step, 0)
        return back

    def gather_sum(back, slots):
        if back.gathered is not None:
            sent(back.gathered)
        return back.total(n.own[...])

    def feed_hidden(ag, u, d, up):
        def make(k):
            value, slope = gelu_both(dot(rows_of(ag, k), full(up), NN))
            hidden = low(value)
            u[k] = hidden.reshape(act_rows)
            d[k] = low(slope).reshape(act_rows)
            return hidden

        return make

    def feed_make(ag, u, d, up, dn):
        hide = feed_hidden(ag, u, d, up)

        def make(k):
            return dot(hide(k), full(dn), NN)

        return make

    ag1_dp = spread(n.ag1, norm(z1, gain[2][...]))
    recv(up2_dp)
    up2_z, up2_sib, dn2_z, dn2_sib = up_z(n.up2), up_sib(n.up2), dn_z(n.dn2), dn_sib(n.dn2)
    for m in range(nz):
        for g, line in ((up1_z, up1_sib), (dn1_z, dn1_sib)):
            if m > 0:
                g.recv(m)
            start(line[m])
    for m in range(nz):
        recv(up1_sib[m])
        recv(dn1_sib[m])

    def later_weights():
        sq_z.relay()
        so_z.relay()
        up2_z.start()

    out1 = collect(feed_make(n.ag1, n.u1, n.d1, n.up1, n.dn1), ag1_dp, n.sa, n.ra, None, later_weights)
    out1.combine()
    dn2_z.start()
    for g in ([cross_z, gains_z, gains_dp, up1_z, dn1_z] + gains_sib + cross_dp
              + [g for line in cross_sib for g in line]):
        sent(g)
    z2 = n.z1[...] + gather_sum(out1, n.ra)
    n.z2[...] = z2

    bg_dp = spread(n.bg, norm(z2, gain[3][...]), ag1_dp)
    for m in range(nz):
        for g, line in ((sq_z, sq_sib), (so_z, so_sib)):
            if m > 0:
                g.recv(m)
            start(line[m])
    up2_z.relay()
    for m in range(nz):
        recv(sq_sib[m])
        recv(so_sib[m])

    def self_make(k):
        normed = rows_of(n.bg, k)
        for i, ref in enumerate((n.q2, n.k2, n.v2)):
            ref[k] = low(dot(normed, n.sq[i].reshape(width, cols), NN))
        for h in range(local_heads):
            at = slice(h * hd, (h + 1) * hd)
            probs = softmax(dot(n.q2[k, :, at], n.k2[k, :, at], NT) * scale)
            n.p2[k, h] = probs
            n.c2[k, :, at] = low(dot(probs, n.v2[k, :, at], NN))
        return dot(n.c2[k], n.so[...].reshape(cols, width), NN)

    out_self = collect(self_make, bg_dp, n.sa, n.rb, out1)
    out_self.combine()
    dn2_z.relay()
    z3 = n.z2[...] + gather_sum(out_self, n.rb)
    n.z3[...] = z3

    ag2_dp = spread(n.ag2, norm(z3, gain[4][...]), ag1_dp)
    for m in range(nz):
        if m > 0:
            up2_z.recv(m)
        start(up2_sib[m])
    for m in range(nz):
        recv(up2_sib[m])

    sc, rc = n.sc, n.rb

    def feed_back(ks, g, d, up, dn, sends):
        def rows_together(ref):
            parts = [rows_of(ref, k) for k in ks]
            return parts[0] if len(parts) == 1 else jnp.concatenate(parts, axis=0)

        step = width // nd
        left = rows_together(g)
        for i in range(nd):
            at = slice(i * step, (i + 1) * step)
            grad = dot(left, dn[i].reshape(step, width), NT)
            for j, k in enumerate(ks):
                slope = d[k, :, :, at].reshape(lat, step).astype(F32)
                d[k, :, :, at] = low(slope * grad[j * lat:(j + 1) * lat]).reshape(nz, rows, step)
        left = rows_together(d)
        for i in range(nd):
            at = slice(i * step, (i + 1) * step)
            value = dot(left, up[i].reshape(step, width), NT)
            for j, k in enumerate(ks):
                part = value[j * lat:(j + 1) * lat]
                if k == 0:
                    n.own[:, at] = part
                else:
                    sends[k - 1, :, :, at] = low(part).reshape(nz, rows, step)

    hide2 = feed_hidden(n.ag2, n.u2, n.d2, n.up2)
    final_dp = Merge(lambda k, h: sc.at[k - 1, halves[h]], rc)
    sent(up1_dp)
    sent(up2_dp)
    hide2(0)
    ag2_dp.relay()

    def hide_step(i, _):
        ag2_dp.recv(i + 1)
        hide2(i + 1)
        return 0

    lax.fori_loop(0, nd - 1, hide_step, 0)

    def put_grad(value, ref, first):
        for i in range(value.shape[0] // rows):
            ai, bi = divmod(first + i, nf)
            zi, ci = divmod(bi, 2)
            ref[ci, zi, ai] = value[i * rows:(i + 1) * rows]

    def put_down(value, ref, first):
        for i in range(value.shape[0] // rows):
            bi, ai = divmod(first + i, nd)
            zi, ci = divmod(bi, 2)
            ref[ci, zi, ai] = value[i * rows:(i + 1) * rows]

    tall = 256

    def every_row(ref, at=slice(None)):
        value = ref[:, :, :, at]
        return value.reshape(value.shape[0] * value.shape[1] * value.shape[2], value.shape[3])

    def up_grad(ag, d):
        for i in range(width // tall):
            at = slice(i * tall, (i + 1) * tall)
            put_grad(low(dot(every_row(ag, at), every_row(d), TN)), n.GU, i * tall // rows)

    def down_grad(u, g):
        for i in range(width // tall):
            at = slice(i * tall, (i + 1) * tall)
            put_down(low(dot(every_row(u, at), every_row(g), TN)), n.GD, i * tall // rows)

    def core_sum(grad, other):
        for i in range(nz):
            grad[c, i] = low(grad[c, i].astype(F32) + other[i].astype(F32))

    def sib_grads(grad, other):
        g = sib_group(grad.at[1 - c], other)
        start(g)
        return g

    def z_grads(grad, slots, after):
        g = Reduce(lambda zi: grad.at[c, zi], slots, after)
        g.start()
        return g

    for k in range(1, nd):
        cot_dp.recv(k)
    down_grad(n.u2, n.gg)
    gd2_sib = sib_grads(n.GD, n.SD)
    for m in range(nz):
        if m > 0:
            dn2_z.recv(m)
        start(dn2_sib[m])
    for m in range(nz):
        recv(dn2_sib[m])
    sent(out_self)
    dm2 = Merge(lambda k, h: n.sa.at[k - 1, halves[h]], n.ra, out1)
    dm2.gathered = None
    recv(gd2_sib)
    core_sum(n.GD, n.SD)
    gd2_z = z_grads(n.GD, n.ZD, cross_z)
    feed_back((3, 0), n.gg, n.d2, n.up2, n.dn2, n.sa)
    dm2.push(3)
    feed_back((1, 2), n.gg, n.d2, n.up2, n.dn2, n.sa)
    dm2.push(1)
    dm2.push(2)
    sent(ag2_dp)
    up_grad(n.ag2, n.d2)
    gu2_sib = sib_grads(n.GU, n.SU)
    dm2.combine()
    n.ob[...] = low(dot(rows_of(n.u2, 0), full(n.dn2), NN))

    def out_step(i, _):
        sc[i] = low(dot(rows_of(n.u2, i + 1), full(n.dn2), NN)).reshape(act_rows)
        return 0

    lax.fori_loop(0, nd - 1, out_step, 0)
    recv(gu2_sib)
    core_sum(n.GU, n.SU)
    gu2_z = z_grads(n.GU, n.ZU, gains_z)

    def set_gain(i, value):
        n.dg[i:i + 1] = value

    n.dg[...] = jnp.zeros_like(n.dg)
    back, gain_part = norm_back(n.z3[...], gain[4][...], gather_sum(dm2, n.ra))
    set_gain(4, gain_part)
    ga = rows_of(n.gg, 0).astype(F32) + back
    n.ga[...] = ga

    sent(cot_dp)

    gs_dp = spread(n.ggs, low(ga), ag1_dp)
    gd2_z.combine()

    def attend_back(q, k, v, probs, grad):
        grad_probs = dot(grad, v, NT)
        wide_probs = probs.astype(F32)
        inner = jnp.sum(wide_probs * grad_probs, axis=-1, keepdims=True)
        scores = low(wide_probs * (grad_probs - inner))
        return (low(dot(scores, k, NN) * scale), low(dot(scores, q, TN) * scale),
                low(dot(probs, grad, TN)))

    def self_back(k):
        grad = low(dot(rows_of(n.ggs, k), n.so[...].reshape(cols, width), NT))
        for h in range(local_heads):
            at = slice(h * hd, (h + 1) * hd)
            dq, dk, dv = attend_back(n.q2[k, :, at], n.k2[k, :, at], n.v2[k, :, at],
                                     n.p2[k, h], grad[:, at])
            n.q2[k, :, at] = dq
            n.k2[k, :, at] = dk
            n.v2[k, :, at] = dv
        total = 0.0
        for i, ref in enumerate((n.q2, n.k2, n.v2)):
            total = total + dot(ref[k], n.sq[i].reshape(width, cols), NT)
        return total

    db = collect(self_back, gs_dp, n.sa, n.rb, dm2)
    for i, ref in enumerate((n.q2, n.k2, n.v2)):
        value = low(dot(every_row(n.bg), ref[...].reshape(nd * lat, cols), TN))
        for j in range(width // rows):
            ai, bi = divmod(j, nf)
            zi, ci = divmod(bi, 2)
            n.GQ[ci, zi, ai, i] = value[j * rows:(j + 1) * rows]
    value = low(dot(n.c2[...].reshape(nd * lat, cols), every_row(n.ggs), TN))
    for bi in range(nf):
        zi, ci = divmod(bi, 2)
        n.GO[ci, zi] = value[bi * rows:(bi + 1) * rows]
    gq_sib = sib_grads(n.GQ, n.SQ)
    go_sib = sib_grads(n.GO, n.SO)
    db.combine()
    gu2_z.combine()
    recv(gq_sib)
    core_sum(n.GQ, n.SQ)
    gq_z = z_grads(n.GQ, n.ZQ, up1_z)
    recv(go_sib)
    core_sum(n.GO, n.SO)
    go_z = z_grads(n.GO, n.ZO, dn1_z)
    back, gain_part = norm_back(n.z2[...], gain[3][...], gather_sum(db, n.rb))
    set_gain(3, gain_part)
    ga = n.ga[...] + back
    n.ga[...] = ga

    outs = []
    gf_dp = spread(n.gg, low(ga), ag1_dp)
    sent(db)
    dm1 = Merge(lambda k, h: n.sa.at[k - 1, halves[h]], n.ra, out1)
    dm1.gathered = gf_dp
    feed_back((0,), n.gg, n.d1, n.up1, n.dn1, n.sa)
    gf_dp.relay()
    gf_dp.recv(1)
    gf_dp.recv(2)
    feed_back((1, 2), n.gg, n.d1, n.up1, n.dn1, n.sa)
    dm1.push(1)
    dm1.push(2)
    gf_dp.recv(3)
    feed_back((3,), n.gg, n.d1, n.up1, n.dn1, n.sa)
    dm1.push(3)

    def out_rows(value, staged, target):
        staged[...] = value.reshape(staged.shape)
        return load(staged, target)

    gq_z.combine()
    go_z.combine()
    total = gd2_z.total()
    down_out = out_rows(total, n.z2, n.ogd)
    total = gu2_z.total()

    def column_grads(total, sends, slots):
        sends[...] = low(total)
        return dp_group(lambda k: sends.at[apos(k)], lambda k: slots.at[k - 1])

    su3, su4 = n.d2.at[0], n.d2.at[1]
    cu2_dp = column_grads(total, su3, n.CU2)
    for g in (gu2_sib, gd2_sib, gu2_z, gd2_z):
        sent(g)
    down_grad(n.u1, n.gg)
    gd1_sib = sib_grads(n.GD, n.SD)
    dm1.combine()
    zu1, zd1 = n.ag2, n.u2
    for g in (up2_z, dn2_z, sq_z, so_z):
        sent(g)
    recv(gd1_sib)
    core_sum(n.GD, n.SD)
    gd1_z = z_grads(n.GD, zd1, up2_z)
    up_grad(n.ag1, n.d1)
    gu1_sib = sib_grads(n.GU, n.SU)
    recv(gu1_sib)
    core_sum(n.GU, n.SU)
    gu1_z = z_grads(n.GU, zu1, dn2_z)
    back, gain_part = norm_back(n.z1[...], gain[2][...], gather_sum(dm1, n.ra))
    set_gain(2, gain_part)
    ga = n.ga[...] + back
    n.ga[...] = ga

    n.gb[...] = low(ga)
    mats = (n.up2, n.dn2, n.up1, n.dn1)
    others = (n.u1, n.d1, n.ag1, n.bg)

    def put_cross(value, ref, first):
        for i in range(value.shape[0] // rows):
            ai, bi = divmod(first + i, nf)
            zi, ci = divmod(bi, 2)
            ref[ai, ci * nz + zi] = value[i * rows:(i + 1) * rows]

    def cross_grad(left, right, which):
        short = tall // 2
        for i in range(width // short):
            put_cross(low(dot(left[:, i * short:(i + 1) * short], right, TN)), mats[which],
                      i * short // rows)

    def half(ref, ci):
        return ref.at[:, pl.ds(ci * nz, nz)]

    for g in up1_sib + dn1_sib + up2_sib + dn2_sib:
        sent(g)
    for k in (3, 1, 2):
        final_dp.push(k)
    cross_grad(n.cc, n.gb[...], 3)
    core_dp = [group(1, lambda i, w=w: (half(mats[w], 1 - c), others[w], sib)) for w in range(4)]
    start(core_dp[3])
    n.dc[...] = low(dot(n.gb[...], n.wx[3].reshape(width, width), NT))
    own_half = pl.ds(c * nz, nz)
    cross_xy, cross_back_z = {}, {}

    def over_dp(w):
        recv(core_dp[w])
        for ai in range(nd):
            mats[w][ai, own_half] = low(mats[w][ai, own_half].astype(F32) + others[w][ai].astype(F32))
        cross_xy[w] = Merge(lambda k, h, w=w: mats[w].at[apos(k), pl.ds(c * nz + h * mid, mid)], n.xw.at[w],
                            cross_dp[w])
        for k in (3, 1, 2):
            cross_xy[w].push(k)

    def z_start(w, slots, after):
        mats[w][a, own_half] = low(cross_xy[w].total(mats[w][a, own_half].astype(F32)))
        cross_back_z[w] = Reduce(lambda zi: mats[w].at[a, c * nz + zi], slots, after)
        cross_back_z[w].start()

    over_dp(3)

    def cross_back(h, _):
        at = pl.ds(pl.multiple_of(h * hd, hd), hd)
        dq, dk, dv = attend_back(n.qq[:, at], n.kk[:, at], n.vv[:, at], n.pp[h], n.dc[:, at])
        n.qq[:, at] = dq
        n.kk[:, at] = dk
        n.vv[:, at] = dv
        return 0

    lax.fori_loop(0, HEADS, cross_back, 0, unroll=2)
    again = [load(n.inputs.at[0, pl.ds(i * block, block)], n.pp.at[i]) for i in range(span // block)]
    cross_grad(n.xn, n.vv[...], 2)
    start(core_dp[2])
    cross_xy[3].combine()
    final_dp.combine()
    cross_grad(n.xn, n.kk[...], 1)
    start(core_dp[1])
    over_dp(2)
    cross_grad(n.an, n.qq[...], 0)
    start(core_dp[0])
    over_dp(1)
    gd1_z.combine()
    cross_xy[2].combine()
    over_dp(0)
    gu1_z.combine()

    back, gain_part = norm_back(n.lt[...].astype(F32), gain[0][...],
                                dot(n.qq[...], n.wx[0].reshape(width, width), NT))
    set_gain(0, gain_part)
    n.gb[...] = low(n.ga[...] + back)
    outs.append(load(n.gb, n.glat.at[0]))
    arrived(again)

    def token_back(i, total):
        at = pl.ds(pl.multiple_of(i * 2 * block, 2 * block), 2 * block)
        step = width // nd
        for j in range(nd):
            to = slice(j * step, (j + 1) * step)
            grad = (dot(n.kk[at], n.wx[1, j].reshape(step, width), NT)
                    + dot(n.vv[at], n.wx[2, j].reshape(step, width), NT))
            n.z1[:, to] = grad[:block]
            n.own[:, to] = grad[block:]
        for j, ref in enumerate((n.z1, n.own)):
            back, gain_part = norm_back(n.pp[2 * i + j].astype(F32), gain[1][...], ref[...])
            n.pp[2 * i + j] = low(back)
            total = total + gain_part
        return total

    steps = span // (2 * block)
    total = lax.fori_loop(0, steps // 4, token_back, jnp.zeros((1, width), F32))
    cross_xy[1].combine()
    z_start(3, n.d2.at[2], sq_z)
    total = lax.fori_loop(steps // 4, steps // 2, token_back, total)
    cross_xy[0].combine()
    z_start(2, n.d2.at[3], so_z)
    cross_back_z[3].combine()
    set_gain(1, lax.fori_loop(steps // 2, steps, token_back, total))
    for i in range(span // block):
        outs.append(load(n.pp.at[i], n.ginp.at[0, pl.ds(i * block, block)]))
    gain_hops = small_sum(n.dg)
    gain_hops[0][0]()

    total = gd1_z.total()
    outs.append(out_rows(total, n.z1, n.ofd))
    cu1_dp = column_grads(gu1_z.total(), su4, n.CU1)
    gain_hops[0][1]()
    gain_hops[1][0]()
    start(cu2_dp)
    start(cu1_dp)
    z_start(1, n.ZU.at[1], gd2_z)
    cross_back_z[2].combine()
    total = go_z.total()
    down_out.wait()
    n.z2[0:rows] = total
    outs.append(load(n.z2.at[0:rows], n.oso))
    total = gq_z.total()
    sq_send = n.sqs
    sent(sq_dp)
    sq_send[...] = low(total)
    cq_dp = dp_group(lambda k: sq_send.at[apos(k)], lambda k: n.CQ.at[k - 1])
    start(cq_dp)
    z_start(0, n.ZU.at[0], gu2_z)
    cross_back_z[1].combine()
    cross_back_z[0].combine()
    gain_hops[1][1]()
    gain_hops[2][0]()
    n.dc[...] = low(final_dp.total(n.z3[...] + n.ob[...].astype(F32)))
    outs.append(load(n.dc, n.out.at[0]))

    def put_columns(g, own, slots, staged, target):
        staged[0:rows] = own
        copies = [load(staged.at[0:rows], target.at[:, pl.ds(pl.multiple_of(a * width, width), width)])]
        for i in range(nd - 1):
            g(i).wait_recv()
            staged[(i + 1) * rows:(i + 2) * rows] = slots[i].astype(F32)
            copies.append(load(staged.at[(i + 1) * rows:(i + 2) * rows],
                               target.at[:, pl.ds(pl.multiple_of(apos(i + 1) * width, width), width)]))
        return copies

    outs += put_columns(cu2_dp, su3[a].astype(F32), n.CU2, n.z3, n.ogu)
    outs += put_columns(cu1_dp, su4[a].astype(F32), n.CU1, n.own, n.ofu)
    recv(cq_dp)
    for i, target in enumerate((n.osq, n.osk, n.osv)):
        at = slice((i + 1) * rows, (i + 2) * rows)
        n.z2[at, pl.ds(pl.multiple_of(a * cols, cols), cols)] = sq_send[a, i].astype(F32)
        for k in range(1, nd):
            n.z2[at, pl.ds(pl.multiple_of(apos(k) * cols, cols), cols)] = n.CQ[k - 1, i].astype(F32)
        outs.append(load(n.z2.at[at], target))
    for w, target in ((3, n.oco), (2, n.ocv), (1, n.ock), (0, n.ocq)):
        total = cross_back_z[w].total()
        at = slice(w * rows, (w + 1) * rows)
        n.ga[at] = total
        outs.append(load(n.ga.at[at], target))
    gain_hops[2][1]()
    outs.append(load(n.dg, n.ggain))
    for g in ([final_dp, dm1, gq_sib, go_sib, gq_z, go_z, cu1_dp, cu2_dp, cq_dp, gu1_sib, gd1_sib, gu1_z, gd1_z]
              + sq_sib + so_sib + core_dp + list(cross_xy.values()) + list(cross_back_z.values())):
        sent(g)
    arrived(outs)


def layer_norm(value, gain):
    center = value - jnp.mean(value, axis=-1, keepdims=True)
    spread = jnp.mean(center * center, axis=-1, keepdims=True)
    return center * lax.rsqrt(spread + EPS) * gain


def activate(value):
    return jax.nn.gelu(value, approximate=True)


def product(left, right):
    return jnp.dot(left, right, preferred_element_type=jnp.float32)


def weight_grad(left, right):
    return lax.dot_general(
        left, right, (((0,), (0,)), ((), ())), preferred_element_type=jnp.float32
    )


def back_product(grad, weight):
    return lax.dot_general(
        grad, weight, (((1,), (1,)), ((), ())), preferred_element_type=jnp.float32
    )


def plain_norm_back(value, gain, grad):
    _, pull = jax.vjp(layer_norm, value, gain)
    return pull(grad)


def activate_back(value, grad):
    _, pull = jax.vjp(activate, value)
    return pull(grad)[0]


def split_heads(value, groups):
    return value.reshape(groups, -1, HEADS, value.shape[-1] // HEADS)


def merge_heads(value):
    return value.reshape(-1, value.shape[2] * value.shape[3])


def masked_scores(query, key, valid):
    scale = query.shape[-1] ** (-0.5)
    scores = jnp.einsum("gqhd,gkhd->ghqk", query, key, preferred_element_type=jnp.float32) * scale
    return jnp.where(valid[:, None, None, :], scores, NEG)


def attend_forward(query, key, value, valid):
    scores = masked_scores(query, key, valid)
    top = jnp.max(scores, axis=-1, keepdims=True)
    expo = jnp.exp(scores - top)
    denom = jnp.sum(expo, axis=-1, keepdims=True)
    weights = (expo / denom).astype(jnp.bfloat16)
    mixed = jnp.einsum("ghqk,gkhd->gqhd", weights, value, preferred_element_type=jnp.float32)
    return (merge_heads(mixed).astype(jnp.bfloat16), top + jnp.log(denom))


def plain_attend_back(query, key, value, valid, logsum, grad_mixed):
    scale = query.shape[-1] ** (-0.5)
    probs = jnp.exp(masked_scores(query, key, valid) - logsum)
    grad_probs = jnp.einsum(
        "gqhd,gkhd->ghqk", grad_mixed, value, preferred_element_type=jnp.float32
    )
    inner = jnp.sum(probs * grad_probs, axis=-1, keepdims=True)
    grad_scores = (probs * (grad_probs - inner)).astype(jnp.bfloat16)
    weights = probs.astype(jnp.bfloat16)
    grad_query = (
        jnp.einsum("ghqk,gkhd->gqhd", grad_scores, key, preferred_element_type=jnp.float32) * scale
    )
    grad_key = (
        jnp.einsum("ghqk,gqhd->gkhd", grad_scores, query, preferred_element_type=jnp.float32)
        * scale
    )
    grad_value = jnp.einsum(
        "ghqk,gqhd->gkhd", weights, grad_mixed, preferred_element_type=jnp.float32
    )
    return (
        merge_heads(grad_query).astype(jnp.bfloat16),
        merge_heads(grad_key).astype(jnp.bfloat16),
        merge_heads(grad_value).astype(jnp.bfloat16),
    )


def feed_forward(resid, gain, w_up, w_down):
    normed = layer_norm(resid, gain.astype(jnp.float32)).astype(jnp.bfloat16)
    before = product(normed, w_up)
    hidden = activate(before).astype(jnp.bfloat16)
    return (resid + product(hidden, w_down), (normed, before, hidden))


def plain_feed_back(grad, resid, gain, saved, w_up, w_down):
    normed, before, hidden = saved
    grad_low = grad.astype(jnp.bfloat16)
    grad_down = weight_grad(hidden, grad_low)
    grad_before = activate_back(before, back_product(grad_low, w_down)).astype(jnp.bfloat16)
    grad_up = weight_grad(normed, grad_before)
    grad_resid, grad_gain = plain_norm_back(
        resid, gain.astype(jnp.float32), back_product(grad_before, w_up)
    )
    return (grad + grad_resid, grad_gain, grad_up, grad_down)


def project_back(grad, mixed, w_out, query, key, value, valid, logsum, groups):
    grad_low = grad.astype(jnp.bfloat16)
    grad_out = weight_grad(mixed, grad_low)
    grad_mixed = back_product(grad_low, w_out).astype(jnp.bfloat16)
    grad_query, grad_key, grad_value = plain_attend_back(
        split_heads(query, groups),
        split_heads(key, groups),
        split_heads(value, groups),
        valid,
        logsum,
        split_heads(grad_mixed, groups),
    )
    return (grad_out, grad_query, grad_key, grad_value)


def plain_layer(
    latents,
    inputs,
    frames,
    norm_latent,
    norm_input,
    cross_query,
    cross_key,
    cross_value,
    cross_output,
    norm_first,
    first_up,
    first_down,
    norm_self,
    self_query,
    self_key,
    self_value,
    self_output,
    norm_second,
    second_up,
    second_down,
    cotangent,
    mesh_size,
):
    groups, lat_rows, width = latents.shape
    span = inputs.shape[1]
    hidden_width = first_up.shape[1]
    low_type = jnp.bfloat16
    parts = mesh_size
    gains = (norm_latent, norm_input, norm_first, norm_self, norm_second)
    mats = (cross_query, cross_key, cross_value, cross_output, first_up, first_down,
            self_query, self_key, self_value, self_output, second_up, second_down)
    blocks = []
    for mat in mats:
        for start in range(0, mat.shape[1], width):
            blocks.append(mat[:, start:start + width])
    gain_row = jnp.concatenate([jnp.concatenate(gains), jnp.zeros((width - 5 * gains[0].shape[0],), jnp.float32)])
    gain_rows = jnp.concatenate([gain_row[None], jnp.zeros((15, width), jnp.float32)])
    packed = jnp.concatenate([gain_rows] + blocks).astype(low_type)
    whole = lax.all_gather(packed, ("dp", "fsdp"), axis=0, tiled=False)
    per = gains[0].shape[0]
    gathered_gains = [whole[:, 0, i * per:(i + 1) * per].reshape(width) for i in range(5)]
    gain_lat, gain_inp, gain_first, gain_self, gain_second = gathered_gains
    at = 16
    full = []
    for mat in mats:
        columns = []
        for start in range(0, mat.shape[1], width):
            columns.append(whole[:, at:at + mat.shape[0]].reshape(parts * mat.shape[0], width))
            at += mat.shape[0]
        full.append(columns[0] if len(columns) == 1 else jnp.concatenate(columns, axis=1))
    w_query, w_key, w_value, w_out, up_one, down_one, s_query, s_key, s_value, s_out, up_two, down_two = full
    positions = jnp.arange(span, dtype=jnp.int32)
    valid = positions[None, :] < (frames * FRAME_TOK)[:, None]
    every = jnp.ones((groups, lat_rows), dtype=bool)
    latent_rows = latents.reshape(groups * lat_rows, width).astype(jnp.float32)
    input_rows = inputs.reshape(groups * span, width).astype(jnp.float32)
    normed_lat = layer_norm(latent_rows, gain_lat.astype(jnp.float32)).astype(low_type)
    normed_inp = layer_norm(input_rows, gain_inp.astype(jnp.float32)).astype(low_type)
    query_one = product(normed_lat, w_query).astype(low_type)
    key_one = product(normed_inp, w_key).astype(low_type)
    value_one = product(normed_inp, w_value).astype(low_type)
    mixed_one, logsum_one = attend_forward(
        split_heads(query_one, groups),
        split_heads(key_one, groups),
        split_heads(value_one, groups),
        valid,
    )
    first_resid = latent_rows + product(mixed_one, w_out)
    second_resid, saved_one = feed_forward(first_resid, gain_first, up_one, down_one)
    normed_self = layer_norm(second_resid, gain_self.astype(jnp.float32)).astype(low_type)
    query_two = product(normed_self, s_query).astype(low_type)
    key_two = product(normed_self, s_key).astype(low_type)
    value_two = product(normed_self, s_value).astype(low_type)
    mixed_two, logsum_two = attend_forward(
        split_heads(query_two, groups),
        split_heads(key_two, groups),
        split_heads(value_two, groups),
        every,
    )
    third_resid = second_resid + product(mixed_two, s_out)
    final_resid, saved_two = feed_forward(third_resid, gain_second, up_two, down_two)
    result = final_resid.reshape(groups, lat_rows, width).astype(low_type)
    grad_final = cotangent.reshape(groups * lat_rows, width).astype(jnp.float32)
    grad_third, grad_gain_second, grad_up_two, grad_down_two = plain_feed_back(
        grad_final, third_resid, gain_second, saved_two, up_two, down_two
    )
    grad_s_out, grad_query_two, grad_key_two, grad_value_two = project_back(
        grad_third, mixed_two, s_out, query_two, key_two, value_two, every, logsum_two, groups
    )
    grad_s_query = weight_grad(normed_self, grad_query_two)
    grad_s_key = weight_grad(normed_self, grad_key_two)
    grad_s_value = weight_grad(normed_self, grad_value_two)
    grad_normed_self = (
        back_product(grad_query_two, s_query)
        + back_product(grad_key_two, s_key)
        + back_product(grad_value_two, s_value)
    )
    grad_from_self, grad_gain_self = plain_norm_back(
        second_resid, gain_self.astype(jnp.float32), grad_normed_self
    )
    grad_second = grad_third + grad_from_self
    grad_first, grad_gain_first, grad_up_one, grad_down_one = plain_feed_back(
        grad_second, first_resid, gain_first, saved_one, up_one, down_one
    )
    grad_w_out, grad_query_one, grad_key_one, grad_value_one = project_back(
        grad_first, mixed_one, w_out, query_one, key_one, value_one, valid, logsum_one, groups
    )
    grad_w_query = weight_grad(normed_lat, grad_query_one)
    grad_w_key = weight_grad(normed_inp, grad_key_one)
    grad_w_value = weight_grad(normed_inp, grad_value_one)
    grad_from_lat, grad_gain_lat = plain_norm_back(
        latent_rows, gain_lat.astype(jnp.float32), back_product(grad_query_one, w_query)
    )
    grad_latent_rows = grad_first + grad_from_lat
    grad_normed_inp = back_product(grad_key_one, w_key) + back_product(grad_value_one, w_value)
    grad_input_rows, grad_gain_inp = plain_norm_back(
        input_rows, gain_inp.astype(jnp.float32), grad_normed_inp
    )
    grad_mats = (grad_w_query, grad_w_key, grad_w_value, grad_w_out, grad_up_one, grad_down_one,
                 grad_s_query, grad_s_key, grad_s_value, grad_s_out, grad_up_two, grad_down_two)
    gain_grads = jnp.stack([grad_gain_lat, grad_gain_inp, grad_gain_first, grad_gain_self, grad_gain_second])
    gain_grads = jnp.moveaxis(gain_grads.reshape(5, parts, per), 1, 0).reshape(parts, 1, 5 * per)
    gain_grads = jnp.pad(gain_grads, ((0, 0), (0, 15), (0, width - 5 * per)))
    pieces = [gain_grads.astype(low_type)]
    for grad in grad_mats:
        for start in range(0, grad.shape[1], width):
            pieces.append(grad[:, start:start + width].reshape(parts, -1, width).astype(low_type))
    summed = lax.psum_scatter(jnp.concatenate(pieces, axis=1), ("dp", "fsdp"), scatter_dimension=0, tiled=False)
    summed = summed.astype(jnp.float32)
    gain_out = [summed[0, i * per:(i + 1) * per] for i in range(5)]
    at = 16
    out = []
    for mat in mats:
        columns = []
        for start in range(0, mat.shape[1], width):
            columns.append(summed[at:at + mat.shape[0]])
            at += mat.shape[0]
        out.append(columns[0] if len(columns) == 1 else jnp.concatenate(columns, axis=1))
    grad_latents = grad_latent_rows.reshape(groups, lat_rows, width).astype(low_type)
    grad_inputs = grad_input_rows.reshape(groups, span, width).astype(low_type)
    return (
        result, grad_latents, grad_inputs,
        gain_out[0], gain_out[1], out[0], out[1], out[2], out[3],
        gain_out[2], out[4], out[5],
        gain_out[3], out[6], out[7], out[8], out[9],
        gain_out[4], out[10], out[11],
    )


def hand_over(count, *refs):
    ins, outs, held, sems = refs[:count], refs[count:2 * count], refs[2 * count:3 * count], refs[-1]
    first = [pltpu.make_async_copy(ins[i], held[i], sems.at[i]) for i in range(count)]
    second = [pltpu.make_async_copy(held[i], outs[i], sems.at[count + i]) for i in range(count)]
    for copy in first:
        copy.start()
    for one, two in zip(first, second):
        one.wait()
        two.start()
    for copy in second:
        copy.wait()


def fits(mesh, lat, span, width, hidden):
    nd, nf = mesh.shape["dp"], mesh.shape["fsdp"]
    return (nd == 4 and nf == 8 and HEADS % nd == 0 and hidden == nd * width
            and width % (32 * nd * nf) == 0 and span == HEADS * lat and width // HEADS % 128 == 0)


def local(latents, inputs, frames, *rest, mesh):
    nd, nf = mesh.shape["dp"], mesh.shape["fsdp"]
    groups, lat, width = latents.shape
    span = inputs.shape[1]
    if groups != 1 or not fits(mesh, lat, span, width, rest[7].shape[1]):
        return plain_layer(latents, inputs, frames, *rest, mesh_size=mesh.size)
    (norm_latent, norm_input, cross_query, cross_key, cross_value, cross_output, norm_first, first_up,
     first_down, norm_self, self_query, self_key, self_value, self_output, norm_second, second_up,
     second_down, cotangent) = rest
    rows = cross_query.shape[0]
    index = lax.axis_index("dp") * nf + lax.axis_index("fsdp")
    gains = jnp.stack([norm_latent, norm_input, norm_first, norm_self, norm_second])
    lanes = lax.broadcasted_iota(jnp.int32, (8, 128), 1)
    gains = jnp.where(lanes // rows == lax.rem(index, 128 // rows),
                      jnp.tile(jnp.pad(gains, ((0, 3), (0, 0))), (1, 128 // rows)), 0.0)
    scratch = scratch_list(nd, nf, rows, width, lat, span, HEADS)
    anywhere = pl.BlockSpec(memory_space=pl.ANY)
    out_shape = (
        [jax.ShapeDtypeStruct(latents.shape, BF16)] * 2 + [jax.ShapeDtypeStruct(inputs.shape, BF16)]
        + [jax.ShapeDtypeStruct((8, width), F32)]
        + [jax.ShapeDtypeStruct(w.shape, F32) for w in (
            cross_query, cross_key, cross_value, cross_output, first_up, first_down,
            self_query, self_key, self_value, self_output, second_up, second_down)])
    flops = 2 * 3 * (lat * width * width * 22 + span * width * width * 2)
    results = pl.pallas_call(
        functools.partial(layer_kernel, INPUTS + OUTPUTS + tuple(scratch), nd, nf, rows),
        out_shape=out_shape,
        in_specs=[pl.BlockSpec(memory_space=pltpu.SMEM), pl.BlockSpec(memory_space=pltpu.VMEM)]
        + [anywhere] * (len(INPUTS) - 2),
        out_specs=[anywhere] * len(OUTPUTS),
        scratch_shapes=list(scratch.values()),
        compiler_params=pltpu.CompilerParams(
            collective_id=0, has_side_effects=True, vmem_limit_bytes=64 * 1024 * 1024),
        cost_estimate=pl.CostEstimate(flops=flops, bytes_accessed=30_000_000, transcendentals=4_000_000),
        name="layer",
    )(frames, gains, latents, inputs, cotangent, cross_query, cross_key, cross_value, cross_output,
      first_up, first_down, self_query, self_key, self_value, self_output, second_up, second_down)
    (result, grad_latents, grad_inputs, gain_grads, g_cq, g_ck, g_cv, g_co, g_fu, g_fd,
     g_sq, g_sk, g_sv, g_so, g_gu, g_gd) = pl.pallas_call(
        functools.partial(hand_over, len(OUTPUTS)),
        out_shape=out_shape,
        in_specs=[anywhere] * len(OUTPUTS),
        out_specs=[anywhere] * len(OUTPUTS),
        scratch_shapes=[pltpu.VMEM(o.shape, o.dtype) for o in out_shape]
        + [pltpu.SemaphoreType.DMA((2 * len(OUTPUTS),))],
        compiler_params=pltpu.CompilerParams(vmem_limit_bytes=64 * 1024 * 1024),
        cost_estimate=pl.CostEstimate(flops=0, bytes_accessed=12_000_000, transcendentals=0),
        name="hand_over",
    )(*results)
    own = lax.dynamic_slice(gain_grads, (0, index * rows), (8, rows))
    return (result, grad_latents, grad_inputs, own[0], own[1], g_cq, g_ck, g_cv, g_co, own[2], g_fu, g_fd,
            own[3], g_sq, g_sk, g_sv, g_so, own[4], g_gu, g_gd)


def solution(mesh):
    in_specs = (
        P(("dp", "fsdp"), None, None),
        P(("dp", "fsdp"), None, None),
        P(("dp", "fsdp")),
        P(("dp", "fsdp")),
        P(("dp", "fsdp")),
        P(("dp", "fsdp"), None),
        P(("dp", "fsdp"), None),
        P(("dp", "fsdp"), None),
        P(("dp", "fsdp"), None),
        P(("dp", "fsdp")),
        P(("dp", "fsdp"), None),
        P(("dp", "fsdp"), None),
        P(("dp", "fsdp")),
        P(("dp", "fsdp"), None),
        P(("dp", "fsdp"), None),
        P(("dp", "fsdp"), None),
        P(("dp", "fsdp"), None),
        P(("dp", "fsdp")),
        P(("dp", "fsdp"), None),
        P(("dp", "fsdp"), None),
        P(("dp", "fsdp"), None, None),
    )
    out_specs = (
        P(("dp", "fsdp"), None, None),
        P(("dp", "fsdp"), None, None),
        P(("dp", "fsdp"), None, None),
        P(("dp", "fsdp")),
        P(("dp", "fsdp")),
        P(("dp", "fsdp"), None),
        P(("dp", "fsdp"), None),
        P(("dp", "fsdp"), None),
        P(("dp", "fsdp"), None),
        P(("dp", "fsdp")),
        P(("dp", "fsdp"), None),
        P(("dp", "fsdp"), None),
        P(("dp", "fsdp")),
        P(("dp", "fsdp"), None),
        P(("dp", "fsdp"), None),
        P(("dp", "fsdp"), None),
        P(("dp", "fsdp"), None),
        P(("dp", "fsdp")),
        P(("dp", "fsdp"), None),
        P(("dp", "fsdp"), None),
    )
    return jax.shard_map(functools.partial(local, mesh=mesh), mesh=mesh, in_specs=in_specs, out_specs=out_specs,
                         check_vma=False)
```
